32 devices in a mesh: seq: 8 (over y, x, core), group: 4 (over z).
Axes of the slice: x: 2, y: 2, z: 4, core: 2. Of those that a mesh axis runs over, the one named last changes fastest.
Arguments:
- hidden_in: bfloat16 [8, 2048, 1024], P('seq', 'group'), may hold values from -6 to 6
- doc_lengths: int32 [8, 8], P('seq'), may hold values from 1 to 1024, 2048 in all within a row
- ln_gain: bfloat16 [1024], P(('seq', 'group')), may hold values from 0.099609375 to 1.8984375
- ln_bias: bfloat16 [1024], P(('seq', 'group')), may hold values from -3 to 3
- w_qkv: bfloat16 [1024, 3072], P(('seq', 'group')), may hold values from -0.25 to 0.25
- b_qkv: bfloat16 [3072], P(('seq', 'group')), may hold values from -3 to 3
- w_dense: bfloat16 [1024, 1024], P(('seq', 'group')), may hold values from -0.75 to 0.75
- b_dense: bfloat16 [1024], P(('seq', 'group')), may hold values from -3 to 3
- w_in: bfloat16 [1024, 4096], P(('seq', 'group')), may hold values from -0.1875 to 0.1875
- b_in: bfloat16 [4096], P(('seq', 'group')), may hold values from -3 to 3
- w_out: bfloat16 [4096, 1024], P(('seq', 'group')), may hold values from -0.09375 to 0.09375
- b_out: bfloat16 [1024], P(('seq', 'group')), may hold values from -3 to 3
- out_grad: bfloat16 [8, 2048, 1024], P('seq', 'group'), may hold values from -6 to 6
Outputs:
- hidden_out: bfloat16 [8, 2048, 1024], P('seq', 'group')
- grad_in: float32 [8, 2048, 1024], P('seq', 'group')
- grad_ln_gain: float32 [1024], P(('seq', 'group'))
- grad_ln_bias: float32 [1024], P(('seq', 'group'))
- grad_w_qkv: float32 [1024, 3072], P(('seq', 'group'))
- grad_b_qkv: float32 [3072], P(('seq', 'group'))
- grad_w_dense: float32 [1024, 1024], P(('seq', 'group'))
- grad_b_dense: float32 [1024], P(('seq', 'group'))
- grad_w_in: float32 [1024, 4096], P(('seq', 'group'))
- grad_b_in: float32 [4096], P(('seq', 'group'))
- grad_w_out: float32 [4096, 1024], P(('seq', 'group'))
- grad_b_out: float32 [1024], P(('seq', 'group'))
The draws below stay inside these ranges and needn't reach their ends.
Inputs may be any that keep to these rules, and one draw needn't show every extreme that they name: `doc_lengths`: each row lists the lengths of the 8 documents of one sequence in order; a row sums to 2048 and its longest document has exactly 1024 tokens.
All inputs are finite; a program needn't handle non-finite values.
Results may differ from the reference program's by a relative error of at most 0.017.
Values may be sent and summed in bfloat16 or wider, within the bound.
No kernel may reach another device: no remote copies, remote signals or barrier semaphores. Data moves between devices by JAX's collectives and lax.ppermute only.
A program may use at most 256 MiB of HBM per device.

```python
import math
import jax
import jax.numpy as jnp
import numpy as np
from jax import lax

D = 1024
HEADS = 16
HEAD_DIM = 64
FF = 4096
ROT_DIM = 16
DOCS = 8
SEQ_LEN = 2048
SEQS = 8


def raised(drawn, key, source, target, blocks, factor):
    owner, partner = [(jnp.arange(drawn.shape[dim]) // (drawn.shape[dim] // blocks)).reshape([-1 if axis == dim else 1 for axis in range(drawn.ndim)]) for dim in (source, target)]
    chosen = jax.random.permutation(key, blocks)[partner]
    strong = (owner == chosen) | (owner == (partner + blocks // 2) % blocks)
    return jnp.where(strong, factor * drawn, drawn)


def levels(stream_key, shape, cuts, least, largest):
    level = 1.0
    for position, blocks in cuts:
        draws = jax.random.uniform(jax.random.fold_in(jax.random.fold_in(stream_key, 6), position), (blocks,), jnp.float32, least / len(cuts), largest / len(cuts))
        level = level * jnp.repeat(jnp.exp(draws), shape[position] // blocks).reshape((-1,) + (1,) * (len(shape) - 1 - position))
    return level


def length_profile(number_of, total, most, lean):
    loads = [(1 << 20) // math.isqrt(grade ** lean) + 1 for grade in range(2, number_of + 1)]
    rest, given = total - most - (number_of - 1), [1] * (number_of - 1)
    while rest > 0:
        movable = [i for i in range(number_of - 1) if given[i] < most]
        whole, left = sum([loads[i] for i in movable]), rest
        for i in movable:
            more = min(most - given[i], max(1, left * loads[i] // whole), rest)
            given[i] = given[i] + more
            rest = rest - more
    return np.array([most] + given)


def uneven(rng, count, total, limit, lean):
    if count == 2:
        one = jax.random.randint(rng, (), max(1, total - limit), min(limit, total - 1) + 1)
        return jnp.stack([one, total - one])
    sizes = jnp.asarray(length_profile(count, total, limit, lean), jnp.int32)
    couples = (count - 1) // 2
    source_of, sink = sizes[1:1 + 2 * couples:2], sizes[2:2 + 2 * couples:2]
    slack = jnp.minimum(source_of - 1, limit - sink)
    passed = jax.random.randint(jax.random.fold_in(rng, 1), (couples,), 0, 1 << 20) % (slack + 1)
    sizes = sizes.at[1:1 + 2 * couples:2].set(source_of - passed).at[2:2 + 2 * couples:2].set(sink + passed)
    return sizes[jax.random.permutation(jax.random.fold_in(rng, 2), count)]


def noise(own_key, shape, deviation, limit, split=(), kind=jnp.bfloat16):
    entries = deviation * jax.random.normal(own_key, shape, jnp.float32)
    if split:
        entries = entries * levels(own_key, shape, split, -0.22, 0.18)
    return jnp.clip(entries, -limit, limit).astype(kind)


def heavy_noise(key, dims, deviation, most, pieces, heavy, held_as=jnp.bfloat16):
    array = deviation * jax.random.normal(key, dims, jnp.float32)
    if pieces:
        array = array * levels(key, dims, pieces, -0.22, 0.18)
    return jnp.clip(raised(array, jax.random.fold_in(key, 3), *heavy), -most, most).astype(held_as)


def setup_inputs(seed: int = 0) -> dict:
    seeds = jax.random.split(jax.random.key(seed), 14)
    return {
        "hidden_in": heavy_noise(seeds[0], (SEQS, SEQ_LEN, D), 1.0, 6.0, ((0, 8), (1, 4)), (0, 2, 8, 2.0)),
        "doc_lengths": jax.vmap(lambda own: uneven(own, DOCS, SEQ_LEN, SEQ_LEN // 2, 2))(jax.random.split(seeds[1], SEQS)).reshape((SEQS, DOCS)).astype(jnp.int32),
        "ln_gain": jnp.clip(1.0 + 0.18 * jax.random.normal(seeds[2], (D,), jnp.float32), 0.099609375, 1.8984375).astype(jnp.bfloat16),
        "ln_bias": noise(seeds[3], (D,), 0.5, 3.0, ((0, 32),)),
        "w_qkv": noise(seeds[4], (D, 3 * D), (D // 2) ** -0.5, 0.25, ((0, 32),)),
        "b_qkv": noise(seeds[5], (3 * D,), 0.5, 3.0, ((0, 32),)),
        "w_dense": noise(seeds[6], (D, D), (D // 16) ** -0.5, 0.75, ((0, 32),)),
        "b_dense": noise(seeds[7], (D,), 0.5, 3.0, ((0, 32),)),
        "w_in": noise(seeds[8], (D, FF), D ** -0.5, 0.1875, ((0, 32),)),
        "b_in": noise(seeds[9], (FF,), 0.5, 3.0, ((0, 32),)),
        "w_out": noise(seeds[10], (FF, D), FF ** -0.5, 0.09375, ((0, 32),)),
        "b_out": noise(seeds[11], (D,), 0.5, 3.0, ((0, 32),)),
        "out_grad": noise(seeds[12], (SEQS, SEQ_LEN, D), 1.0, 6.0, ((0, 8), (1, 4))),
    }


@jax.custom_vjp
def low(v):
    return lax.optimization_barrier(v.astype(jnp.bfloat16)).astype(jnp.float32)

@jax.custom_vjp
def low_back(v):
    return v

def low_keep(v):
    return (low(v), None)

def low_pass(kept, grad):
    return (grad,)

def back_keep(v):
    return (v, None)

def back_low(kept, grad):
    return (low(grad),)
low.defvjp(low_keep, low_pass)
low_back.defvjp(back_keep, back_low)

def highest(left, right):
    return jnp.dot(left, right, precision=lax.Precision.HIGHEST)

def rope_tables(token_positions, rot_dim):
    half_rot = rot_dim // 2
    frequency = jnp.exp(-math.log(10000.0) * 2.0 * jnp.arange(half_rot, dtype=jnp.float32) / rot_dim)
    angles = token_positions.astype(jnp.float32)[:, None] * frequency[None, :]
    return (jnp.cos(angles)[:, None, :], jnp.sin(angles)[:, None, :])

def rotate(heads, cosine, sine, rot_dim):
    half_rot = rot_dim // 2
    first_half = heads[:, :, :half_rot]
    second_half = heads[:, :, half_rot:rot_dim]
    remainder = heads[:, :, rot_dim:]
    return jnp.concatenate([first_half * cosine - second_half * sine, second_half * cosine + first_half * sine, remainder], axis=2)

def gelu_exact(preact):
    return jax.nn.gelu(preact, approximate=False)

def sequence_forward(params, tokens, lengths):
    ln_gain, ln_bias, w_qkv, b_qkv, w_dense, b_dense, w_in, b_in, w_out, b_out = params
    seq_len = tokens.shape[0]
    row_mean = lax.optimization_barrier(jnp.mean(tokens, axis=1, keepdims=True))
    centered = tokens - row_mean
    variance = lax.optimization_barrier(jnp.mean(centered * centered, axis=1, keepdims=True))
    normed = low(centered * lax.rsqrt(variance + 1e-05) * ln_gain + ln_bias)
    mixed = low_back(highest(normed, w_qkv) + b_qkv)
    token_positions = jnp.arange(seq_len, dtype=jnp.int32)
    cosine, sine = rope_tables(token_positions, ROT_DIM)
    head_shape = (seq_len, HEADS, HEAD_DIM)
    queries = low_back(low(rotate(mixed[:, :D].reshape(head_shape), cosine, sine, ROT_DIM)))
    key_rows = low_back(low(rotate(mixed[:, D:2 * D].reshape(head_shape), cosine, sine, ROT_DIM)))
    value_rows = low_back(low(mixed[:, 2 * D:].reshape(head_shape)))
    doc_ends = jnp.cumsum(lengths)
    document_segment = lax.optimization_barrier(jnp.sum((token_positions[:, None] >= doc_ends[None, :]).astype(jnp.int32), axis=1))
    block_of_rows = min(512, seq_len)
    block_count = seq_len // block_of_rows
    score_scale = 1.0 / math.sqrt(HEAD_DIM)

    def attend(block_in):
        query_block, seg_query, pos_query = block_in
        logit_scores = low_back(jnp.einsum('qhd,khd->hqk', query_block, key_rows, precision=lax.Precision.HIGHEST) * score_scale)
        allowed = (seg_query[:, None] == document_segment[None, :]) & (token_positions[None, :] <= pos_query[:, None])
        logit_scores = jnp.where(allowed[None], logit_scores, -1e+30)
        row_max = lax.optimization_barrier(jnp.max(logit_scores, axis=2, keepdims=True))
        attention_weights = jnp.exp(logit_scores - row_max)
        probability = low(attention_weights / lax.optimization_barrier(jnp.sum(attention_weights, axis=2, keepdims=True)))
        return low_back(low(jnp.einsum('hqk,khd->qhd', probability, value_rows, precision=lax.Precision.HIGHEST)))
    attended = lax.map(jax.checkpoint(attend), (queries.reshape(block_count, block_of_rows, HEADS, HEAD_DIM), document_segment.reshape(block_count, block_of_rows), token_positions.reshape(block_count, block_of_rows)))
    attended = attended.reshape(seq_len, D)
    branch_attn = highest(attended, w_dense) + b_dense
    pre_act = low_back(highest(normed, w_in) + b_in)
    activated = low(gelu_exact(pre_act))
    branch_mlp = highest(activated, w_out) + b_out
    return tokens + branch_attn + branch_mlp

def block_forward(tokens, params, doc_lengths):

    def scan_step(state_now, inputs):
        return (state_now, jax.checkpoint(sequence_forward)(params, inputs[0], inputs[1]))
    final_state, outputs = lax.scan(scan_step, jnp.zeros((), jnp.float32), (tokens, doc_lengths))
    return outputs

def reference(hidden_in, doc_lengths, ln_gain, ln_bias, w_qkv, b_qkv, w_dense, b_dense, w_in, b_in, w_out, b_out, out_grad):
    params = tuple((weight.astype(jnp.float32) for weight in (ln_gain, ln_bias, w_qkv, b_qkv, w_dense, b_dense, w_in, b_in, w_out, b_out)))
    tokens = hidden_in.astype(jnp.float32)

    def forward(tokens_in, params_in):
        return block_forward(tokens_in, params_in, doc_lengths)
    result, pullback = jax.vjp(forward, tokens, params)
    grad_tokens, weight_grads = pullback(out_grad.astype(jnp.float32))
    return (result.astype(jnp.bfloat16), grad_tokens, weight_grads[0], weight_grads[1], weight_grads[2], weight_grads[3], weight_grads[4], weight_grads[5], weight_grads[6], weight_grads[7], weight_grads[8], weight_grads[9])
```

```python
import functools
import math

import jax
import jax.numpy as jnp
from jax import lax
from jax.experimental import pallas as pl
from jax.experimental.pallas import tpu as pltpu
from jax.sharding import Mesh
from jax.sharding import PartitionSpec as P

HEADS = 16
HEAD_DIM = 64
ROT_DIM = 16


def prefix_ends(doc_lens):
    order = jnp.arange(doc_lens.shape[0], dtype=jnp.int32)
    return jnp.sum(jnp.where(order[None, :] <= order[:, None], doc_lens[None, :], 0), axis=1)


def dot_rows(left, right):
    return lax.dot_general(
        left, right, (((0,), (0,)), ((), ())), preferred_element_type=jnp.float32
    )


def dot_last(left, right):
    return lax.dot_general(
        left, right, (((1,), (1,)), ((), ())), preferred_element_type=jnp.float32
    )


def rope_tables(token_positions, rot_dim):
    half_rot = rot_dim // 2
    frequency = jnp.exp(
        -math.log(10000.0) * 2.0 * jnp.arange(half_rot, dtype=jnp.float32) / rot_dim
    )
    angles = token_positions.astype(jnp.float32)[:, None] * frequency[None, :]
    return (jnp.cos(angles)[:, None, :], jnp.sin(angles)[:, None, :])


def rotate(heads, cosine, sine, rot_dim):
    half_rot = rot_dim // 2
    first_half = heads[:, :, :half_rot]
    second_half = heads[:, :, half_rot:rot_dim]
    remainder = heads[:, :, rot_dim:]
    return jnp.concatenate(
        [
            first_half * cosine - second_half * sine,
            second_half * cosine + first_half * sine,
            remainder,
        ],
        axis=2,
    )


def gelu_exact(preact):
    return jax.nn.gelu(preact, approximate=False)


def block_scores(query_block, key_tile_block, seg_query, seg_key, pos_query, pos_key, score_scale):
    scaled = (
        jnp.einsum("qhd,khd->hqk", query_block, key_tile_block, preferred_element_type=jnp.float32)
        * score_scale
    )
    allowed = (seg_query[:, None] == seg_key[None, :]) & (pos_key[None, :] <= pos_query[:, None])
    return jnp.where(allowed[None], scaled, -1e30)


def owning_block(source, block_index, block_of_rows):
    return lax.dynamic_slice_in_dim(source, block_index * block_of_rows, block_of_rows, 0)


def add_block(source, block_index, block_of_rows, addend):
    current = owning_block(source, block_index, block_of_rows)
    return lax.dynamic_update_slice_in_dim(source, current + addend, block_index * block_of_rows, 0)


def attention_forward(
    query_heads,
    key_head_rows,
    value_head_rows,
    document_segment,
    token_positions,
    seg_start,
    block_of_rows,
):
    seq_len, head_count, head_dim = query_heads.shape
    score_scale = 1.0 / math.sqrt(head_dim)

    def query_step(qindex, state_now):
        outputs, log_sums = state_now
        query_block = owning_block(query_heads, qindex, block_of_rows)
        seg_query = owning_block(document_segment, qindex, block_of_rows)
        pos_query = owning_block(token_positions, qindex, block_of_rows)
        key_lower = seg_start[qindex * block_of_rows] // block_of_rows

        def scores_for_block(key_position_index):
            return block_scores(
                query_block,
                owning_block(key_head_rows, key_position_index, block_of_rows),
                seg_query,
                owning_block(document_segment, key_position_index, block_of_rows),
                pos_query,
                owning_block(token_positions, key_position_index, block_of_rows),
                score_scale,
            )

        def statistics_step(key_position_index, row_statistics):
            run_max, run_sum = row_statistics
            logit_scores = scores_for_block(key_position_index)
            new_max = jnp.maximum(run_max, jnp.max(logit_scores, axis=2))
            run_sum = run_sum * jnp.exp(run_max - new_max) + jnp.sum(
                jnp.exp(logit_scores - new_max[:, :, None]), axis=2
            )
            return (new_max, run_sum)

        start_stats = (
            jnp.full((head_count, block_of_rows), -1e30, jnp.float32),
            jnp.zeros((head_count, block_of_rows), jnp.float32),
        )
        run_max, run_sum = lax.fori_loop(key_lower, qindex + 1, statistics_step, start_stats)
        log_exp_total = run_max + jnp.log(run_sum)

        def value_loop_step(key_position_index, partial_output):
            attention_weights = jnp.exp(
                scores_for_block(key_position_index) - log_exp_total[:, :, None]
            ).astype(jnp.bfloat16)
            return partial_output + jnp.einsum(
                "hqk,khd->qhd",
                attention_weights,
                owning_block(value_head_rows, key_position_index, block_of_rows),
                preferred_element_type=jnp.float32,
            )

        block_out = lax.fori_loop(
            key_lower,
            qindex + 1,
            value_loop_step,
            jnp.zeros((block_of_rows, head_count, head_dim), jnp.float32),
        )
        outputs = lax.dynamic_update_slice_in_dim(outputs, block_out, qindex * block_of_rows, 0)
        log_sums = lax.dynamic_update_slice_in_dim(
            log_sums, log_exp_total, qindex * block_of_rows, 1
        )
        return (outputs, log_sums)

    start_state = (
        jnp.zeros((seq_len, head_count, head_dim), jnp.float32),
        jnp.zeros((head_count, seq_len), jnp.float32),
    )
    return lax.fori_loop(0, seq_len // block_of_rows, query_step, start_state)


def attention_backward(
    query_heads,
    key_head_rows,
    value_head_rows,
    grad_heads,
    outputs,
    log_sums,
    document_segment,
    token_positions,
    seg_start,
    block_of_rows,
):
    seq_len, head_count, head_dim = query_heads.shape
    score_scale = 1.0 / math.sqrt(head_dim)
    delta_all = jnp.sum(grad_heads.astype(jnp.float32) * outputs, axis=2).T

    def query_step(qindex, state_now):
        grad_query_all, grad_key_all, grad_value_all = state_now
        query_block = owning_block(query_heads, qindex, block_of_rows)
        grad_block = owning_block(grad_heads, qindex, block_of_rows)
        seg_query = owning_block(document_segment, qindex, block_of_rows)
        pos_query = owning_block(token_positions, qindex, block_of_rows)
        log_exp_total = lax.dynamic_slice_in_dim(log_sums, qindex * block_of_rows, block_of_rows, 1)
        delta_block = lax.dynamic_slice_in_dim(delta_all, qindex * block_of_rows, block_of_rows, 1)
        key_lower = seg_start[qindex * block_of_rows] // block_of_rows

        def key_loop_step(key_position_index, loop_state_inner):
            grad_query, grad_keys, grad_values = loop_state_inner
            key_tile_block = owning_block(key_head_rows, key_position_index, block_of_rows)
            value_tile_block = owning_block(value_head_rows, key_position_index, block_of_rows)
            logit_scores = block_scores(
                query_block,
                key_tile_block,
                seg_query,
                owning_block(document_segment, key_position_index, block_of_rows),
                pos_query,
                owning_block(token_positions, key_position_index, block_of_rows),
                score_scale,
            )
            probability = jnp.exp(logit_scores - log_exp_total[:, :, None])
            grad_values = add_block(
                grad_values,
                key_position_index,
                block_of_rows,
                jnp.einsum(
                    "hqk,qhd->khd",
                    probability.astype(jnp.bfloat16),
                    grad_block,
                    preferred_element_type=jnp.float32,
                ),
            )
            grad_probs = jnp.einsum(
                "qhd,khd->hqk", grad_block, value_tile_block, preferred_element_type=jnp.float32
            )
            grad_scores = (probability * (grad_probs - delta_block[:, :, None])).astype(
                jnp.bfloat16
            )
            grad_query = (
                grad_query
                + jnp.einsum(
                    "hqk,khd->qhd", grad_scores, key_tile_block, preferred_element_type=jnp.float32
                )
                * score_scale
            )
            grad_keys = add_block(
                grad_keys,
                key_position_index,
                block_of_rows,
                jnp.einsum(
                    "hqk,qhd->khd", grad_scores, query_block, preferred_element_type=jnp.float32
                )
                * score_scale,
            )
            return (grad_query, grad_keys, grad_values)

        start_inner = (
            jnp.zeros((block_of_rows, head_count, head_dim), jnp.float32),
            grad_key_all,
            grad_value_all,
        )
        grad_query, grad_key_all, grad_value_all = lax.fori_loop(
            key_lower, qindex + 1, key_loop_step, start_inner
        )
        grad_query_all = lax.dynamic_update_slice_in_dim(
            grad_query_all, grad_query, qindex * block_of_rows, 0
        )
        return (grad_query_all, grad_key_all, grad_value_all)

    zero_heads = jnp.zeros((seq_len, head_count, head_dim), jnp.float32)
    return lax.fori_loop(
        0, seq_len // block_of_rows, query_step, (zero_heads, zero_heads, zero_heads)
    )


def local_generic(
    hidden_in,
    doc_lengths,
    ln_gain,
    ln_bias,
    w_qkv,
    b_qkv,
    w_dense,
    b_dense,
    w_in,
    b_in,
    w_out,
    b_out,
    out_grad,
):
    (
        full_gain,
        full_bias,
        full_qkv,
        full_qkv_bias,
        full_dense,
        full_dense_bias,
        full_in,
        full_in_bias,
        full_out,
        full_out_bias,
    ) = (
        lax.all_gather(ln_gain, ("seq", "group"), axis=0, tiled=True),
        lax.all_gather(ln_bias, ("seq", "group"), axis=0, tiled=True),
        lax.all_gather(w_qkv, ("seq", "group"), axis=0, tiled=True),
        lax.all_gather(b_qkv, ("seq", "group"), axis=0, tiled=True),
        lax.all_gather(w_dense, ("seq", "group"), axis=0, tiled=True),
        lax.all_gather(b_dense, ("seq", "group"), axis=0, tiled=True),
        lax.all_gather(w_in, ("seq", "group"), axis=0, tiled=True),
        lax.all_gather(b_in, ("seq", "group"), axis=0, tiled=True),
        lax.all_gather(w_out, ("seq", "group"), axis=0, tiled=True),
        lax.all_gather(b_out, ("seq", "group"), axis=0, tiled=True),
    )
    tokens = hidden_in[0].astype(jnp.float32)
    tok_count = tokens.shape[0]
    width = tokens.shape[1]
    row_mean = jnp.mean(tokens, axis=1, keepdims=True)
    centered = tokens - row_mean
    variance = jnp.mean(centered * centered, axis=1, keepdims=True)
    inv_std = lax.rsqrt(variance + 1e-05)
    normal_rows = centered * inv_std
    normed = (normal_rows * full_gain.astype(jnp.float32) + full_bias.astype(jnp.float32)).astype(
        jnp.bfloat16
    )
    mixed = jnp.dot(normed, full_qkv, preferred_element_type=jnp.float32) + full_qkv_bias.astype(
        jnp.float32
    )
    token_positions = lax.axis_index("group") * tok_count + jnp.arange(tok_count, dtype=jnp.int32)
    cosine, sine = rope_tables(token_positions, ROT_DIM)
    head_shape = (tok_count, HEADS, HEAD_DIM)
    queries = (
        rotate(mixed[:, :width].reshape(head_shape), cosine, sine, ROT_DIM)
        .reshape(tok_count, width)
        .astype(jnp.bfloat16)
    )
    key_rows = (
        rotate(mixed[:, width : 2 * width].reshape(head_shape), cosine, sine, ROT_DIM)
        .reshape(tok_count, width)
        .astype(jnp.bfloat16)
    )
    value_rows = mixed[:, 2 * width :].astype(jnp.bfloat16)
    query_cols, key_cols, value_cols = (
        lax.all_to_all(queries, "group", split_axis=1, concat_axis=0, tiled=True),
        lax.all_to_all(key_rows, "group", split_axis=1, concat_axis=0, tiled=True),
        lax.all_to_all(value_rows, "group", split_axis=1, concat_axis=0, tiled=True),
    )
    seq_len = query_cols.shape[0]
    head_count = query_cols.shape[1] // HEAD_DIM
    heads_shape = (seq_len, head_count, HEAD_DIM)
    query_heads = query_cols.reshape(heads_shape)
    key_head_rows = key_cols.reshape(heads_shape)
    value_head_rows = value_cols.reshape(heads_shape)
    all_pos = jnp.arange(seq_len, dtype=jnp.int32)
    doc_lens = doc_lengths[0]
    doc_ends = prefix_ends(doc_lens)
    document_segment = jnp.sum((all_pos[:, None] >= doc_ends[None, :]).astype(jnp.int32), axis=1)
    doc_starts = doc_ends - doc_lens
    doc_index = jnp.arange(doc_ends.shape[0], dtype=jnp.int32)
    seg_start = jnp.sum(
        jnp.where(document_segment[:, None] == doc_index[None, :], doc_starts[None, :], 0), axis=1
    )
    block_of_rows = min(512, seq_len)
    outputs, log_sums = attention_forward(
        query_heads,
        key_head_rows,
        value_head_rows,
        document_segment,
        all_pos,
        seg_start,
        block_of_rows,
    )
    attended = lax.all_to_all(
        outputs.reshape(seq_len, head_count * HEAD_DIM).astype(jnp.bfloat16),
        "group",
        split_axis=0,
        concat_axis=1,
        tiled=True,
    )
    branch_attn = jnp.dot(
        attended, full_dense, preferred_element_type=jnp.float32
    ) + full_dense_bias.astype(jnp.float32)
    pre_act = jnp.dot(normed, full_in, preferred_element_type=jnp.float32) + full_in_bias.astype(
        jnp.float32
    )
    activated = gelu_exact(pre_act).astype(jnp.bfloat16)
    branch_mlp = jnp.dot(
        activated, full_out, preferred_element_type=jnp.float32
    ) + full_out_bias.astype(jnp.float32)
    hidden_out = (tokens + branch_attn + branch_mlp).astype(jnp.bfloat16)
    grad_rows = out_grad[0]
    grad_float = grad_rows.astype(jnp.float32)
    bias_grad = jnp.sum(grad_float, axis=0)
    grad_dense = dot_rows(attended, grad_rows)
    grad_out_w = dot_rows(activated, grad_rows)
    grad_act = dot_last(grad_rows, full_out)
    grad_pre = jax.vjp(gelu_exact, pre_act)[1](grad_act)[0].astype(jnp.bfloat16)
    grad_in_w = dot_rows(normed, grad_pre)
    grad_in_bias = jnp.sum(grad_pre.astype(jnp.float32), axis=0)
    grad_normed = dot_last(grad_pre, full_in)
    grad_attended = dot_last(grad_rows, full_dense).astype(jnp.bfloat16)
    grad_cols = lax.all_to_all(grad_attended, "group", split_axis=1, concat_axis=0, tiled=True)
    grad_query_all, grad_key_all, grad_value_all = attention_backward(
        query_heads,
        key_head_rows,
        value_head_rows,
        grad_cols.reshape(heads_shape),
        outputs,
        log_sums,
        document_segment,
        all_pos,
        seg_start,
        block_of_rows,
    )
    flat_shape = (seq_len, head_count * HEAD_DIM)
    grad_query_tok, grad_key_tok, grad_value_tok = (
        lax.all_to_all(
            grad_query_all.reshape(flat_shape).astype(jnp.bfloat16),
            "group",
            split_axis=0,
            concat_axis=1,
            tiled=True,
        ),
        lax.all_to_all(
            grad_key_all.reshape(flat_shape).astype(jnp.bfloat16),
            "group",
            split_axis=0,
            concat_axis=1,
            tiled=True,
        ),
        lax.all_to_all(
            grad_value_all.reshape(flat_shape).astype(jnp.bfloat16),
            "group",
            split_axis=0,
            concat_axis=1,
            tiled=True,
        ),
    )
    unrot_query = (
        rotate(grad_query_tok.astype(jnp.float32).reshape(head_shape), cosine, -sine, ROT_DIM)
        .reshape(tok_count, width)
        .astype(jnp.bfloat16)
    )
    unrot_key = (
        rotate(grad_key_tok.astype(jnp.float32).reshape(head_shape), cosine, -sine, ROT_DIM)
        .reshape(tok_count, width)
        .astype(jnp.bfloat16)
    )
    grad_mixed = jnp.concatenate([unrot_query, unrot_key, grad_value_tok], axis=1)
    grad_qkv_w = dot_rows(normed, grad_mixed)
    grad_qkv_bias = jnp.sum(grad_mixed.astype(jnp.float32), axis=0)
    grad_normed = grad_normed + dot_last(grad_mixed, full_qkv)
    scaled_grad = grad_normed * full_gain.astype(jnp.float32)
    grad_gain = jnp.sum(grad_normed * normal_rows, axis=0)
    grad_bias = jnp.sum(grad_normed, axis=0)
    grad_input = grad_float + inv_std * (
        scaled_grad
        - jnp.mean(scaled_grad, axis=1, keepdims=True)
        - normal_rows * jnp.mean(scaled_grad * normal_rows, axis=1, keepdims=True)
    )
    sharded = tuple(
        (
            lax.psum_scatter(grad_gain, ("seq", "group"), scatter_dimension=0, tiled=True),
            lax.psum_scatter(grad_bias, ("seq", "group"), scatter_dimension=0, tiled=True),
            lax.psum_scatter(grad_qkv_w, ("seq", "group"), scatter_dimension=0, tiled=True),
            lax.psum_scatter(grad_qkv_bias, ("seq", "group"), scatter_dimension=0, tiled=True),
            lax.psum_scatter(grad_dense, ("seq", "group"), scatter_dimension=0, tiled=True),
            lax.psum_scatter(bias_grad, ("seq", "group"), scatter_dimension=0, tiled=True),
            lax.psum_scatter(grad_in_w, ("seq", "group"), scatter_dimension=0, tiled=True),
            lax.psum_scatter(grad_in_bias, ("seq", "group"), scatter_dimension=0, tiled=True),
            lax.psum_scatter(grad_out_w, ("seq", "group"), scatter_dimension=0, tiled=True),
            lax.psum_scatter(bias_grad, ("seq", "group"), scatter_dimension=0, tiled=True),
        )
    )
    return (hidden_out[None], grad_input[None]) + sharded


SWAP = [(0, 1), (1, 0)]
CHUNK = 256
LANES = 128
BF = jnp.bfloat16
F32 = jnp.float32


def mm(left, right):
    return jnp.dot(left, right, preferred_element_type=F32)


def other_core(value):
    return lax.ppermute(value, "c", SWAP)


def nt(left, right):
    return lax.dot_general(left, right, (((1,), (1,)), ((), ())), preferred_element_type=F32)


def rotated(heads, keep, low, high):
    return (
        heads * keep
        + pltpu.roll(heads, LANES - ROT_DIM // 2, 1) * low
        + pltpu.roll(heads, ROT_DIM // 2, 1) * high
    )


def attention_kernel(
    halo,
    tok,
    scalar_ref,
    q_ref,
    k_ref,
    v_ref,
    kh_ref,
    vh_ref,
    do_ref,
    keep_ref,
    low_ref,
    high_ref,
    start_ref,
    att_ref,
    dqkv_ref,
    dkvh_ref,
    s_scr,
    p_scr,
    k_scr,
    v_scr,
    kt_scr,
    vt_scr,
    dk_scr,
    dv_scr,
    ot_scr,
    dqt_scr,
):
    s, p = pl.program_id(0), pl.program_id(1)
    pairs = pl.num_programs(1)
    keys = (halo + 1) * tok
    chunks = keys // CHUNK
    lower = scalar_ref[s]
    base = scalar_ref[2]
    scale = 1.0 / math.sqrt(HEAD_DIM)
    lane = lax.broadcasted_iota(jnp.int32, (tok, LANES), 1)
    first = lane < HEAD_DIM

    for b in range(halo + 1):
        rows = pl.ds(b * tok, tok)
        k_raw = (kh_ref[b, 0] if b < halo else k_ref[0]).astype(F32)
        v_raw = vh_ref[b, 0] if b < halo else v_ref[0]
        k_rot = rotated(k_raw, keep_ref[rows, :], low_ref[rows, :], high_ref[rows, :])
        k_scr[rows, :] = k_rot.astype(BF)
        kt_scr[:, rows] = jnp.transpose(k_rot).astype(BF)
        v_scr[rows, :] = v_raw
        vt_scr[:, rows] = jnp.transpose(v_raw.astype(F32)).astype(BF)
    own = pl.ds(halo * tok, tok)
    q_rot = rotated(q_ref[0].astype(F32), keep_ref[own, :], low_ref[own, :], high_ref[own, :])
    q_scaled = (q_rot.astype(BF).astype(F32) * scale).astype(BF)
    zero = jnp.zeros((tok, LANES), BF)
    q_head = (jnp.where(first, q_scaled, zero), jnp.where(first, zero, q_scaled))
    do_all = do_ref[0]
    do_head = (jnp.where(first, do_all, zero), jnp.where(first, zero, do_all))

    q_pos = base + halo * tok + lax.broadcasted_iota(jnp.int32, (CHUNK, tok), 1)
    start = start_ref[0]
    key_iota = base + lax.broadcasted_iota(jnp.int32, (CHUNK, tok), 0)

    def scores(j, tops):
        at = pl.ds(pl.multiple_of(j * CHUNK, CHUNK), CHUNK)
        k_pos = key_iota + j * CHUNK
        allowed = (k_pos >= start) & (k_pos <= q_pos)
        out = []
        for h in range(2):
            value = jnp.where(allowed, nt(k_scr[at, :], q_head[h]), -1e30)
            s_scr[h, at, :] = value
            out.append(jnp.maximum(tops[h], jnp.max(value.reshape(CHUNK // 8, 8, tok), axis=0)))
        return tuple(out)

    tops = lax.fori_loop(lower, chunks, scores, (jnp.full((8, tok), -1e30, F32),) * 2)
    tops = [jnp.max(t, axis=0, keepdims=True) for t in tops]

    def exponents(j, sums):
        at = pl.ds(pl.multiple_of(j * CHUNK, CHUNK), CHUNK)
        out = []
        for h in range(2):
            value = jnp.exp(s_scr[h, at, :] - tops[h])
            s_scr[h, at, :] = value
            out.append(sums[h] + jnp.sum(value.reshape(CHUNK // 8, 8, tok), axis=0))
        return tuple(out)

    sums = lax.fori_loop(lower, chunks, exponents, (jnp.zeros((8, tok), F32),) * 2)
    inverse = [1.0 / jnp.sum(t, axis=0, keepdims=True) for t in sums]

    ot_scr[...] = jnp.zeros_like(ot_scr)
    dqt_scr[...] = jnp.zeros_like(dqt_scr)

    def weigh(j, carry):
        at = pl.ds(pl.multiple_of(j * CHUNK, CHUNK), CHUNK)
        for h in range(2):
            prob = (s_scr[h, at, :] * inverse[h]).astype(BF)
            p_scr[h, at, :] = prob
            rows = pl.ds(h * HEAD_DIM, HEAD_DIM)
            ot_scr[rows, :] += mm(vt_scr[rows, at], prob)
        return carry

    lax.fori_loop(lower, chunks, weigh, 0)
    out_t = ot_scr[...]
    att_ref[0] = jnp.transpose(out_t).astype(BF)
    prod = out_t * jnp.transpose(do_all.astype(F32))
    delta = [
        jnp.sum(prod[:HEAD_DIM], axis=0, keepdims=True),
        jnp.sum(prod[HEAD_DIM:], axis=0, keepdims=True),
    ]

    def clear(j, carry):
        at = pl.ds(pl.multiple_of(j * CHUNK, CHUNK), CHUNK)
        dk_scr[at, :] = jnp.zeros((CHUNK, LANES), F32)
        dv_scr[at, :] = jnp.zeros((CHUNK, LANES), F32)
        return carry

    lax.fori_loop(0, lower, clear, 0)

    def backward(j, carry):
        at = pl.ds(pl.multiple_of(j * CHUNK, CHUNK), CHUNK)
        dk = jnp.zeros((CHUNK, LANES), F32)
        dv = jnp.zeros((CHUNK, LANES), F32)
        for h in range(2):
            prob = p_scr[h, at, :]
            dp = nt(v_scr[at, :], do_head[h])
            ds = (prob.astype(F32) * (dp - delta[h])).astype(BF)
            dv += mm(prob, do_head[h])
            dk += mm(ds, q_head[h])
            rows = pl.ds(h * HEAD_DIM, HEAD_DIM)
            dqt_scr[rows, :] += mm(kt_scr[rows, at], ds)
        dk_scr[at, :] = dk
        dv_scr[at, :] = dv
        return carry

    lax.fori_loop(lower, chunks, backward, 0)

    def lanes_at(block):
        return pl.ds(pl.multiple_of((block * pairs + p) * LANES, LANES), LANES)

    dq = jnp.transpose(dqt_scr[...]) * scale
    dqkv_ref[0, :, lanes_at(0)] = rotated(
        dq, keep_ref[own, :], -low_ref[own, :], -high_ref[own, :]
    ).astype(BF)
    for b in range(halo + 1):
        rows = pl.ds(b * tok, tok)
        dk = rotated(
            dk_scr[rows, :], keep_ref[rows, :], -low_ref[rows, :], -high_ref[rows, :]
        ).astype(BF)
        dv = dv_scr[rows, :].astype(BF)
        if b < halo:
            dkvh_ref[b, 0, :, lanes_at(0)] = dk
            dkvh_ref[b, 0, :, lanes_at(1)] = dv
        else:
            dqkv_ref[0, :, lanes_at(1)] = dk
            dqkv_ref[0, :, lanes_at(2)] = dv


def attention(qkv, kv_halo, grad_att, keep, low, high, starts, scalars):
    halo = kv_halo.shape[0]
    seqs, tok, width = qkv.shape
    pairs = width // 3 // LANES
    keys = (halo + 1) * tok
    row = lambda off: pl.BlockSpec((1, tok, LANES), lambda s, p, _: (s, 0, off + p))
    far = lambda off: pl.BlockSpec((halo, 1, tok, LANES), lambda s, p, _: (0, s, 0, off + p))
    table = pl.BlockSpec((keys, LANES), lambda s, p, _: (0, 0))
    flops = seqs * pairs * 2 * keys * tok * HEAD_DIM * 12 * 3
    return pl.pallas_call(
        functools.partial(attention_kernel, halo, tok),
        grid_spec=pltpu.PrefetchScalarGridSpec(
            num_scalar_prefetch=1,
            grid=(seqs, pairs),
            in_specs=[
                row(0),
                row(pairs),
                row(2 * pairs),
                far(0),
                far(pairs),
                row(0),
                table,
                table,
                table,
                pl.BlockSpec((1, 1, tok), lambda s, p, _: (s, 0, 0)),
            ],
            out_specs=[
                row(0),
                pl.BlockSpec((1, tok, width), lambda s, p, _: (s, 0, 0)),
                pl.BlockSpec((halo, 1, tok, width // 3 * 2), lambda s, p, _: (0, s, 0, 0)),
            ],
            scratch_shapes=[
                pltpu.VMEM((2, keys, tok), F32),
                pltpu.VMEM((2, keys, tok), BF),
                pltpu.VMEM((keys, LANES), BF),
                pltpu.VMEM((keys, LANES), BF),
                pltpu.VMEM((LANES, keys), BF),
                pltpu.VMEM((LANES, keys), BF),
                pltpu.VMEM((keys, LANES), F32),
                pltpu.VMEM((keys, LANES), F32),
                pltpu.VMEM((LANES, tok), F32),
                pltpu.VMEM((LANES, tok), F32),
            ],
        ),
        out_shape=[
            jax.ShapeDtypeStruct((seqs, tok, width // 3), BF),
            jax.ShapeDtypeStruct((seqs, tok, width), BF),
            jax.ShapeDtypeStruct((halo, seqs, tok, width // 3 * 2), BF),
        ],
        compiler_params=pltpu.CompilerParams(vmem_limit_bytes=48 << 20),
        cost_estimate=pl.CostEstimate(flops=flops, bytes_accessed=16 << 20, transcendentals=0),
        name="attention",
    )(scalars, qkv, qkv, qkv, kv_halo, kv_halo, grad_att, keep, low, high, starts)


def plane_gather(piece):
    half = piece.shape[0] // 2
    from_x = lax.ppermute(piece, "x", SWAP)
    from_y = lax.ppermute(piece, "y", SWAP)
    across = (lax.ppermute(from_x[:half], "y", SWAP), lax.ppermute(from_y[half:], "x", SWAP))
    return piece, from_x, from_y, jnp.concatenate(across, axis=0)


def plane_order(pieces, chip):
    whole = jnp.zeros((4,) + pieces[0].shape, pieces[0].dtype)
    for way, piece in enumerate(pieces):
        whole = lax.dynamic_update_index_in_dim(whole, piece, chip ^ way, 0)
    return whole


def plane_scatter(quarter):
    across = quarter(3)
    half = across.shape[0] // 2
    first = lax.ppermute(across[:half], "x", SWAP)
    second = lax.ppermute(across[half:], "y", SWAP)
    to_x, to_y = quarter(1), quarter(2)
    to_x = jnp.concatenate([to_x[:half], (to_x[half:].astype(F32) + second.astype(F32)).astype(BF)])
    to_y = jnp.concatenate([(to_y[:half].astype(F32) + first.astype(F32)).astype(BF), to_y[half:]])
    from_x = lax.ppermute(to_x, "x", SWAP)
    from_y = lax.ppermute(to_y, "y", SWAP)
    return quarter(0).astype(F32) + from_x.astype(F32) + from_y.astype(F32)


def z_gather(piece):
    return lax.all_gather(piece, "z", axis=0, tiled=False)


def z_scatter(piece):
    return lax.psum_scatter(piece, "z", scatter_dimension=0, tiled=False)


def normalise(tokens):
    row_mean = jnp.mean(tokens, axis=-1, keepdims=True)
    centered = tokens - row_mean
    variance = jnp.mean(centered * centered, axis=-1, keepdims=True)
    inv_std = lax.rsqrt(variance + 1e-05)
    return centered * inv_std, inv_std


def local_plane(
    nz,
    hidden_in,
    doc_lengths,
    ln_gain,
    ln_bias,
    w_qkv,
    b_qkv,
    w_dense,
    b_dense,
    w_in,
    b_in,
    w_out,
    b_out,
    out_grad,
):
    core = lax.axis_index("c")
    chip = lax.axis_index("y") * 2 + lax.axis_index("x")
    zi = lax.axis_index("z")
    halo = nz // 2
    _, tok, width = hidden_in.shape
    ff = w_in.shape[1]
    rows = w_in.shape[0]
    out_rows = w_out.shape[0]
    up = [(i, i + 1) for i in range(nz - 1)]
    down = [(i + 1, i) for i in range(nz - 1)]

    hidden_own = hidden_in[0]
    grad_own = out_grad[0]
    before = [hidden_own]
    for _ in range(halo):
        before.append(lax.ppermute(before[-1], "z", up))
    hidden_far_own = jnp.stack(before[:0:-1])
    hidden_other = other_core(hidden_own)
    grad_other = other_core(grad_own)
    lens_other = other_core(doc_lengths)
    hidden_far_other = other_core(hidden_far_own)

    def split(weight, parts):
        blocks = weight.reshape(rows, parts, 4, 2, -1)
        mine = lax.dynamic_index_in_dim(blocks, core, 3, keepdims=False).reshape(rows, -1)
        theirs = lax.dynamic_index_in_dim(blocks, 1 - core, 3, keepdims=False).reshape(rows, -1)
        return mine, theirs

    def by_core(mine, theirs):
        low = jnp.where(core == 0, mine, theirs)
        high = jnp.where(core == 0, theirs, mine)
        return jnp.stack([low, high])

    small_row = jnp.concatenate([ln_gain, ln_bias, b_qkv, b_dense, b_in, b_out])
    small_len = small_row.shape[0]
    qkv_mine, qkv_theirs = split(w_qkv, 3)
    in_mine, in_theirs = split(w_in, 1)
    qkv_w, in_w = qkv_mine.shape[1], in_mine.shape[1]
    sent = jnp.concatenate([qkv_theirs, in_theirs], axis=1)
    small_sent = jnp.zeros((16, sent.shape[1]), BF).at[0, :small_len].set(small_row)
    got = other_core(jnp.concatenate([sent, small_sent]))
    qkv_piece = by_core(qkv_mine, got[:rows, :qkv_w]).reshape(2 * rows, qkv_w)
    in_piece = by_core(in_mine, got[:rows, qkv_w:]).reshape(2 * rows, in_w)
    dense_piece = w_dense.reshape(rows, 2, width // 2).transpose(1, 0, 2).reshape(2 * rows, width // 2)
    first_piece = jnp.concatenate([qkv_piece, dense_piece], axis=1)
    small_pair = by_core(small_row, got[rows, :small_len])
    small_piece = jnp.zeros((16, first_piece.shape[1]), BF).at[:2, :small_len].set(small_pair)
    first_piece = jnp.concatenate([first_piece, small_piece])

    first = plane_gather(z_gather(first_piece))
    second = plane_gather(z_gather(in_piece))
    third = plane_gather(z_gather(w_out))

    def in_order(pieces, count, columns):
        whole = plane_order([p[:, :count, columns] for p in pieces], chip)
        return whole.reshape(4, nz, 2, count // 2, -1).transpose(0, 2, 1, 3, 4)

    w_qkv_f = in_order(first, 2 * rows, slice(0, qkv_w)).reshape(width, qkv_w)
    dense_f = plane_order([p[:, : 2 * rows, qkv_w:] for p in first], chip)
    dense_f = dense_f.reshape(4, nz, 2, rows, width // 2).transpose(0, 1, 3, 2, 4)
    w_dense_f = dense_f.reshape(width // 2, width)
    w_in_f = in_order(second, 2 * rows, slice(None)).reshape(width, in_w)
    w_out_f = plane_order(third, chip).reshape(ff // 2, width)

    small = plane_order([p[:, 2 * rows : 2 * rows + 2, :small_len] for p in first], chip)
    small = small.transpose(0, 2, 1, 3).reshape(8 * nz, small_len).astype(F32)
    sizes = [v.shape[0] for v in (ln_gain, ln_bias, b_qkv, b_dense, b_in, b_out)]
    cuts = [sum(sizes[:i]) for i in range(7)]
    gain, bias, qkv_bias, dense_bias, in_bias, out_bias = (
        small[:, cuts[i] : cuts[i + 1]].reshape(-1) for i in range(6)
    )

    def my_half(vector, parts):
        blocks = vector.reshape(parts, 4, 2, -1)
        return lax.dynamic_index_in_dim(blocks, core, 2, keepdims=False).reshape(-1)

    def spread(vector, parts):
        blocks = vector.reshape(parts, 4, 1, -1)
        mine = (jnp.arange(2) == core)[None, None, :, None]
        return jnp.where(mine, blocks, 0.0).reshape(-1)

    qkv_bias = my_half(qkv_bias, 3)
    in_bias = my_half(in_bias, 1)

    hidden = jnp.stack([hidden_own, hidden_other])
    hidden_far = jnp.stack([hidden_far_own, hidden_far_other], axis=1)
    grad_rows = jnp.stack([grad_own, grad_other]).reshape(2 * tok, width)

    def normed_of(values):
        return (normalise(values.astype(F32))[0] * gain + bias).astype(BF)

    normed = normed_of(hidden).reshape(2 * tok, width)
    normed_far = normed_of(hidden_far).reshape(halo * 2 * tok, width)

    part = qkv_w // 3
    qkv = (mm(normed, w_qkv_f) + qkv_bias).astype(BF).reshape(2, tok, qkv_w)
    kv_far = (mm(normed_far, w_qkv_f[:, part:]) + qkv_bias[part:]).astype(BF)
    grad_att = nt(grad_rows, w_dense_f).astype(BF).reshape(2, tok, part)

    base = (zi - halo) * tok
    positions = (base + jnp.arange((halo + 1) * tok, dtype=jnp.int32)).astype(F32)
    lane = jnp.arange(LANES, dtype=jnp.int32) % HEAD_DIM
    half_rot = ROT_DIM // 2
    frequency = jnp.exp(-math.log(10000.0) * 2.0 * (lane % half_rot).astype(F32) / ROT_DIM)
    angles = positions[:, None] * frequency[None, :]
    cosine, sine = jnp.cos(angles), jnp.sin(angles)
    keep = jnp.where(lane < ROT_DIM, cosine, 1.0)
    low = jnp.where(lane < half_rot, -sine, 0.0)
    high = jnp.where((lane >= half_rot) & (lane < ROT_DIM), sine, 0.0)

    def doc_starts(lens):
        ends = prefix_ends(lens)
        own = zi * tok + jnp.arange(tok, dtype=jnp.int32)
        return jnp.max(jnp.where(own[:, None] >= ends[None, :], ends[None, :], 0), axis=1)

    starts = jnp.stack([doc_starts(doc_lengths[0]), doc_starts(lens_other[0])])
    lower = jnp.clip((starts[:, 0] - base) // CHUNK, 0, halo * tok // CHUNK)
    scalars = jnp.concatenate([lower, base[None]]).astype(jnp.int32)
    attended, dqkv, dkv_far = attention(
        qkv,
        kv_far.reshape(halo, 2, tok, 2 * part),
        grad_att,
        keep,
        low,
        high,
        starts[:, None, :],
        scalars,
    )
    attended = attended.reshape(2 * tok, part)
    dqkv = dqkv.reshape(2 * tok, qkv_w)
    dkv_far = dkv_far.reshape(halo * 2 * tok, 2 * part)

    dn_far = nt(dkv_far, w_qkv_f[:, part:]).astype(BF).reshape(halo, 2, tok, width)
    dn_far = dn_far[:, 0].astype(F32) + other_core(dn_far[:, 1]).astype(F32)
    passed = dn_far[0].astype(BF)
    for step in range(1, halo):
        passed = (dn_far[step] + lax.ppermute(passed, "z", down).astype(F32)).astype(BF)
    dn_back = lax.ppermute(passed, "z", down).astype(F32)

    dkv_all = jnp.concatenate([dqkv[:, part:], dkv_far])
    g_kv = dot_rows(jnp.concatenate([normed, normed_far]), dkv_all)
    g_qkv = jnp.concatenate([dot_rows(normed, dqkv[:, :part]), g_kv], axis=1).astype(BF)
    g_dense = dot_rows(attended, grad_rows).astype(BF)
    g_qkv_bias = jnp.concatenate(
        [
            jnp.sum(dqkv[:, :part].astype(F32), axis=0),
            jnp.sum(dkv_all.astype(F32), axis=0),
        ]
    )
    dn_att = nt(dqkv, w_qkv_f)

    def quarters(full):
        blocks = full.reshape(4, -1, full.shape[-1])
        return lambda way: lax.dynamic_index_in_dim(blocks, chip ^ way, 0, keepdims=False)

    def home_core(mine_columns):
        mine = lax.dynamic_index_in_dim(mine_columns, core, 0, keepdims=False)
        theirs = lax.dynamic_index_in_dim(mine_columns, 1 - core, 0, keepdims=False)
        return by_core(mine, other_core(theirs))

    s_qkv = plane_scatter(quarters(g_qkv)).astype(BF)
    s_qkv = s_qkv.reshape(2, nz, rows, qkv_w).transpose(1, 0, 2, 3)
    s_qkv = home_core(z_scatter(s_qkv))
    grad_w_qkv = s_qkv.reshape(2, rows, 3, 4, -1).transpose(1, 2, 3, 0, 4).reshape(rows, -1).astype(F32)

    pre_act = mm(normed, w_in_f) + in_bias
    activated, gelu_back = jax.vjp(gelu_exact, pre_act)
    activated = activated.astype(BF)
    g_out = dot_rows(activated, grad_rows).astype(BF)
    q_out, q_dense = quarters(g_out), quarters(g_dense)
    s_out = plane_scatter(lambda way: jnp.concatenate([q_out(way), q_dense(way)]))
    s_out = jnp.concatenate(
        [
            s_out[: nz * out_rows].reshape(nz, out_rows, width),
            s_out[nz * out_rows :].reshape(nz, rows, width),
        ],
        axis=1,
    ).astype(BF)
    s_out = z_scatter(s_out).astype(F32)
    grad_w_out, grad_w_dense = s_out[:out_rows], s_out[out_rows:]

    grad_pre = gelu_back(nt(grad_rows, w_out_f))[0].astype(BF)
    branch = (mm(attended, w_dense_f) + mm(activated, w_out_f)).reshape(2, tok, width)
    x = hidden_own.astype(F32)
    hidden_out = (
        x + branch[0] + other_core(branch[1].astype(BF)).astype(F32) + dense_bias + out_bias
    ).astype(BF)

    dn = (dn_att + nt(grad_pre, w_in_f)).reshape(2, tok, width)
    dn = dn[0] + other_core(dn[1].astype(BF)).astype(F32) + dn_back
    xhat, inv_std = normalise(x)
    scaled = dn * gain
    gy = grad_own.astype(F32)
    grad_input = gy + inv_std * (
        scaled
        - jnp.mean(scaled, axis=1, keepdims=True)
        - xhat * jnp.mean(scaled * xhat, axis=1, keepdims=True)
    )

    gy_sum = jnp.sum(gy, axis=0)
    small_grads = [
        jnp.sum(dn * xhat, axis=0),
        jnp.sum(dn, axis=0),
        spread(g_qkv_bias, 3),
        gy_sum,
        spread(jnp.sum(grad_pre.astype(F32), axis=0), 1),
    ]
    small_g = jnp.concatenate([g.reshape(4, 2, nz, -1) for g in small_grads], axis=3).astype(BF)
    g_len = small_g.shape[3]
    small_g = small_g.transpose(0, 2, 1, 3)
    small_g = jnp.pad(small_g, ((0, 0), (0, 0), (0, 14), (0, in_w - g_len)))
    extra = small_g.shape[2]
    q_small = quarters(small_g.reshape(4, nz * extra, in_w))
    g_in = dot_rows(normed, grad_pre).astype(BF)
    q_in = quarters(g_in)
    s_in = plane_scatter(lambda way: jnp.concatenate([q_in(way), q_small(way)]))
    body = s_in[: 2 * nz * rows].reshape(2, nz, rows, in_w).transpose(1, 0, 2, 3)
    s_in = jnp.concatenate(
        [body.reshape(nz, 2 * rows, in_w), s_in[2 * nz * rows :].reshape(nz, extra, in_w)], axis=1
    ).astype(BF)
    s_in = z_scatter(s_in)
    small_mine = s_in[2 * rows : 2 * rows + 2]
    mine = lax.dynamic_index_in_dim(small_mine, core, 0, keepdims=False)
    theirs = lax.dynamic_index_in_dim(small_mine, 1 - core, 0, keepdims=False)
    g_small = mine.astype(F32) + other_core(theirs).astype(F32)
    offs = [0]
    for v in (ln_gain, ln_bias, b_qkv, b_dense, b_in):
        offs.append(offs[-1] + v.shape[0])
    g_gain, g_bias, g_bqkv, g_bdense, g_bin = (g_small[offs[i] : offs[i + 1]] for i in range(5))
    s_in = home_core(s_in[: 2 * rows].reshape(2, rows, in_w))
    grad_w_in = s_in.reshape(2, rows, 4, -1).transpose(1, 2, 0, 3).reshape(rows, -1).astype(F32)
    return (
        hidden_out[None],
        grad_input[None],
        g_gain,
        g_bias,
        grad_w_qkv,
        g_bqkv,
        grad_w_dense,
        g_bdense,
        grad_w_in,
        g_bin,
        grad_w_out,
        g_bdense,
    )


def solution(mesh):
    n_seq, n_group = mesh.devices.shape
    if n_seq == 8 and n_group == 4:
        mesh = Mesh(mesh.devices.reshape(2, 2, 2, n_group), ("y", "x", "c", "z"))
        seq, group = ("y", "x", "c"), "z"
        both = ("y", "x", "c", "z")
        step = functools.partial(local_plane, n_group)
    else:
        seq, group, both = "seq", "group", ("seq", "group")
        step = local_generic
    matrix, vector = P(both, None), P(both)
    tokens = P(seq, group, None)
    weights = (vector, vector) + (matrix, vector) * 4
    return jax.shard_map(
        step,
        mesh=mesh,
        in_specs=(tokens, P(seq, None)) + weights + (tokens,),
        out_specs=(tokens, tokens) + weights,
        check_vma=False,
    )
```

```python
import functools
import math

import jax
import jax.numpy as jnp
from jax import lax
from jax.experimental import pallas as pl
from jax.experimental.pallas import tpu as pltpu
from jax.sharding import Mesh
from jax.sharding import PartitionSpec as P

HEADS = 16
HEAD_DIM = 64
ROT_DIM = 16


def prefix_ends(doc_lens):
    order = jnp.arange(doc_lens.shape[0], dtype=jnp.int32)
    return jnp.sum(jnp.where(order[None, :] <= order[:, None], doc_lens[None, :], 0), axis=1)


def dot_rows(left, right):
    return lax.dot_general(
        left, right, (((0,), (0,)), ((), ())), preferred_element_type=jnp.float32
    )


def dot_last(left, right):
    return lax.dot_general(
        left, right, (((1,), (1,)), ((), ())), preferred_element_type=jnp.float32
    )


def rope_tables(token_positions, rot_dim):
    half_rot = rot_dim // 2
    frequency = jnp.exp(
        -math.log(10000.0) * 2.0 * jnp.arange(half_rot, dtype=jnp.float32) / rot_dim
    )
    angles = token_positions.astype(jnp.float32)[:, None] * frequency[None, :]
    return (jnp.cos(angles)[:, None, :], jnp.sin(angles)[:, None, :])


def rotate(heads, cosine, sine, rot_dim):
    half_rot = rot_dim // 2
    first_half = heads[:, :, :half_rot]
    second_half = heads[:, :, half_rot:rot_dim]
    remainder = heads[:, :, rot_dim:]
    return jnp.concatenate(
        [
            first_half * cosine - second_half * sine,
            second_half * cosine + first_half * sine,
            remainder,
        ],
        axis=2,
    )


def gelu_exact(preact):
    return jax.nn.gelu(preact, approximate=False)


def block_scores(query_block, key_tile_block, seg_query, seg_key, pos_query, pos_key, score_scale):
    scaled = (
        jnp.einsum("qhd,khd->hqk", query_block, key_tile_block, preferred_element_type=jnp.float32)
        * score_scale
    )
    allowed = (seg_query[:, None] == seg_key[None, :]) & (pos_key[None, :] <= pos_query[:, None])
    return jnp.where(allowed[None], scaled, -1e30)


def owning_block(source, block_index, block_of_rows):
    return lax.dynamic_slice_in_dim(source, block_index * block_of_rows, block_of_rows, 0)


def add_block(source, block_index, block_of_rows, addend):
    current = owning_block(source, block_index, block_of_rows)
    return lax.dynamic_update_slice_in_dim(source, current + addend, block_index * block_of_rows, 0)


def attention_forward(
    query_heads,
    key_head_rows,
    value_head_rows,
    document_segment,
    token_positions,
    seg_start,
    block_of_rows,
):
    seq_len, head_count, head_dim = query_heads.shape
    score_scale = 1.0 / math.sqrt(head_dim)

    def query_step(qindex, state_now):
        outputs, log_sums = state_now
        query_block = owning_block(query_heads, qindex, block_of_rows)
        seg_query = owning_block(document_segment, qindex, block_of_rows)
        pos_query = owning_block(token_positions, qindex, block_of_rows)
        key_lower = seg_start[qindex * block_of_rows] // block_of_rows

        def scores_for_block(key_position_index):
            return block_scores(
                query_block,
                owning_block(key_head_rows, key_position_index, block_of_rows),
                seg_query,
                owning_block(document_segment, key_position_index, block_of_rows),
                pos_query,
                owning_block(token_positions, key_position_index, block_of_rows),
                score_scale,
            )

        def statistics_step(key_position_index, row_statistics):
            run_max, run_sum = row_statistics
            logit_scores = scores_for_block(key_position_index)
            new_max = jnp.maximum(run_max, jnp.max(logit_scores, axis=2))
            run_sum = run_sum * jnp.exp(run_max - new_max) + jnp.sum(
                jnp.exp(logit_scores - new_max[:, :, None]), axis=2
            )
            return (new_max, run_sum)

        start_stats = (
            jnp.full((head_count, block_of_rows), -1e30, jnp.float32),
            jnp.zeros((head_count, block_of_rows), jnp.float32),
        )
        run_max, run_sum = lax.fori_loop(key_lower, qindex + 1, statistics_step, start_stats)
        log_exp_total = run_max + jnp.log(run_sum)

        def value_loop_step(key_position_index, partial_output):
            attention_weights = jnp.exp(
                scores_for_block(key_position_index) - log_exp_total[:, :, None]
            ).astype(jnp.bfloat16)
            return partial_output + jnp.einsum(
                "hqk,khd->qhd",
                attention_weights,
                owning_block(value_head_rows, key_position_index, block_of_rows),
                preferred_element_type=jnp.float32,
            )

        block_out = lax.fori_loop(
            key_lower,
            qindex + 1,
            value_loop_step,
            jnp.zeros((block_of_rows, head_count, head_dim), jnp.float32),
        )
        outputs = lax.dynamic_update_slice_in_dim(outputs, block_out, qindex * block_of_rows, 0)
        log_sums = lax.dynamic_update_slice_in_dim(
            log_sums, log_exp_total, qindex * block_of_rows, 1
        )
        return (outputs, log_sums)

    start_state = (
        jnp.zeros((seq_len, head_count, head_dim), jnp.float32),
        jnp.zeros((head_count, seq_len), jnp.float32),
    )
    return lax.fori_loop(0, seq_len // block_of_rows, query_step, start_state)


def attention_backward(
    query_heads,
    key_head_rows,
    value_head_rows,
    grad_heads,
    outputs,
    log_sums,
    document_segment,
    token_positions,
    seg_start,
    block_of_rows,
):
    seq_len, head_count, head_dim = query_heads.shape
    score_scale = 1.0 / math.sqrt(head_dim)
    delta_all = jnp.sum(grad_heads.astype(jnp.float32) * outputs, axis=2).T

    def query_step(qindex, state_now):
        grad_query_all, grad_key_all, grad_value_all = state_now
        query_block = owning_block(query_heads, qindex, block_of_rows)
        grad_block = owning_block(grad_heads, qindex, block_of_rows)
        seg_query = owning_block(document_segment, qindex, block_of_rows)
        pos_query = owning_block(token_positions, qindex, block_of_rows)
        log_exp_total = lax.dynamic_slice_in_dim(log_sums, qindex * block_of_rows, block_of_rows, 1)
        delta_block = lax.dynamic_slice_in_dim(delta_all, qindex * block_of_rows, block_of_rows, 1)
        key_lower = seg_start[qindex * block_of_rows] // block_of_rows

        def key_loop_step(key_position_index, loop_state_inner):
            grad_query, grad_keys, grad_values = loop_state_inner
            key_tile_block = owning_block(key_head_rows, key_position_index, block_of_rows)
            value_tile_block = owning_block(value_head_rows, key_position_index, block_of_rows)
            logit_scores = block_scores(
                query_block,
                key_tile_block,
                seg_query,
                owning_block(document_segment, key_position_index, block_of_rows),
                pos_query,
                owning_block(token_positions, key_position_index, block_of_rows),
                score_scale,
            )
            probability = jnp.exp(logit_scores - log_exp_total[:, :, None])
            grad_values = add_block(
                grad_values,
                key_position_index,
                block_of_rows,
                jnp.einsum(
                    "hqk,qhd->khd",
                    probability.astype(jnp.bfloat16),
                    grad_block,
                    preferred_element_type=jnp.float32,
                ),
            )
            grad_probs = jnp.einsum(
                "qhd,khd->hqk", grad_block, value_tile_block, preferred_element_type=jnp.float32
            )
            grad_scores = (probability * (grad_probs - delta_block[:, :, None])).astype(
                jnp.bfloat16
            )
            grad_query = (
                grad_query
                + jnp.einsum(
                    "hqk,khd->qhd", grad_scores, key_tile_block, preferred_element_type=jnp.float32
                )
                * score_scale
            )
            grad_keys = add_block(
                grad_keys,
                key_position_index,
                block_of_rows,
                jnp.einsum(
                    "hqk,qhd->khd", grad_scores, query_block, preferred_element_type=jnp.float32
                )
                * score_scale,
            )
            return (grad_query, grad_keys, grad_values)

        start_inner = (
            jnp.zeros((block_of_rows, head_count, head_dim), jnp.float32),
            grad_key_all,
            grad_value_all,
        )
        grad_query, grad_key_all, grad_value_all = lax.fori_loop(
            key_lower, qindex + 1, key_loop_step, start_inner
        )
        grad_query_all = lax.dynamic_update_slice_in_dim(
            grad_query_all, grad_query, qindex * block_of_rows, 0
        )
        return (grad_query_all, grad_key_all, grad_value_all)

    zero_heads = jnp.zeros((seq_len, head_count, head_dim), jnp.float32)
    return lax.fori_loop(
        0, seq_len // block_of_rows, query_step, (zero_heads, zero_heads, zero_heads)
    )


def local_generic(
    hidden_in,
    doc_lengths,
    ln_gain,
    ln_bias,
    w_qkv,
    b_qkv,
    w_dense,
    b_dense,
    w_in,
    b_in,
    w_out,
    b_out,
    out_grad,
):
    (
        full_gain,
        full_bias,
        full_qkv,
        full_qkv_bias,
        full_dense,
        full_dense_bias,
        full_in,
        full_in_bias,
        full_out,
        full_out_bias,
    ) = (
        lax.all_gather(ln_gain, ("seq", "group"), axis=0, tiled=True),
        lax.all_gather(ln_bias, ("seq", "group"), axis=0, tiled=True),
        lax.all_gather(w_qkv, ("seq", "group"), axis=0, tiled=True),
        lax.all_gather(b_qkv, ("seq", "group"), axis=0, tiled=True),
        lax.all_gather(w_dense, ("seq", "group"), axis=0, tiled=True),
        lax.all_gather(b_dense, ("seq", "group"), axis=0, tiled=True),
        lax.all_gather(w_in, ("seq", "group"), axis=0, tiled=True),
        lax.all_gather(b_in, ("seq", "group"), axis=0, tiled=True),
        lax.all_gather(w_out, ("seq", "group"), axis=0, tiled=True),
        lax.all_gather(b_out, ("seq", "group"), axis=0, tiled=True),
    )
    tokens = hidden_in[0].astype(jnp.float32)
    tok_count = tokens.shape[0]
    width = tokens.shape[1]
    row_mean = jnp.mean(tokens, axis=1, keepdims=True)
    centered = tokens - row_mean
    variance = jnp.mean(centered * centered, axis=1, keepdims=True)
    inv_std = lax.rsqrt(variance + 1e-05)
    normal_rows = centered * inv_std
    normed = (normal_rows * full_gain.astype(jnp.float32) + full_bias.astype(jnp.float32)).astype(
        jnp.bfloat16
    )
    mixed = jnp.dot(normed, full_qkv, preferred_element_type=jnp.float32) + full_qkv_bias.astype(
        jnp.float32
    )
    token_positions = lax.axis_index("group") * tok_count + jnp.arange(tok_count, dtype=jnp.int32)
    cosine, sine = rope_tables(token_positions, ROT_DIM)
    head_shape = (tok_count, HEADS, HEAD_DIM)
    queries = (
        rotate(mixed[:, :width].reshape(head_shape), cosine, sine, ROT_DIM)
        .reshape(tok_count, width)
        .astype(jnp.bfloat16)
    )
    key_rows = (
        rotate(mixed[:, width : 2 * width].reshape(head_shape), cosine, sine, ROT_DIM)
        .reshape(tok_count, width)
        .astype(jnp.bfloat16)
    )
    value_rows = mixed[:, 2 * width :].astype(jnp.bfloat16)
    query_cols, key_cols, value_cols = (
        lax.all_to_all(queries, "group", split_axis=1, concat_axis=0, tiled=True),
        lax.all_to_all(key_rows, "group", split_axis=1, concat_axis=0, tiled=True),
        lax.all_to_all(value_rows, "group", split_axis=1, concat_axis=0, tiled=True),
    )
    seq_len = query_cols.shape[0]
    head_count = query_cols.shape[1] // HEAD_DIM
    heads_shape = (seq_len, head_count, HEAD_DIM)
    query_heads = query_cols.reshape(heads_shape)
    key_head_rows = key_cols.reshape(heads_shape)
    value_head_rows = value_cols.reshape(heads_shape)
    all_pos = jnp.arange(seq_len, dtype=jnp.int32)
    doc_lens = doc_lengths[0]
    doc_ends = prefix_ends(doc_lens)
    document_segment = jnp.sum((all_pos[:, None] >= doc_ends[None, :]).astype(jnp.int32), axis=1)
    doc_starts = doc_ends - doc_lens
    doc_index = jnp.arange(doc_ends.shape[0], dtype=jnp.int32)
    seg_start = jnp.sum(
        jnp.where(document_segment[:, None] == doc_index[None, :], doc_starts[None, :], 0), axis=1
    )
    block_of_rows = min(512, seq_len)
    outputs, log_sums = attention_forward(
        query_heads,
        key_head_rows,
        value_head_rows,
        document_segment,
        all_pos,
        seg_start,
        block_of_rows,
    )
    attended = lax.all_to_all(
        outputs.reshape(seq_len, head_count * HEAD_DIM).astype(jnp.bfloat16),
        "group",
        split_axis=0,
        concat_axis=1,
        tiled=True,
    )
    branch_attn = jnp.dot(
        attended, full_dense, preferred_element_type=jnp.float32
    ) + full_dense_bias.astype(jnp.float32)
    pre_act = jnp.dot(normed, full_in, preferred_element_type=jnp.float32) + full_in_bias.astype(
        jnp.float32
    )
    activated = gelu_exact(pre_act).astype(jnp.bfloat16)
    branch_mlp = jnp.dot(
        activated, full_out, preferred_element_type=jnp.float32
    ) + full_out_bias.astype(jnp.float32)
    hidden_out = (tokens + branch_attn + branch_mlp).astype(jnp.bfloat16)
    grad_rows = out_grad[0]
    grad_float = grad_rows.astype(jnp.float32)
    bias_grad = jnp.sum(grad_float, axis=0)
    grad_dense = dot_rows(attended, grad_rows)
    grad_out_w = dot_rows(activated, grad_rows)
    grad_act = dot_last(grad_rows, full_out)
    grad_pre = jax.vjp(gelu_exact, pre_act)[1](grad_act)[0].astype(jnp.bfloat16)
    grad_in_w = dot_rows(normed, grad_pre)
    grad_in_bias = jnp.sum(grad_pre.astype(jnp.float32), axis=0)
    grad_normed = dot_last(grad_pre, full_in)
    grad_attended = dot_last(grad_rows, full_dense).astype(jnp.bfloat16)
    grad_cols = lax.all_to_all(grad_attended, "group", split_axis=1, concat_axis=0, tiled=True)
    grad_query_all, grad_key_all, grad_value_all = attention_backward(
        query_heads,
        key_head_rows,
        value_head_rows,
        grad_cols.reshape(heads_shape),
        outputs,
        log_sums,
        document_segment,
        all_pos,
        seg_start,
        block_of_rows,
    )
    flat_shape = (seq_len, head_count * HEAD_DIM)
    grad_query_tok, grad_key_tok, grad_value_tok = (
        lax.all_to_all(
            grad_query_all.reshape(flat_shape).astype(jnp.bfloat16),
            "group",
            split_axis=0,
            concat_axis=1,
            tiled=True,
        ),
        lax.all_to_all(
            grad_key_all.reshape(flat_shape).astype(jnp.bfloat16),
            "group",
            split_axis=0,
            concat_axis=1,
            tiled=True,
        ),
        lax.all_to_all(
            grad_value_all.reshape(flat_shape).astype(jnp.bfloat16),
            "group",
            split_axis=0,
            concat_axis=1,
            tiled=True,
        ),
    )
    unrot_query = (
        rotate(grad_query_tok.astype(jnp.float32).reshape(head_shape), cosine, -sine, ROT_DIM)
        .reshape(tok_count, width)
        .astype(jnp.bfloat16)
    )
    unrot_key = (
        rotate(grad_key_tok.astype(jnp.float32).reshape(head_shape), cosine, -sine, ROT_DIM)
        .reshape(tok_count, width)
        .astype(jnp.bfloat16)
    )
    grad_mixed = jnp.concatenate([unrot_query, unrot_key, grad_value_tok], axis=1)
    grad_qkv_w = dot_rows(normed, grad_mixed)
    grad_qkv_bias = jnp.sum(grad_mixed.astype(jnp.float32), axis=0)
    grad_normed = grad_normed + dot_last(grad_mixed, full_qkv)
    scaled_grad = grad_normed * full_gain.astype(jnp.float32)
    grad_gain = jnp.sum(grad_normed * normal_rows, axis=0)
    grad_bias = jnp.sum(grad_normed, axis=0)
    grad_input = grad_float + inv_std * (
        scaled_grad
        - jnp.mean(scaled_grad, axis=1, keepdims=True)
        - normal_rows * jnp.mean(scaled_grad * normal_rows, axis=1, keepdims=True)
    )
    sharded = tuple(
        (
            lax.psum_scatter(grad_gain, ("seq", "group"), scatter_dimension=0, tiled=True),
            lax.psum_scatter(grad_bias, ("seq", "group"), scatter_dimension=0, tiled=True),
            lax.psum_scatter(grad_qkv_w, ("seq", "group"), scatter_dimension=0, tiled=True),
            lax.psum_scatter(grad_qkv_bias, ("seq", "group"), scatter_dimension=0, tiled=True),
            lax.psum_scatter(grad_dense, ("seq", "group"), scatter_dimension=0, tiled=True),
            lax.psum_scatter(bias_grad, ("seq", "group"), scatter_dimension=0, tiled=True),
            lax.psum_scatter(grad_in_w, ("seq", "group"), scatter_dimension=0, tiled=True),
            lax.psum_scatter(grad_in_bias, ("seq", "group"), scatter_dimension=0, tiled=True),
            lax.psum_scatter(grad_out_w, ("seq", "group"), scatter_dimension=0, tiled=True),
            lax.psum_scatter(bias_grad, ("seq", "group"), scatter_dimension=0, tiled=True),
        )
    )
    return (hidden_out[None], grad_input[None]) + sharded


SWAP = [(0, 1), (1, 0)]
CHUNK = 256
LANES = 128
BF = jnp.bfloat16
F32 = jnp.float32
ANY = pl.BlockSpec(memory_space=pl.ANY)
SMALL = pl.CostEstimate(flops=0, bytes_accessed=1 << 20, transcendentals=0)


def mm(left, right):
    return jnp.dot(left, right, preferred_element_type=F32)


def other_core(value):
    return lax.ppermute(value, "c", SWAP)


def over_x(value):
    return lax.ppermute(value, "x", SWAP)


def over_y(value):
    return lax.ppermute(value, "y", SWAP)


def nt(left, right):
    return lax.dot_general(left, right, (((1,), (1,)), ((), ())), preferred_element_type=F32)


def tn(left, right):
    return lax.dot_general(left, right, (((0,), (0,)), ((), ())), preferred_element_type=F32)


def matmul(left, right, form, deps=(), bias=None, block=512, dtype=BF, rows=None):
    rows = rows or (left.shape[1] if form == "tn" else left.shape[0])
    depth = left.shape[0] if form == "tn" else left.shape[1]
    columns = right.shape[0] if form == "nt" else right.shape[1]
    block = min(block, rows)
    dot = {"nn": mm, "nt": nt, "tn": tn}[form]

    def body(left_ref, right_ref, *rest):
        value = dot(left_ref[...], right_ref[...])
        if bias is not None:
            value = value + rest[0][...]
        rest[-1][...] = value.astype(dtype)

    if form == "tn":
        left_spec = pl.BlockSpec((depth, block), lambda i: (0, i))
    else:
        left_spec = pl.BlockSpec((block, depth), lambda i: (i, 0))
    whole = pl.BlockSpec(right.shape, lambda i: (0, 0))
    row = [] if bias is None else [pl.BlockSpec((1, columns), lambda i: (0, 0))]
    given = [] if bias is None else [bias.reshape(1, columns)]
    return pl.pallas_call(
        body,
        grid=(rows // block,),
        in_specs=[left_spec, whole] + row + [ANY] * len(deps),
        out_specs=pl.BlockSpec((block, columns), lambda i: (i, 0)),
        out_shape=jax.ShapeDtypeStruct((rows, columns), dtype),
        compiler_params=pltpu.CompilerParams(vmem_limit_bytes=48 << 20),
        cost_estimate=SMALL,
        name="matmul_" + form,
    )(left, right, *given, *deps)


def held(value, *deps):
    def body(*refs):
        pass

    return pl.pallas_call(
        body,
        in_specs=[ANY] * (1 + len(deps)),
        out_specs=ANY,
        out_shape=jax.ShapeDtypeStruct(value.shape, value.dtype),
        input_output_aliases={0: 0},
        compiler_params=pltpu.CompilerParams(vmem_limit_bytes=1 << 20),
        name="held",
    )(value, *deps)


def gelu_parts(value):
    size = jnp.abs(value)
    t = 1.0 / (1.0 + (0.3275911 / math.sqrt(2.0)) * size)
    poly = t * (
        0.254829592
        + t * (-0.284496736 + t * (1.421413741 + t * (-1.453152027 + t * 1.061405429)))
    )
    density = jnp.exp(-0.5 * value * value)
    tail = 0.5 * poly * density
    below = jnp.where(value < 0, tail, 1.0 - tail)
    return value * below, below + value * density * (1.0 / math.sqrt(2.0 * math.pi))


def feed_forward(normed, grads, w_in, bias, w_out, deps=(), block=256):
    tokens, width = normed.shape
    units = w_in.shape[1]

    def body(n_ref, g_ref, wi_ref, b_ref, wo_ref, *rest):
        act_ref, pre_ref, sum_ref = rest[-3:]
        value, slope = gelu_parts(mm(n_ref[...], wi_ref[...]) + b_ref[...])
        act_ref[...] = value.astype(BF)
        grad_pre = (slope * nt(g_ref[...], wo_ref[...])).astype(BF)
        pre_ref[...] = grad_pre
        total = jnp.sum(grad_pre.astype(F32).reshape(block // 8, 8, units), axis=0)

        @pl.when(pl.program_id(0) == 0)
        def _():
            sum_ref[...] = total

        @pl.when(pl.program_id(0) != 0)
        def _():
            sum_ref[...] += total

    rows = lambda n: pl.BlockSpec((block, n), lambda i: (i, 0))
    whole = lambda a: pl.BlockSpec(a.shape, lambda i: (0, 0))
    bias = bias.reshape(1, units)
    return pl.pallas_call(
        body,
        grid=(tokens // block,),
        in_specs=[rows(width), rows(width), whole(w_in), whole(bias), whole(w_out)]
        + [ANY] * len(deps),
        out_specs=[rows(units), rows(units), pl.BlockSpec((8, units), lambda i: (0, 0))],
        out_shape=[
            jax.ShapeDtypeStruct((tokens, units), BF),
            jax.ShapeDtypeStruct((tokens, units), BF),
            jax.ShapeDtypeStruct((8, units), F32),
        ],
        compiler_params=pltpu.CompilerParams(vmem_limit_bytes=48 << 20),
        cost_estimate=SMALL,
        name="feed_forward",
    )(normed, grads, w_in, bias, w_out, *deps)


def attention_kernel(halo, tok, heads, scalar_ref, q_ref, k_ref, v_ref, do_ref, keep_ref, sine_ref, start_ref, *rest):
    att_ref, dq_ref, dkv_ref = rest[-13:-10]
    s_scr, p_scr, k_scr, v_scr, kt_scr, vt_scr, dk_scr, dv_scr, ot_scr, dqt_scr = rest[-10:]
    s, p = pl.program_id(0), pl.program_id(1)
    groups = pl.num_programs(1)
    lanes = heads * HEAD_DIM
    blocks = tok // CHUNK
    chunks = (halo + 1) * blocks
    base = scalar_ref[2 * blocks]
    scale = 1.0 / math.sqrt(HEAD_DIM)
    row = lax.broadcasted_iota(jnp.int32, (CHUNK, CHUNK), 0)
    column = lax.broadcasted_iota(jnp.int32, (CHUNK, CHUNK), 1)
    unit = (row == column).astype(F32).astype(BF)
    from_lane = lax.broadcasted_iota(jnp.int32, (lanes, lanes), 0)
    to_lane = lax.broadcasted_iota(jnp.int32, (lanes, lanes), 1)
    half_rot = ROT_DIM // 2
    place = to_lane % HEAD_DIM
    turn = jnp.where((place < half_rot) & (from_lane == to_lane + half_rot), -1.0, 0.0)
    turn = jnp.where(
        (place >= half_rot) & (place < ROT_DIM) & (from_lane == to_lane - half_rot), 1.0, turn
    ).astype(BF)
    head_of = lax.broadcasted_iota(jnp.int32, (CHUNK, lanes), 1) // HEAD_DIM
    zero = jnp.zeros((CHUNK, lanes), BF)

    def flip(value):
        return nt(unit, value)

    def wide(table_ref, at):
        value = table_ref[at, :]
        return jnp.concatenate([value] * (lanes // LANES), axis=1)

    def chunk_at(j):
        return pl.ds(pl.multiple_of(j * CHUNK, CHUNK), CHUNK)

    def turned(value, at, sign):
        return value.astype(F32) * wide(keep_ref, at) + mm(value, turn) * (sign * wide(sine_ref, at))

    def by_head(value):
        return [jnp.where(head_of == h, value, zero) for h in range(heads)]

    def prepare(j, carry):
        at = chunk_at(j)
        inner = pl.ds(pl.multiple_of((j % blocks) * CHUNK, CHUNK), CHUNK)
        v_raw = v_ref[j // blocks, 0, inner, :]
        k_rot = turned(k_ref[j // blocks, 0, inner, :], at, 1.0).astype(BF)
        k_scr[at, :] = k_rot
        kt_scr[:, at] = nt_t(k_rot)
        v_scr[at, :] = v_raw
        vt_scr[:, at] = nt_t(v_raw)
        return carry

    unit_lanes = (from_lane == to_lane).astype(F32).astype(BF)

    def nt_t(value):
        return nt(unit_lanes, value).astype(BF)

    lowest = scalar_ref[s * blocks]

    lax.fori_loop(lowest, chunks, prepare, 0)

    def clear(j, carry):
        at = chunk_at(j)
        dk_scr[at, :] = jnp.zeros((CHUNK, lanes), F32)
        dv_scr[at, :] = jnp.zeros((CHUNK, lanes), F32)
        return carry

    lax.fori_loop(0, chunks, clear, 0)

    for b in range(blocks):
        lower = scalar_ref[s * blocks + b]
        upper = halo * blocks + b + 1
        inner = pl.ds(b * CHUNK, CHUNK)
        own = pl.ds((halo * blocks + b) * CHUNK, CHUNK)
        q_rot = turned(q_ref[0, inner, :], own, 1.0).astype(BF)
        q_head = by_head((q_rot.astype(F32) * scale).astype(BF))
        grad_out = do_ref[0, inner, :]
        start = start_ref[0, :, inner] - base
        q_pos = (halo * blocks + b) * CHUNK + column

        def scores(j, tops):
            at = chunk_at(j)
            k_pos = j * CHUNK + row
            allowed = (k_pos >= start) & (k_pos <= q_pos)
            keys = k_scr[at, :]
            out = []
            for h in range(heads):
                value = jnp.where(allowed, nt(keys, q_head[h]), -1e30)
                s_scr[h, at, :] = value
                out.append(
                    jnp.maximum(tops[h], jnp.max(value.reshape(CHUNK // 8, 8, CHUNK), axis=0))
                )
            return tuple(out)

        tops = lax.fori_loop(
            lower, upper, scores, (jnp.full((8, CHUNK), -1e30, F32),) * heads
        )
        tops = [jnp.max(t, axis=0, keepdims=True) for t in tops]
        ot_scr[...] = jnp.zeros_like(ot_scr)
        dqt_scr[...] = jnp.zeros_like(dqt_scr)

        def weigh(j, sums):
            at = chunk_at(j)
            out = []
            for h in range(heads):
                value = jnp.exp(s_scr[h, at, :] - tops[h])
                out.append(sums[h] + jnp.sum(value.reshape(CHUNK // 8, 8, CHUNK), axis=0))
                value = value.astype(BF)
                p_scr[h, at, :] = value
                rows = pl.ds(h * HEAD_DIM, HEAD_DIM)
                ot_scr[rows, :] += mm(vt_scr[rows, at], value)
            return tuple(out)

        sums = lax.fori_loop(lower, upper, weigh, (jnp.zeros((8, CHUNK), F32),) * heads)
        inverse = [1.0 / jnp.sum(t, axis=0, keepdims=True) for t in sums]
        out_t = jnp.concatenate(
            [ot_scr[h * HEAD_DIM : (h + 1) * HEAD_DIM, :] * inverse[h] for h in range(heads)]
        )
        att_ref[0, inner, :] = flip(out_t.astype(BF)).astype(BF)
        scaled = grad_out.astype(F32)
        spread = jnp.zeros((CHUNK, lanes), F32)
        for h in range(heads):
            down = jnp.transpose(jnp.broadcast_to(inverse[h], (LANES, CHUNK)))
            down = jnp.concatenate([down] * (lanes // LANES), axis=1)
            spread = jnp.where(head_of == h, down, spread)
        scaled = (scaled * spread).astype(BF)
        prod = out_t * nt(unit_lanes, scaled)
        delta = [
            jnp.sum(prod[h * HEAD_DIM : (h + 1) * HEAD_DIM], axis=0, keepdims=True)
            for h in range(heads)
        ]
        do_head = by_head(scaled)

        def backward(j, carry):
            at = chunk_at(j)
            values = v_scr[at, :]
            dk, dv = dk_scr[at, :], dv_scr[at, :]
            for h in range(heads):
                prob = p_scr[h, at, :]
                ds = (prob.astype(F32) * (nt(values, do_head[h]) - delta[h])).astype(BF)
                dv += mm(prob, do_head[h])
                dk += mm(ds, q_head[h])
                rows = pl.ds(h * HEAD_DIM, HEAD_DIM)
                dqt_scr[rows, :] += mm(kt_scr[rows, at], ds)
            dk_scr[at, :] = dk
            dv_scr[at, :] = dv
            return carry

        lax.fori_loop(lower, upper, backward, 0)
        dq = (flip((dqt_scr[...] * scale).astype(BF))).astype(BF)
        dq_ref[0, inner, :] = turned(dq, own, -1.0).astype(BF)

    for j in range(chunks):
        at = pl.ds(j * CHUNK, CHUNK)
        inner = pl.ds((j % blocks) * CHUNK, CHUNK)
        dk = turned(dk_scr[at, :].astype(BF), at, -1.0).astype(BF)
        for k, value in enumerate((dk, dv_scr[at, :].astype(BF))):
            columns = pl.ds(pl.multiple_of((k * groups + p) * lanes, LANES), lanes)
            dkv_ref[j // blocks, 0, inner, columns] = value


def attention(queries, key_values, grad_att, keep, sine, starts, scalars, deps=(), heads=4):
    spans, seqs, tok, width = key_values.shape
    halo = spans - 1
    lanes = heads * HEAD_DIM
    groups = width // 2 // lanes
    keys = spans * tok
    row = pl.BlockSpec((1, tok, lanes), lambda s, p, _: (s, 0, p))
    far = lambda off: pl.BlockSpec((spans, 1, tok, lanes), lambda s, p, _: (0, s, 0, off + p))
    table = pl.BlockSpec((keys, LANES), lambda s, p, _: (0, 0))
    flops = seqs * groups * heads * keys * tok * HEAD_DIM * 12 * 3
    return pl.pallas_call(
        functools.partial(attention_kernel, halo, tok, heads),
        grid_spec=pltpu.PrefetchScalarGridSpec(
            num_scalar_prefetch=1,
            grid=(seqs, groups),
            in_specs=[
                row,
                far(0),
                far(groups),
                row,
                table,
                table,
                pl.BlockSpec((1, 1, tok), lambda s, p, _: (s, 0, 0)),
            ]
            + [ANY] * len(deps),
            out_specs=[
                row,
                row,
                pl.BlockSpec((spans, 1, tok, width), lambda s, p, _: (0, s, 0, 0)),
            ],
            scratch_shapes=[
                pltpu.VMEM((heads, keys, CHUNK), F32),
                pltpu.VMEM((heads, keys, CHUNK), BF),
                pltpu.VMEM((keys, lanes), BF),
                pltpu.VMEM((keys, lanes), BF),
                pltpu.VMEM((lanes, keys), BF),
                pltpu.VMEM((lanes, keys), BF),
                pltpu.VMEM((keys, lanes), F32),
                pltpu.VMEM((keys, lanes), F32),
                pltpu.VMEM((lanes, CHUNK), F32),
                pltpu.VMEM((lanes, CHUNK), F32),
            ],
        ),
        out_shape=[
            jax.ShapeDtypeStruct((seqs, tok, width // 2), BF),
            jax.ShapeDtypeStruct((seqs, tok, width // 2), BF),
            jax.ShapeDtypeStruct((spans, seqs, tok, width), BF),
        ],
        compiler_params=pltpu.CompilerParams(vmem_limit_bytes=48 << 20),
        cost_estimate=SMALL,
        name="attention",
    )(scalars, queries, key_values, key_values, grad_att, keep, sine, starts, *deps)


def away_columns(whole, core, part):
    chips, rows, _ = whole.shape
    strip = part // 4

    def body(core_ref, w_ref, away_ref):
        for b in range(12):
            at = pl.multiple_of((2 * b + 1 - core_ref[0]) * strip, strip)
            away_ref[:, :, b * strip : (b + 1) * strip] = w_ref[:, :, pl.ds(at, strip)]

    return pl.pallas_call(
        body,
        grid=(4,),
        in_specs=[
            pl.BlockSpec(memory_space=pltpu.SMEM),
            pl.BlockSpec((chips // 4, rows, 6 * part), lambda i: (i, 0, 0)),
        ],
        out_specs=pl.BlockSpec((chips // 4, rows, 3 * part), lambda i: (i, 0, 0)),
        out_shape=jax.ShapeDtypeStruct((chips, rows, 3 * part), BF),
        compiler_params=pltpu.CompilerParams(vmem_limit_bytes=16 << 20),
        cost_estimate=SMALL,
        name="away_columns",
    )(core[None], whole)


def attention_weights(whole, come, core, nz, part):
    rows = whole.shape[1]
    depth = 8 * nz * rows
    strip = part // 4

    def body(core_ref, w_ref, c_ref, q_ref, kv_ref, dense_ref):
        mine = core_ref[0]
        for z in range(nz):
            own = pl.ds(pl.multiple_of((mine * nz + z) * rows, rows), rows)
            other = pl.ds(pl.multiple_of(((1 - mine) * nz + z) * rows, rows), rows)
            for b in range(12):
                value = w_ref[z, :, pl.ds(pl.multiple_of((2 * b + mine) * strip, strip), strip)]
                if b < 4:
                    q_ref[own, b * strip : (b + 1) * strip] = value
                else:
                    kv_ref[own, (b - 4) * strip : (b - 3) * strip] = value
            q_ref[other, :] = c_ref[z, :, :part]
            kv_ref[other, :] = c_ref[z, :, part:]
            dense_ref[z * rows : (z + 1) * rows, :] = w_ref[z, :, 6 * part :]

    block = lambda n: pl.BlockSpec((nz, rows, n), lambda i: (i, 0, 0))
    return pl.pallas_call(
        body,
        grid=(4,),
        in_specs=[pl.BlockSpec(memory_space=pltpu.SMEM), block(8 * part), block(3 * part)],
        out_specs=[
            pl.BlockSpec((depth // 4, part), lambda i: (i, 0)),
            pl.BlockSpec((depth // 4, 2 * part), lambda i: (i, 0)),
            pl.BlockSpec((depth // 8, 2 * part), lambda i: (i, 0)),
        ],
        out_shape=[
            jax.ShapeDtypeStruct((depth, part), BF),
            jax.ShapeDtypeStruct((depth, 2 * part), BF),
            jax.ShapeDtypeStruct((depth // 2, 2 * part), BF),
        ],
        compiler_params=pltpu.CompilerParams(vmem_limit_bytes=16 << 20),
        cost_estimate=SMALL,
        name="attention_weights",
    )(core[None], whole, come)


def unit_weights(whole, nz, rows, out_rows):
    columns = whole.shape[2]

    def body(w_ref, in_ref, out_ref):
        for z in range(nz):
            for j in range(4):
                at = (j * nz + z) * rows
                in_ref[at : at + rows, :] = w_ref[z, j * rows : (j + 1) * rows, :]
            out_ref[z * out_rows : (z + 1) * out_rows, :] = w_ref[z, 4 * rows :, :]

    return pl.pallas_call(
        body,
        grid=(2,),
        in_specs=[pl.BlockSpec((nz, 4 * rows + out_rows, columns), lambda i: (i, 0, 0))],
        out_specs=[
            pl.BlockSpec((4 * nz * rows, columns), lambda i: (i, 0)),
            pl.BlockSpec((nz * out_rows, columns), lambda i: (i, 0)),
        ],
        out_shape=[
            jax.ShapeDtypeStruct((8 * nz * rows, columns), BF),
            jax.ShapeDtypeStruct((2 * nz * out_rows, columns), BF),
        ],
        compiler_params=pltpu.CompilerParams(vmem_limit_bytes=16 << 20),
        cost_estimate=SMALL,
        name="unit_weights",
    )(whole)


def layer_norm(pieces, gain, bias, rows, first, extra, into=None, block=256):
    _, tok, width = pieces[0][0].shape
    steps = tok // block
    count = len(pieces)
    kept = 2 if extra else count

    def body(*refs):
        gain_ref, bias_ref = refs[count : count + 2]
        outs = refs[-2:] if extra else refs[-1:]
        i = pl.program_id(0)
        for p in range(count):

            @pl.when(i == p)
            def _():
                x = refs[p][0].astype(F32)
                centered = x - jnp.mean(x, axis=1, keepdims=True)
                variance = jnp.mean(centered * centered, axis=1, keepdims=True)
                value = centered * lax.rsqrt(variance + 1e-05)
                value = value * gain_ref[...] + bias_ref[...]
                if p < kept:
                    outs[0][...] = value.astype(BF)
                if extra:
                    outs[1][...] = value.astype(BF)

    def piece_spec(p):
        return pl.BlockSpec(
            (1, block, width),
            lambda i, b: (pieces[p][1], jnp.where(i == p, b, jnp.where(i < p, 0, steps - 1)), 0),
        )

    def kept_at(i, b):
        return first // block + jnp.where(i < kept, i * steps + b, kept * steps - 1)

    line = pl.BlockSpec((1, width), lambda i, b: (0, 0))
    out_specs = [pl.BlockSpec((block, width), lambda i, b: (kept_at(i, b), 0))]
    out_shape = [jax.ShapeDtypeStruct((rows, width), BF)]
    if extra:
        out_specs += [pl.BlockSpec((block, width), lambda i, b: (i * steps + b, 0))]
        out_shape += [jax.ShapeDtypeStruct((count * tok, width), BF)]
    given = [] if into is None else [into]
    return pl.pallas_call(
        body,
        grid=(count, steps),
        in_specs=[piece_spec(p) for p in range(count)] + [line, line] + [ANY] * len(given),
        out_specs=out_specs,
        out_shape=out_shape,
        input_output_aliases={} if into is None else {count + 2: 0},
        compiler_params=pltpu.CompilerParams(vmem_limit_bytes=32 << 20),
        cost_estimate=SMALL,
        name="layer_norm",
    )(*(p[0] for p in pieces), gain.reshape(1, width), bias.reshape(1, width), *given)


def attention_weight_grads(normed, attended, dq, dkv, grads, nz):
    tokens, part = dq.shape
    all_tokens, width = normed.shape
    near = all_tokens - tokens
    block, strip = width // 4, part // 4

    rows = strip // nz

    def body(n_ref, a_ref, d_ref, dkv_ref, g_ref, o_ref):
        def put(value, at):
            for h in range(2):
                for z in range(nz):
                    low = (h * nz + z) * rows
                    o_ref[0, z, h, :, at] = value[low : low + rows]

        put(tn(n_ref[near:, :], d_ref[...]).astype(BF), slice(0, part))
        put(tn(n_ref[...], dkv_ref[...]).astype(BF), slice(part, 3 * part))
        dense = tn(a_ref[...], g_ref[...]).astype(BF)
        put(jnp.concatenate([dense[:, :part], dense[:, part:]]), slice(3 * part, 4 * part))

    whole = lambda a: pl.BlockSpec(a.shape, lambda i: (0, 0))
    return pl.pallas_call(
        body,
        grid=(4,),
        in_specs=[
            pl.BlockSpec((all_tokens, block), lambda i: (0, i)),
            pl.BlockSpec((tokens, strip), lambda i: (0, i)),
            whole(dq),
            whole(dkv),
            pl.BlockSpec((tokens, width), lambda i: (0, 0)),
        ],
        out_specs=pl.BlockSpec((1, nz, 2, rows, 4 * part), lambda i: (i, 0, 0, 0, 0)),
        out_shape=jax.ShapeDtypeStruct((4, nz, 2, rows, 4 * part), BF),
        compiler_params=pltpu.CompilerParams(vmem_limit_bytes=48 << 20),
        cost_estimate=SMALL,
        name="attention_weight_grads",
    )(normed, attended, dq, dkv, grads)


def summed(*values):
    return sum(v.astype(F32) for v in values).astype(BF)


def z_scatter(parts, axis, zi, nz):
    for k, pairs in enumerate(z_pairs(nz)):
        shape = parts.shape
        blocks = parts.reshape(shape[:axis] + (shape[axis] // 2, 2) + shape[axis + 1 :])
        bit = (zi >> k) & 1
        come = lax.ppermute(pick(blocks, 1 - bit, axis + 1), "z", pairs)
        parts = summed(pick(blocks, bit, axis + 1), come)
    return lax.squeeze(parts, (axis,))


def normalise(tokens):
    row_mean = jnp.mean(tokens, axis=-1, keepdims=True)
    centered = tokens - row_mean
    variance = jnp.mean(centered * centered, axis=-1, keepdims=True)
    inv_std = lax.rsqrt(variance + 1e-05)
    return centered * inv_std, inv_std


def pick(blocks, index, axis):
    return lax.dynamic_index_in_dim(blocks, index, axis, keepdims=False)


def by_place(place, mine, theirs):
    low = jnp.where(place == 0, mine, theirs)
    high = jnp.where(place == 0, theirs, mine)
    return jnp.stack([low, high])


def z_pairs(nz):
    return [[(i, i ^ (1 << k)) for i in range(nz)] for k in range(nz.bit_length() - 1)]


def local_plane(
    nz,
    hidden_in,
    doc_lengths,
    ln_gain,
    ln_bias,
    w_qkv,
    b_qkv,
    w_dense,
    b_dense,
    w_in,
    b_in,
    w_out,
    b_out,
    out_grad,
):
    core, xi, yi, zi = (lax.axis_index(a) for a in "cxyz")
    chip = yi * 2 + xi
    halo = nz // 2
    _, tok, width = hidden_in.shape
    rows, ff = w_in.shape
    out_rows = w_out.shape[0]
    part = width // 2
    units = ff // 4
    up = [(i, i + 1) for i in range(nz - 1)]
    down = [(i + 1, i) for i in range(nz - 1)]
    hidden_own, grad_own = hidden_in[0], out_grad[0]

    small = jnp.concatenate([ln_gain, ln_bias, b_qkv, b_dense, b_in, b_out])[None]
    sizes = [v.shape[0] for v in (ln_gain, ln_bias, b_qkv, b_dense, b_in, b_out)]
    small_len = small.shape[1]
    first_whole = lax.all_gather(
        jnp.concatenate([w_qkv, w_dense], axis=1), ("y", "x", "z"), axis=0, tiled=False
    )
    come = other_core(away_columns(first_whole, core, part))

    def halves(weight, shape, axis, place):
        blocks = weight.reshape(shape)
        return pick(blocks, place, axis), pick(blocks, 1 - place, axis)

    in_mine, in_theirs = halves(w_in, (rows, 4, 2, -1), 2, core)
    in_got = other_core(in_theirs.reshape(rows, -1))
    in_core = by_place(core, in_mine.reshape(rows, -1), in_got)
    in_mine, in_theirs = halves(in_core, (2 * rows, 2, 2, -1), 2, xi)
    in_got = over_x(in_theirs.reshape(2 * rows, units))
    in_piece = by_place(xi, in_mine.reshape(2 * rows, units), in_got).reshape(4 * rows, units)

    before = [hidden_own]
    for _ in range(halo):
        before.append(lax.ppermute(before[-1], "z", up))
    pair_own = jnp.stack([hidden_own, grad_own])
    pair_x = over_x(pair_own)
    pair_other, pair_x_other = other_core(pair_own), other_core(pair_x)
    lens_other = other_core(doc_lengths)
    near = [pair_own, pair_other, pair_x, pair_x_other]

    for place, move in ((core, other_core), (xi, over_x), (yi, over_y)):
        small = by_place(place, small, move(small)).reshape(-1, small_len)
    for k, pairs in enumerate(z_pairs(nz)):
        small = by_place((zi >> k) & 1, small, lax.ppermute(small, "z", pairs))
        small = small.reshape(-1, small_len)
    small = small.reshape(nz, 8, small_len).transpose(1, 0, 2).reshape(8 * nz, small_len).astype(F32)
    cuts = [sum(sizes[:i]) for i in range(7)]
    gain, bias, qkv_bias, dense_bias, in_bias, out_bias = (
        small[:, cuts[i] : cuts[i + 1]].reshape(-1) for i in range(6)
    )
    qkv_bias = pick(qkv_bias.reshape(3, 4, 2, -1), core, 2).reshape(-1)
    in_bias = pick(pick(in_bias.reshape(2, 2, 2, -1), core, 2), xi, 1).reshape(-1)

    both = 2 * tok
    kv_rows = (halo + 1) * both
    normed_kv, normed_all = layer_norm(
        [(v, 0) for v in near], gain, bias, kv_rows, halo * both, True
    )
    grads_all = jnp.concatenate([v[1] for v in near])

    w_q_f, w_kv_f, w_dense_f = attention_weights(first_whole, come, core, nz, part)
    queries = matmul(normed_all, w_q_f, "nn", bias=qkv_bias[:part], rows=both)
    grad_att = matmul(grads_all, w_dense_f, "nt", rows=both)
    far = []
    for value in before[:0:-1]:
        far += [(value[None], 0), (other_core(value)[None], 0)]
    (normed_kv,) = layer_norm(far, gain, bias, kv_rows, 0, False, into=normed_kv)
    key_values = (mm(normed_kv, w_kv_f) + qkv_bias[part:]).astype(BF)
    second_whole = lax.all_gather(
        held(jnp.concatenate([in_piece, w_out]), first_whole), ("y", "z"), axis=0, tiled=False
    )

    base = (zi - halo) * tok
    positions = (base + jnp.arange((halo + 1) * tok, dtype=jnp.int32)).astype(F32)
    lane = jnp.arange(LANES, dtype=jnp.int32) % HEAD_DIM
    half_rot = ROT_DIM // 2
    frequency = jnp.exp(-math.log(10000.0) * 2.0 * (lane % half_rot).astype(F32) / ROT_DIM)
    angles = positions[:, None] * frequency[None, :]
    cosine, sine = jnp.cos(angles), jnp.sin(angles)
    keep = jnp.where(lane < ROT_DIM, cosine, 1.0)
    sine = jnp.where(lane < ROT_DIM, sine, 0.0)

    def doc_starts(lens):
        ends = prefix_ends(lens)
        own = zi * tok + jnp.arange(tok, dtype=jnp.int32)
        return jnp.max(jnp.where(own[:, None] >= ends[None, :], ends[None, :], 0), axis=1)

    starts = jnp.stack([doc_starts(doc_lengths[0]), doc_starts(lens_other[0])])
    lower = jnp.maximum((starts[:, ::CHUNK] - base) // CHUNK, 0)
    scalars = jnp.concatenate([lower.reshape(-1), base[None]]).astype(jnp.int32)
    attended, dq, dkv = attention(
        queries.reshape(2, tok, part),
        key_values.reshape(halo + 1, 2, tok, 2 * part),
        grad_att.reshape(2, tok, part),
        keep,
        sine,
        starts[:, None, :],
        scalars,
    )
    attended = attended.reshape(both, part)
    dq = dq.reshape(both, part)
    dkv = dkv.reshape(kv_rows, 2 * part)

    def after(*deps):
        return held(jnp.zeros((1, width), F32), *deps)

    dn_kv = nt(dkv, w_kv_f).astype(BF).reshape(halo + 1, 2, tok, width)
    dn_come = other_core(dn_kv[:halo, 1])
    g_att = attention_weight_grads(normed_kv, attended, dq, dkv, grads_all, nz)
    dn_far = summed(dn_kv[:halo, 0], held(dn_come, g_att))
    dn_q = matmul(dq, w_q_f, "nt").reshape(2, tok, width)
    dn_att = summed(dn_q, dn_kv[halo])

    s_att = lax.psum_scatter(
        g_att.reshape(4, nz, 2, rows, 4 * part), ("y", "x"), scatter_dimension=0, tiled=False
    )
    s_att = lax.psum_scatter(s_att, "z", scatter_dimension=0, tiled=False)

    w_in_f, w_out_f = unit_weights(second_whole, nz, rows, out_rows)
    activated, grad_pre, pre_sum = feed_forward(
        normed_all, grads_all, w_in_f, in_bias, w_out_f, deps=(dn_far, dn_att)
    )
    passed = dn_far[0]
    for step in range(1, halo):
        come = held(lax.ppermute(passed, "z", down), pre_sum)
        passed = summed(dn_far[step], come)
    dn_back = lax.ppermute(passed, "z", down)

    def away_tokens(shared, attn):
        return jnp.stack([summed(shared[0, 1], attn[1]), shared[1, 1]])

    g_in = matmul(normed_all, grad_pre, "tn", deps=(passed,)).reshape(2, -1, units)
    in_away = pick(g_in, 1 - yi, 0)
    in_y = over_y(in_away)
    dn_ff = (nt(grad_pre, w_in_f) + after(in_away)).astype(BF).reshape(2, 2, tok, width)
    dn_away = away_tokens(dn_ff, dn_att)
    g_out = matmul(activated, grads_all, "tn", deps=(dn_away,)).reshape(2, -1, width)
    out_away = pick(g_out, 1 - yi, 0)
    out_y = over_y(out_away)
    dn_come = held(other_core(dn_away), g_out)
    dn_send = summed(dn_ff[1, 0], dn_come[1])
    dn_x = over_x(dn_send)
    branch = (mm(activated, w_out_f) + after(out_away, dn_send)).astype(BF)
    branch = branch.reshape(2, 2, tok, width)
    branch_att = matmul(attended, w_dense_f, "nn", deps=(dn_send,)).reshape(2, tok, width)
    br_come = other_core(away_tokens(branch, branch_att))
    br_send = summed(branch[1, 0], br_come[1])
    br_x = over_x(br_send)

    s_in = summed(pick(g_in, yi, 0), held(in_y, br_send)).reshape(4, nz, rows, units)
    dn_x = held(dn_x, s_in)
    dn_parts = [dn_ff[0, 0], dn_att[0], dn_come[0]]
    br_parts = [branch[0, 0], branch_att[0], br_come[0]]

    x = hidden_own.astype(F32)
    gy = grad_own.astype(F32)
    dn = sum(v.astype(F32) for v in (*dn_parts, dn_x, dn_back))
    xhat, inv_std = normalise(x)
    scaled = dn * gain
    grad_input = gy + inv_std * (
        scaled
        - jnp.mean(scaled, axis=1, keepdims=True)
        - xhat * jnp.mean(scaled * xhat, axis=1, keepdims=True)
    )
    out_y, br_x = held(out_y, grad_input), held(br_x, grad_input)
    s_in = z_scatter(s_in, 1, zi, nz)
    s_out = summed(pick(g_out, yi, 0), out_y).reshape(nz, out_rows, width)
    grad_w_out = z_scatter(s_out, 0, zi, nz).astype(F32)
    hidden_out = (
        x + sum(v.astype(F32) for v in (*br_parts, br_x)) + dense_bias + out_bias
    ).astype(BF)

    def spread(vector, shape, mine):
        return jnp.where(mine, vector.reshape(shape), 0.0).reshape(-1)

    two = jnp.arange(2)
    g_qkv_bias = jnp.concatenate([jnp.sum(v.astype(F32), axis=0) for v in (dq, dkv)])
    small_grads = [
        jnp.sum(dn * xhat, axis=0),
        jnp.sum(dn, axis=0),
        spread(g_qkv_bias, (3, 4, 1, -1), (two == core)[None, None, :, None]),
        jnp.sum(gy, axis=0),
        spread(
            jnp.sum(pre_sum, axis=0),
            (2, 1, 1, -1),
            ((two == xi)[:, None] & (two == core)[None, :])[None, :, :, None],
        ),
    ]
    small_sizes = [g.shape[0] for g in small_grads]
    total = jnp.concatenate(small_grads)
    for move in (other_core, over_x, over_y):
        total = total + move(total)
    for pairs in z_pairs(nz):
        total = total + lax.ppermute(total, "z", pairs)
    device = (chip * 2 + core) * nz + zi
    small_out, at = [], 0
    for size in small_sizes:
        share = size // (8 * nz)
        small_out.append(lax.dynamic_slice_in_dim(total, at + device * share, share, 0))
        at += size
    g_gain, g_bias, g_bqkv, g_bdense, g_bin = small_out

    def home_core(columns):
        axis = columns.ndim - 3
        return by_place(core, pick(columns, core, axis), other_core(pick(columns, 1 - core, axis)))

    grad_w_dense = s_att[:, :, 3 * part :].transpose(1, 0, 2).reshape(rows, width).astype(F32)
    s_qkv = home_core(s_att[:, :, : 3 * part])
    grad_w_qkv = s_qkv.reshape(2, rows, 3, 4, -1).transpose(1, 2, 3, 0, 4).reshape(rows, -1)
    s_in = s_in.reshape(2, 2, rows, units)
    s_in = home_core(by_place(xi, pick(s_in, xi, 0), over_x(pick(s_in, 1 - xi, 0))))
    grad_w_in = s_in.reshape(2, 2, rows, 2, -1).transpose(2, 3, 1, 0, 4).reshape(rows, -1)
    return (
        hidden_out[None],
        grad_input[None],
        g_gain,
        g_bias,
        grad_w_qkv.astype(F32),
        g_bqkv,
        grad_w_dense,
        g_bdense,
        grad_w_in.astype(F32),
        g_bin,
        grad_w_out,
        g_bdense,
    )


def solution(mesh):
    n_seq, n_group = mesh.devices.shape
    if n_seq == 8 and n_group == 4:
        mesh = Mesh(mesh.devices.reshape(2, 2, 2, n_group), ("y", "x", "c", "z"))
        seq, group = ("y", "x", "c"), "z"
        both = ("y", "x", "c", "z")
        step = functools.partial(local_plane, n_group)
    else:
        seq, group, both = "seq", "group", ("seq", "group")
        step = local_generic
    matrix, vector = P(both, None), P(both)
    tokens = P(seq, group, None)
    weights = (vector, vector) + (matrix, vector) * 4
    return jax.shard_map(
        step,
        mesh=mesh,
        in_specs=(tokens, P(seq, None)) + weights + (tokens,),
        out_specs=(tokens, tokens) + weights,
        check_vma=False,
    )
```

```python
import functools
import math

import jax
import jax.numpy as jnp
from jax import lax
from jax.experimental import pallas as pl
from jax.experimental.pallas import tpu as pltpu
from jax.sharding import Mesh
from jax.sharding import PartitionSpec as P

HEADS = 16
HEAD_DIM = 64
ROT_DIM = 16


def prefix_ends(doc_lens):
    order = jnp.arange(doc_lens.shape[0], dtype=jnp.int32)
    return jnp.sum(jnp.where(order[None, :] <= order[:, None], doc_lens[None, :], 0), axis=1)


def dot_rows(left, right):
    return lax.dot_general(
        left, right, (((0,), (0,)), ((), ())), preferred_element_type=jnp.float32
    )


def dot_last(left, right):
    return lax.dot_general(
        left, right, (((1,), (1,)), ((), ())), preferred_element_type=jnp.float32
    )


def rope_tables(token_positions, rot_dim):
    half_rot = rot_dim // 2
    frequency = jnp.exp(
        -math.log(10000.0) * 2.0 * jnp.arange(half_rot, dtype=jnp.float32) / rot_dim
    )
    angles = token_positions.astype(jnp.float32)[:, None] * frequency[None, :]
    return (jnp.cos(angles)[:, None, :], jnp.sin(angles)[:, None, :])


def rotate(heads, cosine, sine, rot_dim):
    half_rot = rot_dim // 2
    first_half = heads[:, :, :half_rot]
    second_half = heads[:, :, half_rot:rot_dim]
    remainder = heads[:, :, rot_dim:]
    return jnp.concatenate(
        [
            first_half * cosine - second_half * sine,
            second_half * cosine + first_half * sine,
            remainder,
        ],
        axis=2,
    )


def gelu_exact(preact):
    return jax.nn.gelu(preact, approximate=False)


def block_scores(query_block, key_tile_block, seg_query, seg_key, pos_query, pos_key, score_scale):
    scaled = (
        jnp.einsum("qhd,khd->hqk", query_block, key_tile_block, preferred_element_type=jnp.float32)
        * score_scale
    )
    allowed = (seg_query[:, None] == seg_key[None, :]) & (pos_key[None, :] <= pos_query[:, None])
    return jnp.where(allowed[None], scaled, -1e30)


def owning_block(source, block_index, block_of_rows):
    return lax.dynamic_slice_in_dim(source, block_index * block_of_rows, block_of_rows, 0)


def add_block(source, block_index, block_of_rows, addend):
    current = owning_block(source, block_index, block_of_rows)
    return lax.dynamic_update_slice_in_dim(source, current + addend, block_index * block_of_rows, 0)


def attention_forward(
    query_heads,
    key_head_rows,
    value_head_rows,
    document_segment,
    token_positions,
    seg_start,
    block_of_rows,
):
    seq_len, head_count, head_dim = query_heads.shape
    score_scale = 1.0 / math.sqrt(head_dim)

    def query_step(qindex, state_now):
        outputs, log_sums = state_now
        query_block = owning_block(query_heads, qindex, block_of_rows)
        seg_query = owning_block(document_segment, qindex, block_of_rows)
        pos_query = owning_block(token_positions, qindex, block_of_rows)
        key_lower = seg_start[qindex * block_of_rows] // block_of_rows

        def scores_for_block(key_position_index):
            return block_scores(
                query_block,
                owning_block(key_head_rows, key_position_index, block_of_rows),
                seg_query,
                owning_block(document_segment, key_position_index, block_of_rows),
                pos_query,
                owning_block(token_positions, key_position_index, block_of_rows),
                score_scale,
            )

        def statistics_step(key_position_index, row_statistics):
            run_max, run_sum = row_statistics
            logit_scores = scores_for_block(key_position_index)
            new_max = jnp.maximum(run_max, jnp.max(logit_scores, axis=2))
            run_sum = run_sum * jnp.exp(run_max - new_max) + jnp.sum(
                jnp.exp(logit_scores - new_max[:, :, None]), axis=2
            )
            return (new_max, run_sum)

        start_stats = (
            jnp.full((head_count, block_of_rows), -1e30, jnp.float32),
            jnp.zeros((head_count, block_of_rows), jnp.float32),
        )
        run_max, run_sum = lax.fori_loop(key_lower, qindex + 1, statistics_step, start_stats)
        log_exp_total = run_max + jnp.log(run_sum)

        def value_loop_step(key_position_index, partial_output):
            attention_weights = jnp.exp(
                scores_for_block(key_position_index) - log_exp_total[:, :, None]
            ).astype(jnp.bfloat16)
            return partial_output + jnp.einsum(
                "hqk,khd->qhd",
                attention_weights,
                owning_block(value_head_rows, key_position_index, block_of_rows),
                preferred_element_type=jnp.float32,
            )

        block_out = lax.fori_loop(
            key_lower,
            qindex + 1,
            value_loop_step,
            jnp.zeros((block_of_rows, head_count, head_dim), jnp.float32),
        )
        outputs = lax.dynamic_update_slice_in_dim(outputs, block_out, qindex * block_of_rows, 0)
        log_sums = lax.dynamic_update_slice_in_dim(
            log_sums, log_exp_total, qindex * block_of_rows, 1
        )
        return (outputs, log_sums)

    start_state = (
        jnp.zeros((seq_len, head_count, head_dim), jnp.float32),
        jnp.zeros((head_count, seq_len), jnp.float32),
    )
    return lax.fori_loop(0, seq_len // block_of_rows, query_step, start_state)


def attention_backward(
    query_heads,
    key_head_rows,
    value_head_rows,
    grad_heads,
    outputs,
    log_sums,
    document_segment,
    token_positions,
    seg_start,
    block_of_rows,
):
    seq_len, head_count, head_dim = query_heads.shape
    score_scale = 1.0 / math.sqrt(head_dim)
    delta_all = jnp.sum(grad_heads.astype(jnp.float32) * outputs, axis=2).T

    def query_step(qindex, state_now):
        grad_query_all, grad_key_all, grad_value_all = state_now
        query_block = owning_block(query_heads, qindex, block_of_rows)
        grad_block = owning_block(grad_heads, qindex, block_of_rows)
        seg_query = owning_block(document_segment, qindex, block_of_rows)
        pos_query = owning_block(token_positions, qindex, block_of_rows)
        log_exp_total = lax.dynamic_slice_in_dim(log_sums, qindex * block_of_rows, block_of_rows, 1)
        delta_block = lax.dynamic_slice_in_dim(delta_all, qindex * block_of_rows, block_of_rows, 1)
        key_lower = seg_start[qindex * block_of_rows] // block_of_rows

        def key_loop_step(key_position_index, loop_state_inner):
            grad_query, grad_keys, grad_values = loop_state_inner
            key_tile_block = owning_block(key_head_rows, key_position_index, block_of_rows)
            value_tile_block = owning_block(value_head_rows, key_position_index, block_of_rows)
            logit_scores = block_scores(
                query_block,
                key_tile_block,
                seg_query,
                owning_block(document_segment, key_position_index, block_of_rows),
                pos_query,
                owning_block(token_positions, key_position_index, block_of_rows),
                score_scale,
            )
            probability = jnp.exp(logit_scores - log_exp_total[:, :, None])
            grad_values = add_block(
                grad_values,
                key_position_index,
                block_of_rows,
                jnp.einsum(
                    "hqk,qhd->khd",
                    probability.astype(jnp.bfloat16),
                    grad_block,
                    preferred_element_type=jnp.float32,
                ),
            )
            grad_probs = jnp.einsum(
                "qhd,khd->hqk", grad_block, value_tile_block, preferred_element_type=jnp.float32
            )
            grad_scores = (probability * (grad_probs - delta_block[:, :, None])).astype(
                jnp.bfloat16
            )
            grad_query = (
                grad_query
                + jnp.einsum(
                    "hqk,khd->qhd", grad_scores, key_tile_block, preferred_element_type=jnp.float32
                )
                * score_scale
            )
            grad_keys = add_block(
                grad_keys,
                key_position_index,
                block_of_rows,
                jnp.einsum(
                    "hqk,qhd->khd", grad_scores, query_block, preferred_element_type=jnp.float32
                )
                * score_scale,
            )
            return (grad_query, grad_keys, grad_values)

        start_inner = (
            jnp.zeros((block_of_rows, head_count, head_dim), jnp.float32),
            grad_key_all,
            grad_value_all,
        )
        grad_query, grad_key_all, grad_value_all = lax.fori_loop(
            key_lower, qindex + 1, key_loop_step, start_inner
        )
        grad_query_all = lax.dynamic_update_slice_in_dim(
            grad_query_all, grad_query, qindex * block_of_rows, 0
        )
        return (grad_query_all, grad_key_all, grad_value_all)

    zero_heads = jnp.zeros((seq_len, head_count, head_dim), jnp.float32)
    return lax.fori_loop(
        0, seq_len // block_of_rows, query_step, (zero_heads, zero_heads, zero_heads)
    )


def local_generic(
    hidden_in,
    doc_lengths,
    ln_gain,
    ln_bias,
    w_qkv,
    b_qkv,
    w_dense,
    b_dense,
    w_in,
    b_in,
    w_out,
    b_out,
    out_grad,
):
    (
        full_gain,
        full_bias,
        full_qkv,
        full_qkv_bias,
        full_dense,
        full_dense_bias,
        full_in,
        full_in_bias,
        full_out,
        full_out_bias,
    ) = (
        lax.all_gather(ln_gain, ("seq", "group"), axis=0, tiled=True),
        lax.all_gather(ln_bias, ("seq", "group"), axis=0, tiled=True),
        lax.all_gather(w_qkv, ("seq", "group"), axis=0, tiled=True),
        lax.all_gather(b_qkv, ("seq", "group"), axis=0, tiled=True),
        lax.all_gather(w_dense, ("seq", "group"), axis=0, tiled=True),
        lax.all_gather(b_dense, ("seq", "group"), axis=0, tiled=True),
        lax.all_gather(w_in, ("seq", "group"), axis=0, tiled=True),
        lax.all_gather(b_in, ("seq", "group"), axis=0, tiled=True),
        lax.all_gather(w_out, ("seq", "group"), axis=0, tiled=True),
        lax.all_gather(b_out, ("seq", "group"), axis=0, tiled=True),
    )
    tokens = hidden_in[0].astype(jnp.float32)
    tok_count = tokens.shape[0]
    width = tokens.shape[1]
    row_mean = jnp.mean(tokens, axis=1, keepdims=True)
    centered = tokens - row_mean
    variance = jnp.mean(centered * centered, axis=1, keepdims=True)
    inv_std = lax.rsqrt(variance + 1e-05)
    normal_rows = centered * inv_std
    normed = (normal_rows * full_gain.astype(jnp.float32) + full_bias.astype(jnp.float32)).astype(
        jnp.bfloat16
    )
    mixed = jnp.dot(normed, full_qkv, preferred_element_type=jnp.float32) + full_qkv_bias.astype(
        jnp.float32
    )
    token_positions = lax.axis_index("group") * tok_count + jnp.arange(tok_count, dtype=jnp.int32)
    cosine, sine = rope_tables(token_positions, ROT_DIM)
    head_shape = (tok_count, HEADS, HEAD_DIM)
    queries = (
        rotate(mixed[:, :width].reshape(head_shape), cosine, sine, ROT_DIM)
        .reshape(tok_count, width)
        .astype(jnp.bfloat16)
    )
    key_rows = (
        rotate(mixed[:, width : 2 * width].reshape(head_shape), cosine, sine, ROT_DIM)
        .reshape(tok_count, width)
        .astype(jnp.bfloat16)
    )
    value_rows = mixed[:, 2 * width :].astype(jnp.bfloat16)
    query_cols, key_cols, value_cols = (
        lax.all_to_all(queries, "group", split_axis=1, concat_axis=0, tiled=True),
        lax.all_to_all(key_rows, "group", split_axis=1, concat_axis=0, tiled=True),
        lax.all_to_all(value_rows, "group", split_axis=1, concat_axis=0, tiled=True),
    )
    seq_len = query_cols.shape[0]
    head_count = query_cols.shape[1] // HEAD_DIM
    heads_shape = (seq_len, head_count, HEAD_DIM)
    query_heads = query_cols.reshape(heads_shape)
    key_head_rows = key_cols.reshape(heads_shape)
    value_head_rows = value_cols.reshape(heads_shape)
    all_pos = jnp.arange(seq_len, dtype=jnp.int32)
    doc_lens = doc_lengths[0]
    doc_ends = prefix_ends(doc_lens)
    document_segment = jnp.sum((all_pos[:, None] >= doc_ends[None, :]).astype(jnp.int32), axis=1)
    doc_starts = doc_ends - doc_lens
    doc_index = jnp.arange(doc_ends.shape[0], dtype=jnp.int32)
    seg_start = jnp.sum(
        jnp.where(document_segment[:, None] == doc_index[None, :], doc_starts[None, :], 0), axis=1
    )
    block_of_rows = min(512, seq_len)
    outputs, log_sums = attention_forward(
        query_heads,
        key_head_rows,
        value_head_rows,
        document_segment,
        all_pos,
        seg_start,
        block_of_rows,
    )
    attended = lax.all_to_all(
        outputs.reshape(seq_len, head_count * HEAD_DIM).astype(jnp.bfloat16),
        "group",
        split_axis=0,
        concat_axis=1,
        tiled=True,
    )
    branch_attn = jnp.dot(
        attended, full_dense, preferred_element_type=jnp.float32
    ) + full_dense_bias.astype(jnp.float32)
    pre_act = jnp.dot(normed, full_in, preferred_element_type=jnp.float32) + full_in_bias.astype(
        jnp.float32
    )
    activated = gelu_exact(pre_act).astype(jnp.bfloat16)
    branch_mlp = jnp.dot(
        activated, full_out, preferred_element_type=jnp.float32
    ) + full_out_bias.astype(jnp.float32)
    hidden_out = (tokens + branch_attn + branch_mlp).astype(jnp.bfloat16)
    grad_rows = out_grad[0]
    grad_float = grad_rows.astype(jnp.float32)
    bias_grad = jnp.sum(grad_float, axis=0)
    grad_dense = dot_rows(attended, grad_rows)
    grad_out_w = dot_rows(activated, grad_rows)
    grad_act = dot_last(grad_rows, full_out)
    grad_pre = jax.vjp(gelu_exact, pre_act)[1](grad_act)[0].astype(jnp.bfloat16)
    grad_in_w = dot_rows(normed, grad_pre)
    grad_in_bias = jnp.sum(grad_pre.astype(jnp.float32), axis=0)
    grad_normed = dot_last(grad_pre, full_in)
    grad_attended = dot_last(grad_rows, full_dense).astype(jnp.bfloat16)
    grad_cols = lax.all_to_all(grad_attended, "group", split_axis=1, concat_axis=0, tiled=True)
    grad_query_all, grad_key_all, grad_value_all = attention_backward(
        query_heads,
        key_head_rows,
        value_head_rows,
        grad_cols.reshape(heads_shape),
        outputs,
        log_sums,
        document_segment,
        all_pos,
        seg_start,
        block_of_rows,
    )
    flat_shape = (seq_len, head_count * HEAD_DIM)
    grad_query_tok, grad_key_tok, grad_value_tok = (
        lax.all_to_all(
            grad_query_all.reshape(flat_shape).astype(jnp.bfloat16),
            "group",
            split_axis=0,
            concat_axis=1,
            tiled=True,
        ),
        lax.all_to_all(
            grad_key_all.reshape(flat_shape).astype(jnp.bfloat16),
            "group",
            split_axis=0,
            concat_axis=1,
            tiled=True,
        ),
        lax.all_to_all(
            grad_value_all.reshape(flat_shape).astype(jnp.bfloat16),
            "group",
            split_axis=0,
            concat_axis=1,
            tiled=True,
        ),
    )
    unrot_query = (
        rotate(grad_query_tok.astype(jnp.float32).reshape(head_shape), cosine, -sine, ROT_DIM)
        .reshape(tok_count, width)
        .astype(jnp.bfloat16)
    )
    unrot_key = (
        rotate(grad_key_tok.astype(jnp.float32).reshape(head_shape), cosine, -sine, ROT_DIM)
        .reshape(tok_count, width)
        .astype(jnp.bfloat16)
    )
    grad_mixed = jnp.concatenate([unrot_query, unrot_key, grad_value_tok], axis=1)
    grad_qkv_w = dot_rows(normed, grad_mixed)
    grad_qkv_bias = jnp.sum(grad_mixed.astype(jnp.float32), axis=0)
    grad_normed = grad_normed + dot_last(grad_mixed, full_qkv)
    scaled_grad = grad_normed * full_gain.astype(jnp.float32)
    grad_gain = jnp.sum(grad_normed * normal_rows, axis=0)
    grad_bias = jnp.sum(grad_normed, axis=0)
    grad_input = grad_float + inv_std * (
        scaled_grad
        - jnp.mean(scaled_grad, axis=1, keepdims=True)
        - normal_rows * jnp.mean(scaled_grad * normal_rows, axis=1, keepdims=True)
    )
    sharded = tuple(
        (
            lax.psum_scatter(grad_gain, ("seq", "group"), scatter_dimension=0, tiled=True),
            lax.psum_scatter(grad_bias, ("seq", "group"), scatter_dimension=0, tiled=True),
            lax.psum_scatter(grad_qkv_w, ("seq", "group"), scatter_dimension=0, tiled=True),
            lax.psum_scatter(grad_qkv_bias, ("seq", "group"), scatter_dimension=0, tiled=True),
            lax.psum_scatter(grad_dense, ("seq", "group"), scatter_dimension=0, tiled=True),
            lax.psum_scatter(bias_grad, ("seq", "group"), scatter_dimension=0, tiled=True),
            lax.psum_scatter(grad_in_w, ("seq", "group"), scatter_dimension=0, tiled=True),
            lax.psum_scatter(grad_in_bias, ("seq", "group"), scatter_dimension=0, tiled=True),
            lax.psum_scatter(grad_out_w, ("seq", "group"), scatter_dimension=0, tiled=True),
            lax.psum_scatter(bias_grad, ("seq", "group"), scatter_dimension=0, tiled=True),
        )
    )
    return (hidden_out[None], grad_input[None]) + sharded


SWAP = [(0, 1), (1, 0)]
CHUNK = 256
LANES = 128
BF = jnp.bfloat16
F32 = jnp.float32
ANY = pl.BlockSpec(memory_space=pl.ANY)
SMALL = pl.CostEstimate(flops=0, bytes_accessed=1 << 20, transcendentals=0)


def mm(left, right):
    return jnp.dot(left, right, preferred_element_type=F32)


def other_core(value):
    return lax.ppermute(value, "c", SWAP)


def over_x(value):
    return lax.ppermute(value, "x", SWAP)


def over_y(value):
    return lax.ppermute(value, "y", SWAP)


def nt(left, right):
    return lax.dot_general(left, right, (((1,), (1,)), ((), ())), preferred_element_type=F32)


def tn(left, right):
    return lax.dot_general(left, right, (((0,), (0,)), ((), ())), preferred_element_type=F32)


def matmul(left, right, form, deps=(), bias=None, block=512, dtype=BF, rows=None):
    rows = rows or (left.shape[1] if form == "tn" else left.shape[0])
    depth = left.shape[0] if form == "tn" else left.shape[1]
    columns = right.shape[0] if form == "nt" else right.shape[1]
    block = min(block, rows)
    dot = {"nn": mm, "nt": nt, "tn": tn}[form]

    def body(left_ref, right_ref, *rest):
        value = dot(left_ref[...], right_ref[...])
        if bias is not None:
            value = value + rest[0][...]
        rest[-1][...] = value.astype(dtype)

    if form == "tn":
        left_spec = pl.BlockSpec((depth, block), lambda i: (0, i))
    else:
        left_spec = pl.BlockSpec((block, depth), lambda i: (i, 0))
    whole = pl.BlockSpec(right.shape, lambda i: (0, 0))
    row = [] if bias is None else [pl.BlockSpec((1, columns), lambda i: (0, 0))]
    given = [] if bias is None else [bias.reshape(1, columns)]
    return pl.pallas_call(
        body,
        grid=(rows // block,),
        in_specs=[left_spec, whole] + row + [ANY] * len(deps),
        out_specs=pl.BlockSpec((block, columns), lambda i: (i, 0)),
        out_shape=jax.ShapeDtypeStruct((rows, columns), dtype),
        compiler_params=pltpu.CompilerParams(vmem_limit_bytes=48 << 20),
        cost_estimate=SMALL,
        name="matmul_" + form,
    )(left, right, *given, *deps)


def held(value, *deps):
    def body(*refs):
        pass

    return pl.pallas_call(
        body,
        in_specs=[ANY] * (1 + len(deps)),
        out_specs=ANY,
        out_shape=jax.ShapeDtypeStruct(value.shape, value.dtype),
        input_output_aliases={0: 0},
        compiler_params=pltpu.CompilerParams(vmem_limit_bytes=1 << 20),
        name="held",
    )(value, *deps)


def gelu_parts(value):
    size = jnp.abs(value)
    t = 1.0 / (1.0 + (0.3275911 / math.sqrt(2.0)) * size)
    poly = t * (
        0.254829592
        + t * (-0.284496736 + t * (1.421413741 + t * (-1.453152027 + t * 1.061405429)))
    )
    density = jnp.exp(-0.5 * value * value)
    tail = 0.5 * poly * density
    below = jnp.where(value < 0, tail, 1.0 - tail)
    return value * below, below + value * density * (1.0 / math.sqrt(2.0 * math.pi))


def feed_forward(normed, grads, w_in, bias, w_out, deps=(), block=256):
    tokens, width = normed.shape
    units = w_in.shape[1]

    def body(n_ref, g_ref, wi_ref, b_ref, wo_ref, *rest):
        act_ref, pre_ref, sum_ref = rest[-3:]
        value, slope = gelu_parts(mm(n_ref[...], wi_ref[...]) + b_ref[...])
        act_ref[...] = value.astype(BF)
        grad_pre = (slope * nt(g_ref[...], wo_ref[...])).astype(BF)
        pre_ref[...] = grad_pre
        total = jnp.sum(grad_pre.astype(F32).reshape(block // 8, 8, units), axis=0)

        @pl.when(pl.program_id(0) == 0)
        def _():
            sum_ref[...] = total

        @pl.when(pl.program_id(0) != 0)
        def _():
            sum_ref[...] += total

    rows = lambda n: pl.BlockSpec((block, n), lambda i: (i, 0))
    whole = lambda a: pl.BlockSpec(a.shape, lambda i: (0, 0))
    bias = bias.reshape(1, units)
    return pl.pallas_call(
        body,
        grid=(tokens // block,),
        in_specs=[rows(width), rows(width), whole(w_in), whole(bias), whole(w_out)]
        + [ANY] * len(deps),
        out_specs=[rows(units), rows(units), pl.BlockSpec((8, units), lambda i: (0, 0))],
        out_shape=[
            jax.ShapeDtypeStruct((tokens, units), BF),
            jax.ShapeDtypeStruct((tokens, units), BF),
            jax.ShapeDtypeStruct((8, units), F32),
        ],
        compiler_params=pltpu.CompilerParams(vmem_limit_bytes=48 << 20),
        cost_estimate=SMALL,
        name="feed_forward",
    )(normed, grads, w_in, bias, w_out, *deps)


def attention_kernel(halo, tok, heads, scalar_ref, q_ref, k_ref, v_ref, do_ref, keep_ref, sine_ref, start_ref, *rest):
    att_ref, dq_ref, dkv_ref = rest[-13:-10]
    s_scr, p_scr, k_scr, v_scr, kt_scr, vt_scr, dk_scr, dv_scr, ot_scr, dqt_scr = rest[-10:]
    s, p = pl.program_id(0), pl.program_id(1)
    groups = pl.num_programs(1)
    lanes = heads * HEAD_DIM
    blocks = tok // CHUNK
    chunks = (halo + 1) * blocks
    base = scalar_ref[2 * blocks]
    scale = 1.0 / math.sqrt(HEAD_DIM)
    row = lax.broadcasted_iota(jnp.int32, (CHUNK, CHUNK), 0)
    column = lax.broadcasted_iota(jnp.int32, (CHUNK, CHUNK), 1)
    unit = (row == column).astype(F32).astype(BF)
    from_lane = lax.broadcasted_iota(jnp.int32, (lanes, lanes), 0)
    to_lane = lax.broadcasted_iota(jnp.int32, (lanes, lanes), 1)
    half_rot = ROT_DIM // 2
    place = to_lane % HEAD_DIM
    turn = jnp.where((place < half_rot) & (from_lane == to_lane + half_rot), -1.0, 0.0)
    turn = jnp.where(
        (place >= half_rot) & (place < ROT_DIM) & (from_lane == to_lane - half_rot), 1.0, turn
    ).astype(BF)
    head_of = lax.broadcasted_iota(jnp.int32, (CHUNK, lanes), 1) // HEAD_DIM
    zero = jnp.zeros((CHUNK, lanes), BF)
    head_down = lax.broadcasted_iota(jnp.int32, (lanes, CHUNK), 0) // HEAD_DIM
    zero_down = jnp.zeros((lanes, CHUNK), BF)

    def flip(value):
        return nt(unit, value)

    def wide(table_ref, at):
        value = table_ref[at, :]
        return jnp.concatenate([value] * (lanes // LANES), axis=1)

    def chunk_at(j):
        return pl.ds(pl.multiple_of(j * CHUNK, CHUNK), CHUNK)

    def turned(value, at, sign):
        return value.astype(F32) * wide(keep_ref, at) + mm(value, turn) * (sign * wide(sine_ref, at))

    def by_head(value):
        return jnp.concatenate([jnp.where(head_of == h, value, zero) for h in range(heads)])

    def beside(value):
        return jnp.concatenate([jnp.where(head_down == h, value, zero_down) for h in range(heads)], axis=1)

    def part_of(h):
        return pl.ds(h * CHUNK, CHUNK)

    def prepare(b, carry):
        at = pl.ds(pl.multiple_of(b * tok, tok), tok)
        k_rot = turned(k_ref[b, 0], at, 1.0).astype(BF)
        k_scr[at, :] = k_rot
        kt_scr[:, at] = nt_t(k_rot)
        v_scr[at, :] = v_ref[b, 0]
        vt_scr[:, at] = nt_t(v_ref[b, 0])
        return carry

    unit_lanes = (from_lane == to_lane).astype(F32).astype(BF)

    def nt_t(value):
        return nt(unit_lanes, value).astype(BF)

    lowest = scalar_ref[s * blocks]

    lax.fori_loop(lowest // blocks, halo + 1, prepare, 0)

    def clear(j, carry):
        at = chunk_at(j)
        dk_scr[at, :] = jnp.zeros((CHUNK, lanes), F32)
        dv_scr[at, :] = jnp.zeros((CHUNK, lanes), F32)
        return carry

    lax.fori_loop(0, chunks, clear, 0)

    def both(body, start):
        low = [scalar_ref[s * blocks + b] for b in range(blocks)]
        high = [halo * blocks + b + 1 for b in range(blocks)]
        carry = list(start)
        edges = [(low[b], low[b + 1], b + 1) for b in range(blocks - 1)]
        for lower, upper, n in edges + [(low[-1], high[0], blocks)]:

            def step(j, now, n=n):
                return tuple(body(b, j, c) for b, c in enumerate(now[:n])) + now[n:]

            carry = list(lax.fori_loop(lower, upper, step, tuple(carry)))
        for b in range(1, blocks):

            def tail(j, now, b=b):
                return now[:b] + tuple(body(k, j, now[k]) for k in range(b, blocks))

            carry = list(lax.fori_loop(high[b - 1], high[b], tail, tuple(carry)))
        return carry

    q_down, q_beside, starts, inners, owns = [], [], [], [], []
    for b in range(blocks):
        inner = pl.ds(b * CHUNK, CHUNK)
        own = pl.ds((halo * blocks + b) * CHUNK, CHUNK)
        q_rot = turned(q_ref[0, inner, :], own, 1.0).astype(BF)
        q_scaled = (q_rot.astype(F32) * scale).astype(BF)
        q_down.append(by_head(q_scaled))
        q_beside.append(beside(nt_t(q_scaled)))
        starts.append(start_ref[0, :, inner] - base)
        inners.append(inner)
        owns.append(own)

    def scores(b, j, top):
        at = chunk_at(j)
        k_pos = j * CHUNK + row
        q_pos = (halo * blocks + b) * CHUNK + column
        allowed = (k_pos >= starts[b]) & (k_pos <= q_pos)
        value = mm(k_scr[at, :], q_beside[b])
        out = []
        for h in range(heads):
            masked = jnp.where(allowed, value[:, h * CHUNK : (h + 1) * CHUNK], -1e30)
            s_scr[b, at, part_of(h)] = masked
            out.append(jnp.max(masked.reshape(CHUNK // 8, 8, CHUNK), axis=0))
        return jnp.maximum(top, jnp.concatenate(out, axis=1))

    tops = both(scores, [jnp.full((8, heads * CHUNK), -1e30, F32)] * blocks)
    tops = [jnp.max(top, axis=0, keepdims=True) for top in tops]
    ot_scr[...] = jnp.zeros_like(ot_scr)
    dqt_scr[...] = jnp.zeros_like(dqt_scr)

    def weigh(b, j, total):
        at = chunk_at(j)
        value = jnp.exp(s_scr[b, at, :] - tops[b])
        total = total + jnp.sum(value.reshape(CHUNK // 8, 8, heads * CHUNK), axis=0)
        value = value.astype(BF)
        p_scr[b, at, :] = value
        for h in range(heads):
            rows = pl.ds(h * HEAD_DIM, HEAD_DIM)
            ot_scr[b, rows, :] += mm(vt_scr[rows, at], value[:, h * CHUNK : (h + 1) * CHUNK])
        return total

    totals = both(weigh, [jnp.zeros((8, heads * CHUNK), F32)] * blocks)
    do_down, do_beside, deltas = [], [], []
    for b in range(blocks):
        total = 1.0 / jnp.sum(totals[b], axis=0, keepdims=True)
        inverse = [total[:, h * CHUNK : (h + 1) * CHUNK] for h in range(heads)]
        out_t = jnp.concatenate(
            [ot_scr[b, h * HEAD_DIM : (h + 1) * HEAD_DIM, :] * inverse[h] for h in range(heads)]
        )
        att_ref[0, inners[b], :] = flip(out_t.astype(BF)).astype(BF)
        scaled = do_ref[0, inners[b], :].astype(F32)
        spread = jnp.zeros((CHUNK, lanes), F32)
        for h in range(heads):
            down = jnp.transpose(jnp.broadcast_to(inverse[h], (LANES, CHUNK)))
            down = jnp.concatenate([down] * (lanes // LANES), axis=1)
            spread = jnp.where(head_of == h, down, spread)
        scaled = (scaled * spread).astype(BF)
        scaled_t = nt(unit_lanes, scaled)
        prod = out_t * scaled_t
        do_down.append(by_head(scaled))
        do_beside.append(beside(scaled_t.astype(BF)))
        deltas.append(
            jnp.concatenate(
                [
                    jnp.sum(prod[h * HEAD_DIM : (h + 1) * HEAD_DIM], axis=0, keepdims=True)
                    for h in range(heads)
                ],
                axis=1,
            )
        )

    def backward(b, j, carry):
        at = chunk_at(j)
        prob = p_scr[b, at, :]
        ds = (prob.astype(F32) * (mm(v_scr[at, :], do_beside[b]) - deltas[b])).astype(BF)
        dv_scr[at, :] += mm(prob, do_down[b])
        dk_scr[at, :] += mm(ds, q_down[b])
        for h in range(heads):
            rows = pl.ds(h * HEAD_DIM, HEAD_DIM)
            dqt_scr[b, rows, :] += mm(kt_scr[rows, at], ds[:, h * CHUNK : (h + 1) * CHUNK])
        return carry

    both(backward, [0] * blocks)
    for b in range(blocks):
        dq = flip((dqt_scr[b] * scale).astype(BF)).astype(BF)
        dq_ref[0, inners[b], :] = turned(dq, owns[b], -1.0).astype(BF)

    for j in range(chunks):
        at = pl.ds(j * CHUNK, CHUNK)
        inner = pl.ds((j % blocks) * CHUNK, CHUNK)
        dk = turned(dk_scr[at, :].astype(BF), at, -1.0).astype(BF)
        for k, value in enumerate((dk, dv_scr[at, :].astype(BF))):
            columns = pl.ds(pl.multiple_of((k * groups + p) * lanes, LANES), lanes)
            dkv_ref[j // blocks, 0, inner, columns] = value


def attention(queries, key_values, grad_att, keep, sine, starts, scalars, deps=(), heads=4):
    spans, seqs, tok, width = key_values.shape
    halo = spans - 1
    lanes = heads * HEAD_DIM
    groups = width // 2 // lanes
    keys = spans * tok
    row = pl.BlockSpec((1, tok, lanes), lambda s, p, _: (s, 0, p))
    far = lambda off: pl.BlockSpec((spans, 1, tok, lanes), lambda s, p, _: (0, s, 0, off + p))
    table = pl.BlockSpec((keys, LANES), lambda s, p, _: (0, 0))
    flops = seqs * groups * heads * keys * tok * HEAD_DIM * 12 * 3
    return pl.pallas_call(
        functools.partial(attention_kernel, halo, tok, heads),
        grid_spec=pltpu.PrefetchScalarGridSpec(
            num_scalar_prefetch=1,
            grid=(seqs, groups),
            in_specs=[
                row,
                far(0),
                far(groups),
                row,
                table,
                table,
                pl.BlockSpec((1, 1, tok), lambda s, p, _: (s, 0, 0)),
            ]
            + [ANY] * len(deps),
            out_specs=[
                row,
                row,
                pl.BlockSpec((spans, 1, tok, width), lambda s, p, _: (0, s, 0, 0)),
            ],
            scratch_shapes=[
                pltpu.VMEM((tok // CHUNK, keys, heads * CHUNK), F32),
                pltpu.VMEM((tok // CHUNK, keys, heads * CHUNK), BF),
                pltpu.VMEM((keys, lanes), BF),
                pltpu.VMEM((keys, lanes), BF),
                pltpu.VMEM((lanes, keys), BF),
                pltpu.VMEM((lanes, keys), BF),
                pltpu.VMEM((keys, lanes), F32),
                pltpu.VMEM((keys, lanes), F32),
                pltpu.VMEM((tok // CHUNK, lanes, CHUNK), F32),
                pltpu.VMEM((tok // CHUNK, lanes, CHUNK), F32),
            ],
        ),
        out_shape=[
            jax.ShapeDtypeStruct((seqs, tok, width // 2), BF),
            jax.ShapeDtypeStruct((seqs, tok, width // 2), BF),
            jax.ShapeDtypeStruct((spans, seqs, tok, width), BF),
        ],
        compiler_params=pltpu.CompilerParams(vmem_limit_bytes=48 << 20),
        cost_estimate=SMALL,
        name="attention",
    )(scalars, queries, key_values, key_values, grad_att, keep, sine, starts, *deps)


def away_columns(whole, core, part):
    chips, rows, _ = whole.shape
    strip = part // 4

    def body(core_ref, w_ref, away_ref):
        for b in range(12):
            at = pl.multiple_of((2 * b + 1 - core_ref[0]) * strip, strip)
            away_ref[:, :, b * strip : (b + 1) * strip] = w_ref[:, :, pl.ds(at, strip)]

    return pl.pallas_call(
        body,
        grid=(4,),
        in_specs=[
            pl.BlockSpec(memory_space=pltpu.SMEM),
            pl.BlockSpec((chips // 4, rows, 6 * part), lambda i: (i, 0, 0)),
        ],
        out_specs=pl.BlockSpec((chips // 4, rows, 3 * part), lambda i: (i, 0, 0)),
        out_shape=jax.ShapeDtypeStruct((chips, rows, 3 * part), BF),
        compiler_params=pltpu.CompilerParams(vmem_limit_bytes=16 << 20),
        cost_estimate=SMALL,
        name="away_columns",
    )(core[None], whole)


def attention_weights(whole, come, core, nz, part):
    rows = whole.shape[1]
    depth = 8 * nz * rows
    strip = part // 4

    def body(core_ref, w_ref, c_ref, q_ref, kv_ref, dense_ref):
        mine = core_ref[0]
        for z in range(nz):
            own = pl.ds(pl.multiple_of((mine * nz + z) * rows, rows), rows)
            other = pl.ds(pl.multiple_of(((1 - mine) * nz + z) * rows, rows), rows)
            for b in range(12):
                value = w_ref[z, :, pl.ds(pl.multiple_of((2 * b + mine) * strip, strip), strip)]
                if b < 4:
                    q_ref[own, b * strip : (b + 1) * strip] = value
                else:
                    kv_ref[own, (b - 4) * strip : (b - 3) * strip] = value
            q_ref[other, :] = c_ref[z, :, :part]
            kv_ref[other, :] = c_ref[z, :, part:]
            dense_ref[z * rows : (z + 1) * rows, :] = w_ref[z, :, 6 * part :]

    block = lambda n: pl.BlockSpec((nz, rows, n), lambda i: (i, 0, 0))
    return pl.pallas_call(
        body,
        grid=(4,),
        in_specs=[pl.BlockSpec(memory_space=pltpu.SMEM), block(8 * part), block(3 * part)],
        out_specs=[
            pl.BlockSpec((depth // 4, part), lambda i: (i, 0)),
            pl.BlockSpec((depth // 4, 2 * part), lambda i: (i, 0)),
            pl.BlockSpec((depth // 8, 2 * part), lambda i: (i, 0)),
        ],
        out_shape=[
            jax.ShapeDtypeStruct((depth, part), BF),
            jax.ShapeDtypeStruct((depth, 2 * part), BF),
            jax.ShapeDtypeStruct((depth // 2, 2 * part), BF),
        ],
        compiler_params=pltpu.CompilerParams(vmem_limit_bytes=16 << 20),
        cost_estimate=SMALL,
        name="attention_weights",
    )(core[None], whole, come)


def unit_weights(whole, nz, rows, out_rows):
    columns = whole.shape[2]

    def body(w_ref, in_ref, out_ref):
        for z in range(nz):
            for j in range(4):
                at = (j * nz + z) * rows
                in_ref[at : at + rows, :] = w_ref[z, j * rows : (j + 1) * rows, :]
            out_ref[z * out_rows : (z + 1) * out_rows, :] = w_ref[z, 4 * rows :, :]

    return pl.pallas_call(
        body,
        grid=(2,),
        in_specs=[pl.BlockSpec((nz, 4 * rows + out_rows, columns), lambda i: (i, 0, 0))],
        out_specs=[
            pl.BlockSpec((4 * nz * rows, columns), lambda i: (i, 0)),
            pl.BlockSpec((nz * out_rows, columns), lambda i: (i, 0)),
        ],
        out_shape=[
            jax.ShapeDtypeStruct((8 * nz * rows, columns), BF),
            jax.ShapeDtypeStruct((2 * nz * out_rows, columns), BF),
        ],
        compiler_params=pltpu.CompilerParams(vmem_limit_bytes=16 << 20),
        cost_estimate=SMALL,
        name="unit_weights",
    )(whole)


def layer_norm(pieces, gain, bias, rows, first, extra, into=None, block=256):
    _, tok, width = pieces[0][0].shape
    steps = tok // block
    count = len(pieces)
    kept = 2 if extra else count

    def body(*refs):
        gain_ref, bias_ref = refs[count : count + 2]
        outs = refs[-2:] if extra else refs[-1:]
        i = pl.program_id(0)
        for p in range(count):

            @pl.when(i == p)
            def _():
                x = refs[p][0].astype(F32)
                centered = x - jnp.mean(x, axis=1, keepdims=True)
                variance = jnp.mean(centered * centered, axis=1, keepdims=True)
                value = centered * lax.rsqrt(variance + 1e-05)
                value = value * gain_ref[...] + bias_ref[...]
                if p < kept:
                    outs[0][...] = value.astype(BF)
                if extra:
                    outs[1][...] = value.astype(BF)

    def piece_spec(p):
        return pl.BlockSpec(
            (1, block, width),
            lambda i, b: (pieces[p][1], jnp.where(i == p, b, jnp.where(i < p, 0, steps - 1)), 0),
        )

    def kept_at(i, b):
        return first // block + jnp.where(i < kept, i * steps + b, kept * steps - 1)

    line = pl.BlockSpec((1, width), lambda i, b: (0, 0))
    out_specs = [pl.BlockSpec((block, width), lambda i, b: (kept_at(i, b), 0))]
    out_shape = [jax.ShapeDtypeStruct((rows, width), BF)]
    if extra:
        out_specs += [pl.BlockSpec((block, width), lambda i, b: (i * steps + b, 0))]
        out_shape += [jax.ShapeDtypeStruct((count * tok, width), BF)]
    given = [] if into is None else [into]
    return pl.pallas_call(
        body,
        grid=(count, steps),
        in_specs=[piece_spec(p) for p in range(count)] + [line, line] + [ANY] * len(given),
        out_specs=out_specs,
        out_shape=out_shape,
        input_output_aliases={} if into is None else {count + 2: 0},
        compiler_params=pltpu.CompilerParams(vmem_limit_bytes=32 << 20),
        cost_estimate=SMALL,
        name="layer_norm",
    )(*(p[0] for p in pieces), gain.reshape(1, width), bias.reshape(1, width), *given)


def attention_weight_grads(normed, attended, dq, dkv, grads, nz):
    tokens, part = dq.shape
    all_tokens, width = normed.shape
    near = all_tokens - tokens
    block, strip = width // 4, part // 4

    rows = strip // nz

    def body(n_ref, a_ref, d_ref, dkv_ref, g_ref, o_ref):
        def put(value, at):
            for h in range(2):
                for z in range(nz):
                    low = (h * nz + z) * rows
                    o_ref[0, z, h, :, at] = value[low : low + rows]

        put(tn(n_ref[near:, :], d_ref[...]).astype(BF), slice(0, part))
        put(tn(n_ref[...], dkv_ref[...]).astype(BF), slice(part, 3 * part))
        dense = tn(a_ref[...], g_ref[...]).astype(BF)
        put(jnp.concatenate([dense[:, :part], dense[:, part:]]), slice(3 * part, 4 * part))

    whole = lambda a: pl.BlockSpec(a.shape, lambda i: (0, 0))
    return pl.pallas_call(
        body,
        grid=(4,),
        in_specs=[
            pl.BlockSpec((all_tokens, block), lambda i: (0, i)),
            pl.BlockSpec((tokens, strip), lambda i: (0, i)),
            whole(dq),
            whole(dkv),
            pl.BlockSpec((tokens, width), lambda i: (0, 0)),
        ],
        out_specs=pl.BlockSpec((1, nz, 2, rows, 4 * part), lambda i: (i, 0, 0, 0, 0)),
        out_shape=jax.ShapeDtypeStruct((4, nz, 2, rows, 4 * part), BF),
        compiler_params=pltpu.CompilerParams(vmem_limit_bytes=48 << 20),
        cost_estimate=SMALL,
        name="attention_weight_grads",
    )(normed, attended, dq, dkv, grads)


def summed(*values):
    return sum(v.astype(F32) for v in values).astype(BF)


def z_scatter(parts, axis, zi, nz):
    steps = []
    for k, pairs in enumerate(z_pairs(nz)):
        shape = parts.shape
        blocks = parts.reshape(shape[:axis] + (shape[axis] // 2, 2) + shape[axis + 1 :])
        bit = (zi >> k) & 1
        come = lax.ppermute(pick(blocks, 1 - bit, axis + 1), "z", pairs)
        parts = summed(pick(blocks, bit, axis + 1), come)
        steps.append(parts)
    return steps[:-1] + [lax.squeeze(parts, (axis,))]


def normalise(tokens):
    row_mean = jnp.mean(tokens, axis=-1, keepdims=True)
    centered = tokens - row_mean
    variance = jnp.mean(centered * centered, axis=-1, keepdims=True)
    inv_std = lax.rsqrt(variance + 1e-05)
    return centered * inv_std, inv_std


def pick(blocks, index, axis):
    return lax.dynamic_index_in_dim(blocks, index, axis, keepdims=False)


def by_place(place, mine, theirs):
    low = jnp.where(place == 0, mine, theirs)
    high = jnp.where(place == 0, theirs, mine)
    return jnp.stack([low, high])


def z_pairs(nz):
    return [[(i, i ^ (1 << k)) for i in range(nz)] for k in range(nz.bit_length() - 1)]


def local_plane(
    nz,
    hidden_in,
    doc_lengths,
    ln_gain,
    ln_bias,
    w_qkv,
    b_qkv,
    w_dense,
    b_dense,
    w_in,
    b_in,
    w_out,
    b_out,
    out_grad,
):
    core, xi, yi, zi = (lax.axis_index(a) for a in "cxyz")
    chip = yi * 2 + xi
    halo = nz // 2
    _, tok, width = hidden_in.shape
    rows, ff = w_in.shape
    out_rows = w_out.shape[0]
    part = width // 2
    units = ff // 4
    up = [(i, i + 1) for i in range(nz - 1)]
    down = [(i + 1, i) for i in range(nz - 1)]
    hidden_own, grad_own = hidden_in[0], out_grad[0]

    small = jnp.concatenate([ln_gain, ln_bias, b_qkv, b_dense, b_in, b_out])[None]
    sizes = [v.shape[0] for v in (ln_gain, ln_bias, b_qkv, b_dense, b_in, b_out)]
    small_len = small.shape[1]
    first_whole = lax.all_gather(
        jnp.concatenate([w_qkv, w_dense], axis=1), ("y", "x", "z"), axis=0, tiled=False
    )
    come = other_core(away_columns(first_whole, core, part))

    def halves(weight, shape, axis, place):
        blocks = weight.reshape(shape)
        return pick(blocks, place, axis), pick(blocks, 1 - place, axis)

    in_mine, in_theirs = halves(w_in, (rows, 4, 2, -1), 2, core)
    in_got = other_core(in_theirs.reshape(rows, -1))
    in_core = by_place(core, in_mine.reshape(rows, -1), in_got)
    in_mine, in_theirs = halves(in_core, (2 * rows, 2, 2, -1), 2, xi)
    in_got = over_x(in_theirs.reshape(2 * rows, units))
    in_piece = by_place(xi, in_mine.reshape(2 * rows, units), in_got).reshape(4 * rows, units)

    before = [hidden_own]
    for _ in range(halo):
        before.append(lax.ppermute(before[-1], "z", up))
    pair_own = jnp.stack([hidden_own, grad_own])
    pair_x = over_x(pair_own)
    pair_other, pair_x_other = other_core(pair_own), other_core(pair_x)
    lens_other = other_core(doc_lengths)
    near = [pair_own, pair_other, pair_x, pair_x_other]

    for place, move in ((core, other_core), (xi, over_x), (yi, over_y)):
        small = by_place(place, small, move(small)).reshape(-1, small_len)
    for k, pairs in enumerate(z_pairs(nz)):
        small = by_place((zi >> k) & 1, small, lax.ppermute(small, "z", pairs))
        small = small.reshape(-1, small_len)
    small = small.reshape(nz, 8, small_len).transpose(1, 0, 2).reshape(8 * nz, small_len).astype(F32)
    cuts = [sum(sizes[:i]) for i in range(7)]
    gain, bias, qkv_bias, dense_bias, in_bias, out_bias = (
        small[:, cuts[i] : cuts[i + 1]].reshape(-1) for i in range(6)
    )
    qkv_bias = pick(qkv_bias.reshape(3, 4, 2, -1), core, 2).reshape(-1)
    in_bias = pick(pick(in_bias.reshape(2, 2, 2, -1), core, 2), xi, 1).reshape(-1)

    both = 2 * tok
    kv_rows = (halo + 1) * both
    normed_kv, normed_all = layer_norm(
        [(v, 0) for v in near], gain, bias, kv_rows, halo * both, True
    )
    grads_all = jnp.concatenate([v[1] for v in near])

    w_q_f, w_kv_f, w_dense_f = attention_weights(first_whole, come, core, nz, part)
    queries = matmul(normed_all, w_q_f, "nn", bias=qkv_bias[:part], rows=both)
    grad_att = matmul(grads_all, w_dense_f, "nt", rows=both)
    far = []
    for value in before[:0:-1]:
        far += [(value[None], 0), (other_core(value)[None], 0)]
    (normed_kv,) = layer_norm(far, gain, bias, kv_rows, 0, False, into=normed_kv)
    key_values = (mm(normed_kv, w_kv_f) + qkv_bias[part:]).astype(BF)
    second_whole = lax.all_gather(
        held(jnp.concatenate([in_piece, w_out]), first_whole), ("y", "z"), axis=0, tiled=False
    )

    base = (zi - halo) * tok
    positions = (base + jnp.arange((halo + 1) * tok, dtype=jnp.int32)).astype(F32)
    lane = jnp.arange(LANES, dtype=jnp.int32) % HEAD_DIM
    half_rot = ROT_DIM // 2
    frequency = jnp.exp(-math.log(10000.0) * 2.0 * (lane % half_rot).astype(F32) / ROT_DIM)
    angles = positions[:, None] * frequency[None, :]
    cosine, sine = jnp.cos(angles), jnp.sin(angles)
    keep = jnp.where(lane < ROT_DIM, cosine, 1.0)
    sine = jnp.where(lane < ROT_DIM, sine, 0.0)

    def doc_starts(lens):
        ends = prefix_ends(lens)
        own = zi * tok + jnp.arange(tok, dtype=jnp.int32)
        return jnp.max(jnp.where(own[:, None] >= ends[None, :], ends[None, :], 0), axis=1)

    starts = jnp.stack([doc_starts(doc_lengths[0]), doc_starts(lens_other[0])])
    lower = jnp.maximum((starts[:, ::CHUNK] - base) // CHUNK, 0)
    scalars = jnp.concatenate([lower.reshape(-1), base[None]]).astype(jnp.int32)
    attended, dq, dkv = attention(
        queries.reshape(2, tok, part),
        key_values.reshape(halo + 1, 2, tok, 2 * part),
        grad_att.reshape(2, tok, part),
        keep,
        sine,
        starts[:, None, :],
        scalars,
    )
    attended = attended.reshape(both, part)
    dq = dq.reshape(both, part)
    dkv = dkv.reshape(kv_rows, 2 * part)

    def after(*deps):
        return held(jnp.zeros((1, width), F32), *deps)

    dn_kv = nt(dkv, w_kv_f).astype(BF).reshape(halo + 1, 2, tok, width)
    dn_come = other_core(dn_kv[:halo, 1])
    g_att = attention_weight_grads(normed_kv, attended, dq, dkv, grads_all, nz)
    dn_far = summed(dn_kv[:halo, 0], held(dn_come, g_att))
    dn_q = matmul(dq, w_q_f, "nt").reshape(2, tok, width)
    dn_att = summed(dn_q, dn_kv[halo])

    s_att = lax.psum_scatter(
        g_att.reshape(4, nz, 2, rows, 4 * part), ("y", "x"), scatter_dimension=0, tiled=False
    )
    s_att = lax.psum_scatter(s_att, "z", scatter_dimension=0, tiled=False)

    w_in_f, w_out_f = unit_weights(second_whole, nz, rows, out_rows)
    activated, grad_pre, pre_sum = feed_forward(
        normed_all, grads_all, w_in_f, in_bias, w_out_f, deps=(dn_far, dn_att)
    )
    passed = dn_far[0]
    for step in range(1, halo):
        come = held(lax.ppermute(passed, "z", down), pre_sum)
        passed = summed(dn_far[step], come)
    dn_back = lax.ppermute(passed, "z", down)

    def away_tokens(shared, attn):
        return jnp.stack([summed(shared[0, 1], attn[1]), shared[1, 1]])

    g_in = matmul(normed_all, grad_pre, "tn", deps=(passed,)).reshape(2, -1, units)
    in_away = pick(g_in, 1 - yi, 0)
    in_y = over_y(in_away)
    dn_ff = (nt(grad_pre, w_in_f) + after(in_away)).astype(BF).reshape(2, 2, tok, width)
    dn_away = away_tokens(dn_ff, dn_att)
    g_out = matmul(activated, grads_all, "tn", deps=(dn_away,)).reshape(2, -1, width)
    out_away = pick(g_out, 1 - yi, 0)
    out_y = over_y(out_away)
    dn_come = held(other_core(dn_away), g_out)
    dn_send = summed(dn_ff[1, 0], dn_come[1])
    dn_x = over_x(dn_send)
    branch = (mm(activated, w_out_f) + after(out_away, dn_send)).astype(BF)
    branch = branch.reshape(2, 2, tok, width)
    branch_att = matmul(attended, w_dense_f, "nn", deps=(dn_send,)).reshape(2, tok, width)
    br_come = other_core(away_tokens(branch, branch_att))
    br_send = summed(branch[1, 0], br_come[1])
    br_x = over_x(br_send)

    s_in = summed(pick(g_in, yi, 0), held(in_y, br_send)).reshape(4, nz, rows, units)
    dn_x = held(dn_x, s_in)
    s_in_steps = z_scatter(s_in, 1, zi, nz)
    s_in = s_in_steps[-1].reshape(2, 2, rows, units)
    in_x = over_x(pick(s_in, 1 - xi, 0))
    dn_parts = [dn_ff[0, 0], dn_att[0], dn_come[0]]
    br_parts = [branch[0, 0], branch_att[0], br_come[0]]

    x = hidden_own.astype(F32)
    gy = grad_own.astype(F32)
    dn = sum(v.astype(F32) for v in (*dn_parts, dn_x, dn_back))
    xhat, inv_std = normalise(x)
    scaled = dn * gain
    grad_input = gy + inv_std * (
        scaled
        - jnp.mean(scaled, axis=1, keepdims=True)
        - xhat * jnp.mean(scaled * xhat, axis=1, keepdims=True)
    )
    out_y, br_x = held(out_y, grad_input), held(br_x, grad_input)
    s_out = summed(pick(g_out, yi, 0), out_y).reshape(nz, out_rows, width)
    grad_w_out = z_scatter(s_out, 0, zi, nz)[-1].astype(F32)
    hidden_out = (
        x + sum(v.astype(F32) for v in (*br_parts, br_x)) + dense_bias + out_bias
    ).astype(BF)

    def spread(vector, shape, mine):
        return jnp.where(mine, vector.reshape(shape), 0.0).reshape(-1)

    two = jnp.arange(2)
    g_qkv_bias = jnp.concatenate([jnp.sum(v.astype(F32), axis=0) for v in (dq, dkv)])
    small_grads = [
        jnp.sum(dn * xhat, axis=0),
        jnp.sum(dn, axis=0),
        spread(g_qkv_bias, (3, 4, 1, -1), (two == core)[None, None, :, None]),
        jnp.sum(gy, axis=0),
        spread(
            jnp.sum(pre_sum, axis=0),
            (2, 1, 1, -1),
            ((two == xi)[:, None] & (two == core)[None, :])[None, :, :, None],
        ),
    ]
    small_sizes = [g.shape[0] for g in small_grads]
    total = held(jnp.concatenate(small_grads), s_in_steps[0])
    total = total + other_core(total)
    total = held(total + over_x(total), s_in)
    total = held(total + over_y(total), in_x)
    for pairs in z_pairs(nz):
        total = total + lax.ppermute(total, "z", pairs)
    device = (chip * 2 + core) * nz + zi
    small_out, at = [], 0
    for size in small_sizes:
        share = size // (8 * nz)
        small_out.append(lax.dynamic_slice_in_dim(total, at + device * share, share, 0))
        at += size
    g_gain, g_bias, g_bqkv, g_bdense, g_bin = small_out

    def home_core(columns):
        axis = columns.ndim - 3
        return by_place(core, pick(columns, core, axis), other_core(pick(columns, 1 - core, axis)))

    grad_w_dense = s_att[:, :, 3 * part :].transpose(1, 0, 2).reshape(rows, width).astype(F32)
    s_qkv = home_core(s_att[:, :, : 3 * part])
    grad_w_qkv = s_qkv.reshape(2, rows, 3, 4, -1).transpose(1, 2, 3, 0, 4).reshape(rows, -1)
    s_in = home_core(by_place(xi, pick(s_in, xi, 0), in_x))
    grad_w_in = s_in.reshape(2, 2, rows, 2, -1).transpose(2, 3, 1, 0, 4).reshape(rows, -1)
    return (
        hidden_out[None],
        grad_input[None],
        g_gain,
        g_bias,
        grad_w_qkv.astype(F32),
        g_bqkv,
        grad_w_dense,
        g_bdense,
        grad_w_in.astype(F32),
        g_bin,
        grad_w_out,
        g_bdense,
    )


def solution(mesh):
    n_seq, n_group = mesh.devices.shape
    if n_seq == 8 and n_group == 4:
        mesh = Mesh(mesh.devices.reshape(2, 2, 2, n_group), ("y", "x", "c", "z"))
        seq, group = ("y", "x", "c"), "z"
        both = ("y", "x", "c", "z")
        step = functools.partial(local_plane, n_group)
    else:
        seq, group, both = "seq", "group", ("seq", "group")
        step = local_generic
    matrix, vector = P(both, None), P(both)
    tokens = P(seq, group, None)
    weights = (vector, vector) + (matrix, vector) * 4
    return jax.shard_map(
        step,
        mesh=mesh,
        in_specs=(tokens, P(seq, None)) + weights + (tokens,),
        out_specs=(tokens, tokens) + weights,
        check_vma=False,
    )
```

```python
import functools
import math

import jax
import jax.numpy as jnp
from jax import lax
from jax.experimental import pallas as pl
from jax.experimental.pallas import tpu as pltpu
from jax.sharding import Mesh
from jax.sharding import PartitionSpec as P

HEADS = 16
HEAD_DIM = 64
ROT_DIM = 16


def prefix_ends(doc_lens):
    order = jnp.arange(doc_lens.shape[0], dtype=jnp.int32)
    return jnp.sum(jnp.where(order[None, :] <= order[:, None], doc_lens[None, :], 0), axis=1)


def dot_rows(left, right):
    return lax.dot_general(
        left, right, (((0,), (0,)), ((), ())), preferred_element_type=jnp.float32
    )


def dot_last(left, right):
    return lax.dot_general(
        left, right, (((1,), (1,)), ((), ())), preferred_element_type=jnp.float32
    )


def rope_tables(token_positions, rot_dim):
    half_rot = rot_dim // 2
    frequency = jnp.exp(
        -math.log(10000.0) * 2.0 * jnp.arange(half_rot, dtype=jnp.float32) / rot_dim
    )
    angles = token_positions.astype(jnp.float32)[:, None] * frequency[None, :]
    return (jnp.cos(angles)[:, None, :], jnp.sin(angles)[:, None, :])


def rotate(heads, cosine, sine, rot_dim):
    half_rot = rot_dim // 2
    first_half = heads[:, :, :half_rot]
    second_half = heads[:, :, half_rot:rot_dim]
    remainder = heads[:, :, rot_dim:]
    return jnp.concatenate(
        [
            first_half * cosine - second_half * sine,
            second_half * cosine + first_half * sine,
            remainder,
        ],
        axis=2,
    )


def gelu_exact(preact):
    return jax.nn.gelu(preact, approximate=False)


def block_scores(query_block, key_tile_block, seg_query, seg_key, pos_query, pos_key, score_scale):
    scaled = (
        jnp.einsum("qhd,khd->hqk", query_block, key_tile_block, preferred_element_type=jnp.float32)
        * score_scale
    )
    allowed = (seg_query[:, None] == seg_key[None, :]) & (pos_key[None, :] <= pos_query[:, None])
    return jnp.where(allowed[None], scaled, -1e30)


def owning_block(source, block_index, block_of_rows):
    return lax.dynamic_slice_in_dim(source, block_index * block_of_rows, block_of_rows, 0)


def add_block(source, block_index, block_of_rows, addend):
    current = owning_block(source, block_index, block_of_rows)
    return lax.dynamic_update_slice_in_dim(source, current + addend, block_index * block_of_rows, 0)


def attention_forward(
    query_heads,
    key_head_rows,
    value_head_rows,
    document_segment,
    token_positions,
    seg_start,
    block_of_rows,
):
    seq_len, head_count, head_dim = query_heads.shape
    score_scale = 1.0 / math.sqrt(head_dim)

    def query_step(qindex, state_now):
        outputs, log_sums = state_now
        query_block = owning_block(query_heads, qindex, block_of_rows)
        seg_query = owning_block(document_segment, qindex, block_of_rows)
        pos_query = owning_block(token_positions, qindex, block_of_rows)
        key_lower = seg_start[qindex * block_of_rows] // block_of_rows

        def scores_for_block(key_position_index):
            return block_scores(
                query_block,
                owning_block(key_head_rows, key_position_index, block_of_rows),
                seg_query,
                owning_block(document_segment, key_position_index, block_of_rows),
                pos_query,
                owning_block(token_positions, key_position_index, block_of_rows),
                score_scale,
            )

        def statistics_step(key_position_index, row_statistics):
            run_max, run_sum = row_statistics
            logit_scores = scores_for_block(key_position_index)
            new_max = jnp.maximum(run_max, jnp.max(logit_scores, axis=2))
            run_sum = run_sum * jnp.exp(run_max - new_max) + jnp.sum(
                jnp.exp(logit_scores - new_max[:, :, None]), axis=2
            )
            return (new_max, run_sum)

        start_stats = (
            jnp.full((head_count, block_of_rows), -1e30, jnp.float32),
            jnp.zeros((head_count, block_of_rows), jnp.float32),
        )
        run_max, run_sum = lax.fori_loop(key_lower, qindex + 1, statistics_step, start_stats)
        log_exp_total = run_max + jnp.log(run_sum)

        def value_loop_step(key_position_index, partial_output):
            attention_weights = jnp.exp(
                scores_for_block(key_position_index) - log_exp_total[:, :, None]
            ).astype(jnp.bfloat16)
            return partial_output + jnp.einsum(
                "hqk,khd->qhd",
                attention_weights,
                owning_block(value_head_rows, key_position_index, block_of_rows),
                preferred_element_type=jnp.float32,
            )

        block_out = lax.fori_loop(
            key_lower,
            qindex + 1,
            value_loop_step,
            jnp.zeros((block_of_rows, head_count, head_dim), jnp.float32),
        )
        outputs = lax.dynamic_update_slice_in_dim(outputs, block_out, qindex * block_of_rows, 0)
        log_sums = lax.dynamic_update_slice_in_dim(
            log_sums, log_exp_total, qindex * block_of_rows, 1
        )
        return (outputs, log_sums)

    start_state = (
        jnp.zeros((seq_len, head_count, head_dim), jnp.float32),
        jnp.zeros((head_count, seq_len), jnp.float32),
    )
    return lax.fori_loop(0, seq_len // block_of_rows, query_step, start_state)


def attention_backward(
    query_heads,
    key_head_rows,
    value_head_rows,
    grad_heads,
    outputs,
    log_sums,
    document_segment,
    token_positions,
    seg_start,
    block_of_rows,
):
    seq_len, head_count, head_dim = query_heads.shape
    score_scale = 1.0 / math.sqrt(head_dim)
    delta_all = jnp.sum(grad_heads.astype(jnp.float32) * outputs, axis=2).T

    def query_step(qindex, state_now):
        grad_query_all, grad_key_all, grad_value_all = state_now
        query_block = owning_block(query_heads, qindex, block_of_rows)
        grad_block = owning_block(grad_heads, qindex, block_of_rows)
        seg_query = owning_block(document_segment, qindex, block_of_rows)
        pos_query = owning_block(token_positions, qindex, block_of_rows)
        log_exp_total = lax.dynamic_slice_in_dim(log_sums, qindex * block_of_rows, block_of_rows, 1)
        delta_block = lax.dynamic_slice_in_dim(delta_all, qindex * block_of_rows, block_of_rows, 1)
        key_lower = seg_start[qindex * block_of_rows] // block_of_rows

        def key_loop_step(key_position_index, loop_state_inner):
            grad_query, grad_keys, grad_values = loop_state_inner
            key_tile_block = owning_block(key_head_rows, key_position_index, block_of_rows)
            value_tile_block = owning_block(value_head_rows, key_position_index, block_of_rows)
            logit_scores = block_scores(
                query_block,
                key_tile_block,
                seg_query,
                owning_block(document_segment, key_position_index, block_of_rows),
                pos_query,
                owning_block(token_positions, key_position_index, block_of_rows),
                score_scale,
            )
            probability = jnp.exp(logit_scores - log_exp_total[:, :, None])
            grad_values = add_block(
                grad_values,
                key_position_index,
                block_of_rows,
                jnp.einsum(
                    "hqk,qhd->khd",
                    probability.astype(jnp.bfloat16),
                    grad_block,
                    preferred_element_type=jnp.float32,
                ),
            )
            grad_probs = jnp.einsum(
                "qhd,khd->hqk", grad_block, value_tile_block, preferred_element_type=jnp.float32
            )
            grad_scores = (probability * (grad_probs - delta_block[:, :, None])).astype(
                jnp.bfloat16
            )
            grad_query = (
                grad_query
                + jnp.einsum(
                    "hqk,khd->qhd", grad_scores, key_tile_block, preferred_element_type=jnp.float32
                )
                * score_scale
            )
            grad_keys = add_block(
                grad_keys,
                key_position_index,
                block_of_rows,
                jnp.einsum(
                    "hqk,qhd->khd", grad_scores, query_block, preferred_element_type=jnp.float32
                )
                * score_scale,
            )
            return (grad_query, grad_keys, grad_values)

        start_inner = (
            jnp.zeros((block_of_rows, head_count, head_dim), jnp.float32),
            grad_key_all,
            grad_value_all,
        )
        grad_query, grad_key_all, grad_value_all = lax.fori_loop(
            key_lower, qindex + 1, key_loop_step, start_inner
        )
        grad_query_all = lax.dynamic_update_slice_in_dim(
            grad_query_all, grad_query, qindex * block_of_rows, 0
        )
        return (grad_query_all, grad_key_all, grad_value_all)

    zero_heads = jnp.zeros((seq_len, head_count, head_dim), jnp.float32)
    return lax.fori_loop(
        0, seq_len // block_of_rows, query_step, (zero_heads, zero_heads, zero_heads)
    )


def local_generic(
    hidden_in,
    doc_lengths,
    ln_gain,
    ln_bias,
    w_qkv,
    b_qkv,
    w_dense,
    b_dense,
    w_in,
    b_in,
    w_out,
    b_out,
    out_grad,
):
    (
        full_gain,
        full_bias,
        full_qkv,
        full_qkv_bias,
        full_dense,
        full_dense_bias,
        full_in,
        full_in_bias,
        full_out,
        full_out_bias,
    ) = (
        lax.all_gather(ln_gain, ("seq", "group"), axis=0, tiled=True),
        lax.all_gather(ln_bias, ("seq", "group"), axis=0, tiled=True),
        lax.all_gather(w_qkv, ("seq", "group"), axis=0, tiled=True),
        lax.all_gather(b_qkv, ("seq", "group"), axis=0, tiled=True),
        lax.all_gather(w_dense, ("seq", "group"), axis=0, tiled=True),
        lax.all_gather(b_dense, ("seq", "group"), axis=0, tiled=True),
        lax.all_gather(w_in, ("seq", "group"), axis=0, tiled=True),
        lax.all_gather(b_in, ("seq", "group"), axis=0, tiled=True),
        lax.all_gather(w_out, ("seq", "group"), axis=0, tiled=True),
        lax.all_gather(b_out, ("seq", "group"), axis=0, tiled=True),
    )
    tokens = hidden_in[0].astype(jnp.float32)
    tok_count = tokens.shape[0]
    width = tokens.shape[1]
    row_mean = jnp.mean(tokens, axis=1, keepdims=True)
    centered = tokens - row_mean
    variance = jnp.mean(centered * centered, axis=1, keepdims=True)
    inv_std = lax.rsqrt(variance + 1e-05)
    normal_rows = centered * inv_std
    normed = (normal_rows * full_gain.astype(jnp.float32) + full_bias.astype(jnp.float32)).astype(
        jnp.bfloat16
    )
    mixed = jnp.dot(normed, full_qkv, preferred_element_type=jnp.float32) + full_qkv_bias.astype(
        jnp.float32
    )
    token_positions = lax.axis_index("group") * tok_count + jnp.arange(tok_count, dtype=jnp.int32)
    cosine, sine = rope_tables(token_positions, ROT_DIM)
    head_shape = (tok_count, HEADS, HEAD_DIM)
    queries = (
        rotate(mixed[:, :width].reshape(head_shape), cosine, sine, ROT_DIM)
        .reshape(tok_count, width)
        .astype(jnp.bfloat16)
    )
    key_rows = (
        rotate(mixed[:, width : 2 * width].reshape(head_shape), cosine, sine, ROT_DIM)
        .reshape(tok_count, width)
        .astype(jnp.bfloat16)
    )
    value_rows = mixed[:, 2 * width :].astype(jnp.bfloat16)
    query_cols, key_cols, value_cols = (
        lax.all_to_all(queries, "group", split_axis=1, concat_axis=0, tiled=True),
        lax.all_to_all(key_rows, "group", split_axis=1, concat_axis=0, tiled=True),
        lax.all_to_all(value_rows, "group", split_axis=1, concat_axis=0, tiled=True),
    )
    seq_len = query_cols.shape[0]
    head_count = query_cols.shape[1] // HEAD_DIM
    heads_shape = (seq_len, head_count, HEAD_DIM)
    query_heads = query_cols.reshape(heads_shape)
    key_head_rows = key_cols.reshape(heads_shape)
    value_head_rows = value_cols.reshape(heads_shape)
    all_pos = jnp.arange(seq_len, dtype=jnp.int32)
    doc_lens = doc_lengths[0]
    doc_ends = prefix_ends(doc_lens)
    document_segment = jnp.sum((all_pos[:, None] >= doc_ends[None, :]).astype(jnp.int32), axis=1)
    doc_starts = doc_ends - doc_lens
    doc_index = jnp.arange(doc_ends.shape[0], dtype=jnp.int32)
    seg_start = jnp.sum(
        jnp.where(document_segment[:, None] == doc_index[None, :], doc_starts[None, :], 0), axis=1
    )
    block_of_rows = min(512, seq_len)
    outputs, log_sums = attention_forward(
        query_heads,
        key_head_rows,
        value_head_rows,
        document_segment,
        all_pos,
        seg_start,
        block_of_rows,
    )
    attended = lax.all_to_all(
        outputs.reshape(seq_len, head_count * HEAD_DIM).astype(jnp.bfloat16),
        "group",
        split_axis=0,
        concat_axis=1,
        tiled=True,
    )
    branch_attn = jnp.dot(
        attended, full_dense, preferred_element_type=jnp.float32
    ) + full_dense_bias.astype(jnp.float32)
    pre_act = jnp.dot(normed, full_in, preferred_element_type=jnp.float32) + full_in_bias.astype(
        jnp.float32
    )
    activated = gelu_exact(pre_act).astype(jnp.bfloat16)
    branch_mlp = jnp.dot(
        activated, full_out, preferred_element_type=jnp.float32
    ) + full_out_bias.astype(jnp.float32)
    hidden_out = (tokens + branch_attn + branch_mlp).astype(jnp.bfloat16)
    grad_rows = out_grad[0]
    grad_float = grad_rows.astype(jnp.float32)
    bias_grad = jnp.sum(grad_float, axis=0)
    grad_dense = dot_rows(attended, grad_rows)
    grad_out_w = dot_rows(activated, grad_rows)
    grad_act = dot_last(grad_rows, full_out)
    grad_pre = jax.vjp(gelu_exact, pre_act)[1](grad_act)[0].astype(jnp.bfloat16)
    grad_in_w = dot_rows(normed, grad_pre)
    grad_in_bias = jnp.sum(grad_pre.astype(jnp.float32), axis=0)
    grad_normed = dot_last(grad_pre, full_in)
    grad_attended = dot_last(grad_rows, full_dense).astype(jnp.bfloat16)
    grad_cols = lax.all_to_all(grad_attended, "group", split_axis=1, concat_axis=0, tiled=True)
    grad_query_all, grad_key_all, grad_value_all = attention_backward(
        query_heads,
        key_head_rows,
        value_head_rows,
        grad_cols.reshape(heads_shape),
        outputs,
        log_sums,
        document_segment,
        all_pos,
        seg_start,
        block_of_rows,
    )
    flat_shape = (seq_len, head_count * HEAD_DIM)
    grad_query_tok, grad_key_tok, grad_value_tok = (
        lax.all_to_all(
            grad_query_all.reshape(flat_shape).astype(jnp.bfloat16),
            "group",
            split_axis=0,
            concat_axis=1,
            tiled=True,
        ),
        lax.all_to_all(
            grad_key_all.reshape(flat_shape).astype(jnp.bfloat16),
            "group",
            split_axis=0,
            concat_axis=1,
            tiled=True,
        ),
        lax.all_to_all(
            grad_value_all.reshape(flat_shape).astype(jnp.bfloat16),
            "group",
            split_axis=0,
            concat_axis=1,
            tiled=True,
        ),
    )
    unrot_query = (
        rotate(grad_query_tok.astype(jnp.float32).reshape(head_shape), cosine, -sine, ROT_DIM)
        .reshape(tok_count, width)
        .astype(jnp.bfloat16)
    )
    unrot_key = (
        rotate(grad_key_tok.astype(jnp.float32).reshape(head_shape), cosine, -sine, ROT_DIM)
        .reshape(tok_count, width)
        .astype(jnp.bfloat16)
    )
    grad_mixed = jnp.concatenate([unrot_query, unrot_key, grad_value_tok], axis=1)
    grad_qkv_w = dot_rows(normed, grad_mixed)
    grad_qkv_bias = jnp.sum(grad_mixed.astype(jnp.float32), axis=0)
    grad_normed = grad_normed + dot_last(grad_mixed, full_qkv)
    scaled_grad = grad_normed * full_gain.astype(jnp.float32)
    grad_gain = jnp.sum(grad_normed * normal_rows, axis=0)
    grad_bias = jnp.sum(grad_normed, axis=0)
    grad_input = grad_float + inv_std * (
        scaled_grad
        - jnp.mean(scaled_grad, axis=1, keepdims=True)
        - normal_rows * jnp.mean(scaled_grad * normal_rows, axis=1, keepdims=True)
    )
    sharded = tuple(
        (
            lax.psum_scatter(grad_gain, ("seq", "group"), scatter_dimension=0, tiled=True),
            lax.psum_scatter(grad_bias, ("seq", "group"), scatter_dimension=0, tiled=True),
            lax.psum_scatter(grad_qkv_w, ("seq", "group"), scatter_dimension=0, tiled=True),
            lax.psum_scatter(grad_qkv_bias, ("seq", "group"), scatter_dimension=0, tiled=True),
            lax.psum_scatter(grad_dense, ("seq", "group"), scatter_dimension=0, tiled=True),
            lax.psum_scatter(bias_grad, ("seq", "group"), scatter_dimension=0, tiled=True),
            lax.psum_scatter(grad_in_w, ("seq", "group"), scatter_dimension=0, tiled=True),
            lax.psum_scatter(grad_in_bias, ("seq", "group"), scatter_dimension=0, tiled=True),
            lax.psum_scatter(grad_out_w, ("seq", "group"), scatter_dimension=0, tiled=True),
            lax.psum_scatter(bias_grad, ("seq", "group"), scatter_dimension=0, tiled=True),
        )
    )
    return (hidden_out[None], grad_input[None]) + sharded


SWAP = [(0, 1), (1, 0)]
CHUNK = 256
LANES = 128
BF = jnp.bfloat16
F32 = jnp.float32
ANY = pl.BlockSpec(memory_space=pl.ANY)
SMALL = pl.CostEstimate(flops=0, bytes_accessed=1 << 20, transcendentals=0)


def mm(left, right):
    return jnp.dot(left, right, preferred_element_type=F32)


def other_core(value):
    return lax.ppermute(value, "c", SWAP)


def over_x(value):
    return lax.ppermute(value, "x", SWAP)


def over_y(value):
    return lax.ppermute(value, "y", SWAP)


def nt(left, right):
    return lax.dot_general(left, right, (((1,), (1,)), ((), ())), preferred_element_type=F32)


def tn(left, right):
    return lax.dot_general(left, right, (((0,), (0,)), ((), ())), preferred_element_type=F32)


def matmul(left, right, form, deps=(), bias=None, block=512, dtype=BF, rows=None):
    rows = rows or (left.shape[1] if form == "tn" else left.shape[0])
    depth = left.shape[0] if form == "tn" else left.shape[1]
    columns = right.shape[0] if form == "nt" else right.shape[1]
    block = min(block, rows)
    dot = {"nn": mm, "nt": nt, "tn": tn}[form]

    def body(left_ref, right_ref, *rest):
        value = dot(left_ref[...], right_ref[...])
        if bias is not None:
            value = value + rest[0][...]
        rest[-1][...] = value.astype(dtype)

    if form == "tn":
        left_spec = pl.BlockSpec((depth, block), lambda i: (0, i))
    else:
        left_spec = pl.BlockSpec((block, depth), lambda i: (i, 0))
    whole = pl.BlockSpec(right.shape, lambda i: (0, 0))
    row = [] if bias is None else [pl.BlockSpec((1, columns), lambda i: (0, 0))]
    given = [] if bias is None else [bias.reshape(1, columns)]
    return pl.pallas_call(
        body,
        grid=(rows // block,),
        in_specs=[left_spec, whole] + row + [ANY] * len(deps),
        out_specs=pl.BlockSpec((block, columns), lambda i: (i, 0)),
        out_shape=jax.ShapeDtypeStruct((rows, columns), dtype),
        compiler_params=pltpu.CompilerParams(vmem_limit_bytes=48 << 20),
        cost_estimate=SMALL,
        name="matmul_" + form,
    )(left, right, *given, *deps)


def held(value, *deps):
    def body(*refs):
        pass

    return pl.pallas_call(
        body,
        in_specs=[ANY] * (1 + len(deps)),
        out_specs=ANY,
        out_shape=jax.ShapeDtypeStruct(value.shape, value.dtype),
        input_output_aliases={0: 0},
        compiler_params=pltpu.CompilerParams(vmem_limit_bytes=1 << 20),
        name="held",
    )(value, *deps)


def gelu_parts(value):
    size = jnp.abs(value)
    t = 1.0 / (1.0 + (0.3275911 / math.sqrt(2.0)) * size)
    poly = t * (
        0.254829592
        + t * (-0.284496736 + t * (1.421413741 + t * (-1.453152027 + t * 1.061405429)))
    )
    density = jnp.exp(-0.5 * value * value)
    tail = 0.5 * poly * density
    below = jnp.where(value < 0, tail, 1.0 - tail)
    return value * below, below + value * density * (1.0 / math.sqrt(2.0 * math.pi))


def feed_forward(normed, grads, w_in, bias, w_out, deps=(), block=512):
    tokens, width = normed.shape
    units = w_in.shape[1]

    def body(n_ref, g_ref, wi_ref, b_ref, wo_ref, *rest):
        act_ref, pre_ref, sum_ref = rest[-3:]
        value, slope = gelu_parts(mm(n_ref[...], wi_ref[...]) + b_ref[...])
        act_ref[...] = value.astype(BF)
        grad_pre = (slope * nt(g_ref[...], wo_ref[...])).astype(BF)
        pre_ref[...] = grad_pre
        total = jnp.sum(grad_pre.astype(F32).reshape(block // 8, 8, units), axis=0)

        @pl.when(pl.program_id(0) == 0)
        def _():
            sum_ref[...] = total

        @pl.when(pl.program_id(0) != 0)
        def _():
            sum_ref[...] += total

    rows = lambda n: pl.BlockSpec((block, n), lambda i: (i, 0))
    whole = lambda a: pl.BlockSpec(a.shape, lambda i: (0, 0))
    bias = bias.reshape(1, units)
    return pl.pallas_call(
        body,
        grid=(tokens // block,),
        in_specs=[rows(width), rows(width), whole(w_in), whole(bias), whole(w_out)]
        + [ANY] * len(deps),
        out_specs=[rows(units), rows(units), pl.BlockSpec((8, units), lambda i: (0, 0))],
        out_shape=[
            jax.ShapeDtypeStruct((tokens, units), BF),
            jax.ShapeDtypeStruct((tokens, units), BF),
            jax.ShapeDtypeStruct((8, units), F32),
        ],
        compiler_params=pltpu.CompilerParams(vmem_limit_bytes=48 << 20),
        cost_estimate=SMALL,
        name="feed_forward",
    )(normed, grads, w_in, bias, w_out, *deps)


def attention_kernel(halo, tok, heads, scalar_ref, q_ref, k_ref, v_ref, do_ref, keep_ref, sine_ref, start_ref, *rest):
    att_ref, dq_ref, dkv_ref = rest[-13:-10]
    s_scr, p_scr, k_scr, v_scr, kt_scr, vt_scr, dk_scr, dv_scr, ot_scr, dqt_scr = rest[-10:]
    s, p = pl.program_id(0), pl.program_id(1)
    groups = pl.num_programs(1)
    lanes = heads * HEAD_DIM
    blocks = tok // CHUNK
    chunks = (halo + 1) * blocks
    base = scalar_ref[2 * blocks]
    scale = 1.0 / math.sqrt(HEAD_DIM)
    row = lax.broadcasted_iota(jnp.int32, (CHUNK, CHUNK), 0)
    column = lax.broadcasted_iota(jnp.int32, (CHUNK, CHUNK), 1)
    unit = (row == column).astype(F32).astype(BF)
    from_lane = lax.broadcasted_iota(jnp.int32, (lanes, lanes), 0)
    to_lane = lax.broadcasted_iota(jnp.int32, (lanes, lanes), 1)
    half_rot = ROT_DIM // 2
    place = to_lane % HEAD_DIM
    turn = jnp.where((place < half_rot) & (from_lane == to_lane + half_rot), -1.0, 0.0)
    turn = jnp.where(
        (place >= half_rot) & (place < ROT_DIM) & (from_lane == to_lane - half_rot), 1.0, turn
    ).astype(BF)
    head_of = lax.broadcasted_iota(jnp.int32, (CHUNK, lanes), 1) // HEAD_DIM
    zero = jnp.zeros((CHUNK, lanes), BF)
    head_down = lax.broadcasted_iota(jnp.int32, (lanes, CHUNK), 0) // HEAD_DIM
    zero_down = jnp.zeros((lanes, CHUNK), BF)

    def flip(value):
        return nt(unit, value)

    def wide(table_ref, at):
        value = table_ref[at, :]
        return jnp.concatenate([value] * (lanes // LANES), axis=1)

    def chunk_at(j):
        return pl.ds(pl.multiple_of(j * CHUNK, CHUNK), CHUNK)

    def turned(value, at, sign):
        return value.astype(F32) * wide(keep_ref, at) + mm(value, turn) * (sign * wide(sine_ref, at))

    def by_head(value):
        return jnp.concatenate([jnp.where(head_of == h, value, zero) for h in range(heads)])

    def beside(value):
        return jnp.concatenate([jnp.where(head_down == h, value, zero_down) for h in range(heads)], axis=1)

    def part_of(h):
        return pl.ds(h * CHUNK, CHUNK)

    def prepare(b, carry):
        at = pl.ds(pl.multiple_of(b * tok, tok), tok)
        k_rot = turned(k_ref[b, 0], at, 1.0).astype(BF)
        k_scr[at, :] = k_rot
        kt_scr[:, at] = nt_t(k_rot)
        v_scr[at, :] = v_ref[b, 0]
        vt_scr[:, at] = nt_t(v_ref[b, 0])
        return carry

    unit_lanes = (from_lane == to_lane).astype(F32).astype(BF)

    def nt_t(value):
        return nt(unit_lanes, value).astype(BF)

    lowest = scalar_ref[s * blocks]

    lax.fori_loop(lowest // blocks, halo + 1, prepare, 0)

    def clear(j, carry):
        at = chunk_at(j)
        dk_scr[at, :] = jnp.zeros((CHUNK, lanes), F32)
        dv_scr[at, :] = jnp.zeros((CHUNK, lanes), F32)
        return carry

    lax.fori_loop(0, chunks, clear, 0)

    def both(body, start):
        low = [scalar_ref[s * blocks + b] for b in range(blocks)]
        high = [halo * blocks + b + 1 for b in range(blocks)]
        carry = list(start)
        edges = [(low[b], low[b + 1], b + 1) for b in range(blocks - 1)]
        for lower, upper, n in edges + [(low[-1], high[0], blocks)]:

            def step(j, now, n=n):
                return tuple(body(b, j, c) for b, c in enumerate(now[:n])) + now[n:]

            carry = list(lax.fori_loop(lower, upper, step, tuple(carry)))
        for b in range(1, blocks):

            def tail(j, now, b=b):
                return now[:b] + tuple(body(k, j, now[k]) for k in range(b, blocks))

            carry = list(lax.fori_loop(high[b - 1], high[b], tail, tuple(carry)))
        return carry

    q_down, q_beside, starts, inners, owns = [], [], [], [], []
    for b in range(blocks):
        inner = pl.ds(b * CHUNK, CHUNK)
        own = pl.ds((halo * blocks + b) * CHUNK, CHUNK)
        q_rot = turned(q_ref[0, inner, :], own, 1.0).astype(BF)
        q_scaled = (q_rot.astype(F32) * scale).astype(BF)
        q_down.append(by_head(q_scaled))
        q_beside.append(beside(nt_t(q_scaled)))
        starts.append(start_ref[0, :, inner] - base)
        inners.append(inner)
        owns.append(own)

    def scores(b, j, top):
        at = chunk_at(j)
        k_pos = j * CHUNK + row
        q_pos = (halo * blocks + b) * CHUNK + column
        allowed = (k_pos >= starts[b]) & (k_pos <= q_pos)
        value = mm(k_scr[at, :], q_beside[b])
        out = []
        for h in range(heads):
            masked = jnp.where(allowed, value[:, h * CHUNK : (h + 1) * CHUNK], -1e30)
            s_scr[b, at, part_of(h)] = masked
            out.append(jnp.max(masked.reshape(CHUNK // 8, 8, CHUNK), axis=0))
        return jnp.maximum(top, jnp.concatenate(out, axis=1))

    tops = both(scores, [jnp.full((8, heads * CHUNK), -1e30, F32)] * blocks)
    tops = [jnp.max(top, axis=0, keepdims=True) for top in tops]
    ot_scr[...] = jnp.zeros_like(ot_scr)
    dqt_scr[...] = jnp.zeros_like(dqt_scr)

    def weigh(b, j, total):
        at = chunk_at(j)
        value = jnp.exp(s_scr[b, at, :] - tops[b])
        total = total + jnp.sum(value.reshape(CHUNK // 8, 8, heads * CHUNK), axis=0)
        value = value.astype(BF)
        p_scr[b, at, :] = value
        for h in range(heads):
            rows = pl.ds(h * HEAD_DIM, HEAD_DIM)
            ot_scr[b, rows, :] += mm(vt_scr[rows, at], value[:, h * CHUNK : (h + 1) * CHUNK])
        return total

    totals = both(weigh, [jnp.zeros((8, heads * CHUNK), F32)] * blocks)
    do_down, do_beside, deltas = [], [], []
    for b in range(blocks):
        total = 1.0 / jnp.sum(totals[b], axis=0, keepdims=True)
        inverse = [total[:, h * CHUNK : (h + 1) * CHUNK] for h in range(heads)]
        out_t = jnp.concatenate(
            [ot_scr[b, h * HEAD_DIM : (h + 1) * HEAD_DIM, :] * inverse[h] for h in range(heads)]
        )
        att_ref[0, inners[b], :] = flip(out_t.astype(BF)).astype(BF)
        scaled = do_ref[0, inners[b], :].astype(F32)
        spread = jnp.zeros((CHUNK, lanes), F32)
        for h in range(heads):
            down = jnp.transpose(jnp.broadcast_to(inverse[h], (LANES, CHUNK)))
            down = jnp.concatenate([down] * (lanes // LANES), axis=1)
            spread = jnp.where(head_of == h, down, spread)
        scaled = (scaled * spread).astype(BF)
        scaled_t = nt(unit_lanes, scaled)
        prod = out_t * scaled_t
        do_down.append(by_head(scaled))
        do_beside.append(beside(scaled_t.astype(BF)))
        deltas.append(
            jnp.concatenate(
                [
                    jnp.sum(prod[h * HEAD_DIM : (h + 1) * HEAD_DIM], axis=0, keepdims=True)
                    for h in range(heads)
                ],
                axis=1,
            )
        )

    def backward(b, j, carry):
        at = chunk_at(j)
        prob = p_scr[b, at, :]
        ds = (prob.astype(F32) * (mm(v_scr[at, :], do_beside[b]) - deltas[b])).astype(BF)
        dv_scr[at, :] += mm(prob, do_down[b])
        dk_scr[at, :] += mm(ds, q_down[b])
        for h in range(heads):
            rows = pl.ds(h * HEAD_DIM, HEAD_DIM)
            dqt_scr[b, rows, :] += mm(kt_scr[rows, at], ds[:, h * CHUNK : (h + 1) * CHUNK])
        return carry

    both(backward, [0] * blocks)
    for b in range(blocks):
        dq = flip((dqt_scr[b] * scale).astype(BF)).astype(BF)
        dq_ref[0, inners[b], :] = turned(dq, owns[b], -1.0).astype(BF)

    for j in range(chunks):
        at = pl.ds(j * CHUNK, CHUNK)
        inner = pl.ds((j % blocks) * CHUNK, CHUNK)
        dk = turned(dk_scr[at, :].astype(BF), at, -1.0).astype(BF)
        for k, value in enumerate((dk, dv_scr[at, :].astype(BF))):
            columns = pl.ds(pl.multiple_of((k * groups + p) * lanes, LANES), lanes)
            dkv_ref[j // blocks, 0, inner, columns] = value


def attention(queries, key_values, grad_att, keep, sine, starts, scalars, deps=(), heads=4):
    spans, seqs, tok, width = key_values.shape
    halo = spans - 1
    lanes = heads * HEAD_DIM
    groups = width // 2 // lanes
    keys = spans * tok
    row = pl.BlockSpec((1, tok, lanes), lambda s, p, _: (s, 0, p))
    far = lambda off: pl.BlockSpec((spans, 1, tok, lanes), lambda s, p, _: (0, s, 0, off + p))
    table = pl.BlockSpec((keys, LANES), lambda s, p, _: (0, 0))
    flops = seqs * groups * heads * keys * tok * HEAD_DIM * 12 * 3
    return pl.pallas_call(
        functools.partial(attention_kernel, halo, tok, heads),
        grid_spec=pltpu.PrefetchScalarGridSpec(
            num_scalar_prefetch=1,
            grid=(seqs, groups),
            in_specs=[
                row,
                far(0),
                far(groups),
                row,
                table,
                table,
                pl.BlockSpec((1, 1, tok), lambda s, p, _: (s, 0, 0)),
            ]
            + [ANY] * len(deps),
            out_specs=[
                row,
                row,
                pl.BlockSpec((spans, 1, tok, width), lambda s, p, _: (0, s, 0, 0)),
            ],
            scratch_shapes=[
                pltpu.VMEM((tok // CHUNK, keys, heads * CHUNK), F32),
                pltpu.VMEM((tok // CHUNK, keys, heads * CHUNK), BF),
                pltpu.VMEM((keys, lanes), BF),
                pltpu.VMEM((keys, lanes), BF),
                pltpu.VMEM((lanes, keys), BF),
                pltpu.VMEM((lanes, keys), BF),
                pltpu.VMEM((keys, lanes), F32),
                pltpu.VMEM((keys, lanes), F32),
                pltpu.VMEM((tok // CHUNK, lanes, CHUNK), F32),
                pltpu.VMEM((tok // CHUNK, lanes, CHUNK), F32),
            ],
        ),
        out_shape=[
            jax.ShapeDtypeStruct((seqs, tok, width // 2), BF),
            jax.ShapeDtypeStruct((seqs, tok, width // 2), BF),
            jax.ShapeDtypeStruct((spans, seqs, tok, width), BF),
        ],
        compiler_params=pltpu.CompilerParams(vmem_limit_bytes=48 << 20),
        cost_estimate=SMALL,
        name="attention",
    )(scalars, queries, key_values, key_values, grad_att, keep, sine, starts, *deps)


def away_columns(whole, core, part):
    chips, rows, _ = whole.shape
    strip = part // 4

    def body(core_ref, w_ref, away_ref):
        for b in range(12):
            at = pl.multiple_of((2 * b + 1 - core_ref[0]) * strip, strip)
            away_ref[:, :, b * strip : (b + 1) * strip] = w_ref[:, :, pl.ds(at, strip)]

    return pl.pallas_call(
        body,
        grid=(4,),
        in_specs=[
            pl.BlockSpec(memory_space=pltpu.SMEM),
            pl.BlockSpec((chips // 4, rows, 6 * part), lambda i: (i, 0, 0)),
        ],
        out_specs=pl.BlockSpec((chips // 4, rows, 3 * part), lambda i: (i, 0, 0)),
        out_shape=jax.ShapeDtypeStruct((chips, rows, 3 * part), BF),
        compiler_params=pltpu.CompilerParams(vmem_limit_bytes=16 << 20),
        cost_estimate=SMALL,
        name="away_columns",
    )(core[None], whole)


def attention_weights(whole, come, core, nz, part):
    rows = whole.shape[1]
    depth = 8 * nz * rows
    strip = part // 4

    def body(core_ref, w_ref, c_ref, q_ref, kv_ref, dense_ref):
        mine = core_ref[0]
        for z in range(nz):
            own = pl.ds(pl.multiple_of((mine * nz + z) * rows, rows), rows)
            other = pl.ds(pl.multiple_of(((1 - mine) * nz + z) * rows, rows), rows)
            for b in range(12):
                value = w_ref[z, :, pl.ds(pl.multiple_of((2 * b + mine) * strip, strip), strip)]
                if b < 4:
                    q_ref[own, b * strip : (b + 1) * strip] = value
                else:
                    kv_ref[own, (b - 4) * strip : (b - 3) * strip] = value
            q_ref[other, :] = c_ref[z, :, :part]
            kv_ref[other, :] = c_ref[z, :, part:]
            dense_ref[z * rows : (z + 1) * rows, :] = w_ref[z, :, 6 * part :]

    block = lambda n: pl.BlockSpec((nz, rows, n), lambda i: (i, 0, 0))
    return pl.pallas_call(
        body,
        grid=(4,),
        in_specs=[pl.BlockSpec(memory_space=pltpu.SMEM), block(8 * part), block(3 * part)],
        out_specs=[
            pl.BlockSpec((depth // 4, part), lambda i: (i, 0)),
            pl.BlockSpec((depth // 4, 2 * part), lambda i: (i, 0)),
            pl.BlockSpec((depth // 8, 2 * part), lambda i: (i, 0)),
        ],
        out_shape=[
            jax.ShapeDtypeStruct((depth, part), BF),
            jax.ShapeDtypeStruct((depth, 2 * part), BF),
            jax.ShapeDtypeStruct((depth // 2, 2 * part), BF),
        ],
        compiler_params=pltpu.CompilerParams(vmem_limit_bytes=16 << 20),
        cost_estimate=SMALL,
        name="attention_weights",
    )(core[None], whole, come)


def unit_weights(whole, nz, rows, out_rows):
    columns = whole.shape[2]

    def body(w_ref, in_ref, out_ref):
        for z in range(nz):
            for j in range(4):
                at = (j * nz + z) * rows
                in_ref[at : at + rows, :] = w_ref[z, j * rows : (j + 1) * rows, :]
            out_ref[z * out_rows : (z + 1) * out_rows, :] = w_ref[z, 4 * rows :, :]

    return pl.pallas_call(
        body,
        grid=(2,),
        in_specs=[pl.BlockSpec((nz, 4 * rows + out_rows, columns), lambda i: (i, 0, 0))],
        out_specs=[
            pl.BlockSpec((4 * nz * rows, columns), lambda i: (i, 0)),
            pl.BlockSpec((nz * out_rows, columns), lambda i: (i, 0)),
        ],
        out_shape=[
            jax.ShapeDtypeStruct((8 * nz * rows, columns), BF),
            jax.ShapeDtypeStruct((2 * nz * out_rows, columns), BF),
        ],
        compiler_params=pltpu.CompilerParams(vmem_limit_bytes=16 << 20),
        cost_estimate=SMALL,
        name="unit_weights",
    )(whole)


def layer_norm(pieces, gain, bias, rows, first, extra, into=None, block=256):
    _, tok, width = pieces[0][0].shape
    steps = tok // block
    count = len(pieces)
    kept = 2 if extra else count

    def body(*refs):
        gain_ref, bias_ref = refs[count : count + 2]
        outs = refs[-2:] if extra else refs[-1:]
        i = pl.program_id(0)
        for p in range(count):

            @pl.when(i == p)
            def _():
                x = refs[p][0].astype(F32)
                centered = x - jnp.mean(x, axis=1, keepdims=True)
                variance = jnp.mean(centered * centered, axis=1, keepdims=True)
                value = centered * lax.rsqrt(variance + 1e-05)
                value = value * gain_ref[...] + bias_ref[...]
                if p < kept:
                    outs[0][...] = value.astype(BF)
                if extra:
                    outs[1][...] = value.astype(BF)

    def piece_spec(p):
        return pl.BlockSpec(
            (1, block, width),
            lambda i, b: (pieces[p][1], jnp.where(i == p, b, jnp.where(i < p, 0, steps - 1)), 0),
        )

    def kept_at(i, b):
        return first // block + jnp.where(i < kept, i * steps + b, kept * steps - 1)

    line = pl.BlockSpec((1, width), lambda i, b: (0, 0))
    out_specs = [pl.BlockSpec((block, width), lambda i, b: (kept_at(i, b), 0))]
    out_shape = [jax.ShapeDtypeStruct((rows, width), BF)]
    if extra:
        out_specs += [pl.BlockSpec((block, width), lambda i, b: (i * steps + b, 0))]
        out_shape += [jax.ShapeDtypeStruct((count * tok, width), BF)]
    given = [] if into is None else [into]
    return pl.pallas_call(
        body,
        grid=(count, steps),
        in_specs=[piece_spec(p) for p in range(count)] + [line, line] + [ANY] * len(given),
        out_specs=out_specs,
        out_shape=out_shape,
        input_output_aliases={} if into is None else {count + 2: 0},
        compiler_params=pltpu.CompilerParams(vmem_limit_bytes=32 << 20),
        cost_estimate=SMALL,
        name="layer_norm",
    )(*(p[0] for p in pieces), gain.reshape(1, width), bias.reshape(1, width), *given)


def attention_weight_grads(normed, attended, dq, dkv, grads, nz):
    tokens, part = dq.shape
    all_tokens, width = normed.shape
    near = all_tokens - tokens
    block, strip = width // 4, part // 4

    rows = strip // nz

    def body(n_ref, a_ref, d_ref, dkv_ref, g_ref, o_ref):
        def put(value, at):
            for h in range(2):
                for z in range(nz):
                    low = (h * nz + z) * rows
                    o_ref[0, z, h, :, at] = value[low : low + rows]

        put(tn(n_ref[near:, :], d_ref[...]).astype(BF), slice(0, part))
        put(tn(n_ref[...], dkv_ref[...]).astype(BF), slice(part, 3 * part))
        dense = tn(a_ref[...], g_ref[...]).astype(BF)
        put(jnp.concatenate([dense[:, :part], dense[:, part:]]), slice(3 * part, 4 * part))

    whole = lambda a: pl.BlockSpec(a.shape, lambda i: (0, 0))
    return pl.pallas_call(
        body,
        grid=(4,),
        in_specs=[
            pl.BlockSpec((all_tokens, block), lambda i: (0, i)),
            pl.BlockSpec((tokens, strip), lambda i: (0, i)),
            whole(dq),
            whole(dkv),
            pl.BlockSpec((tokens, width), lambda i: (0, 0)),
        ],
        out_specs=pl.BlockSpec((1, nz, 2, rows, 4 * part), lambda i: (i, 0, 0, 0, 0)),
        out_shape=jax.ShapeDtypeStruct((4, nz, 2, rows, 4 * part), BF),
        compiler_params=pltpu.CompilerParams(vmem_limit_bytes=48 << 20),
        cost_estimate=SMALL,
        name="attention_weight_grads",
    )(normed, attended, dq, dkv, grads)


def summed(*values):
    return sum(v.astype(F32) for v in values).astype(BF)


def z_scatter(parts, axis, zi, nz):
    steps = []
    for k, pairs in enumerate(z_pairs(nz)):
        shape = parts.shape
        blocks = parts.reshape(shape[:axis] + (shape[axis] // 2, 2) + shape[axis + 1 :])
        bit = (zi >> k) & 1
        come = lax.ppermute(pick(blocks, 1 - bit, axis + 1), "z", pairs)
        parts = summed(pick(blocks, bit, axis + 1), come)
        steps.append(parts)
    return steps[:-1] + [lax.squeeze(parts, (axis,))]


def normalise(tokens):
    row_mean = jnp.mean(tokens, axis=-1, keepdims=True)
    centered = tokens - row_mean
    variance = jnp.mean(centered * centered, axis=-1, keepdims=True)
    inv_std = lax.rsqrt(variance + 1e-05)
    return centered * inv_std, inv_std


def pick(blocks, index, axis):
    return lax.dynamic_index_in_dim(blocks, index, axis, keepdims=False)


def by_place(place, mine, theirs):
    low = jnp.where(place == 0, mine, theirs)
    high = jnp.where(place == 0, theirs, mine)
    return jnp.stack([low, high])


def z_pairs(nz):
    return [[(i, i ^ (1 << k)) for i in range(nz)] for k in range(nz.bit_length() - 1)]


def local_plane(
    nz,
    hidden_in,
    doc_lengths,
    ln_gain,
    ln_bias,
    w_qkv,
    b_qkv,
    w_dense,
    b_dense,
    w_in,
    b_in,
    w_out,
    b_out,
    out_grad,
):
    core, xi, yi, zi = (lax.axis_index(a) for a in "cxyz")
    chip = yi * 2 + xi
    halo = nz // 2
    _, tok, width = hidden_in.shape
    rows, ff = w_in.shape
    out_rows = w_out.shape[0]
    part = width // 2
    units = ff // 4
    up = [(i, i + 1) for i in range(nz - 1)]
    down = [(i + 1, i) for i in range(nz - 1)]
    hidden_own, grad_own = hidden_in[0], out_grad[0]

    small = jnp.concatenate([ln_gain, ln_bias, b_qkv, b_dense, b_in, b_out])[None]
    sizes = [v.shape[0] for v in (ln_gain, ln_bias, b_qkv, b_dense, b_in, b_out)]
    small_len = small.shape[1]
    first_whole = lax.all_gather(
        jnp.concatenate([w_qkv, w_dense], axis=1), ("y", "x", "z"), axis=0, tiled=False
    )
    come = other_core(away_columns(first_whole, core, part))

    def halves(weight, shape, axis, place):
        blocks = weight.reshape(shape)
        return pick(blocks, place, axis), pick(blocks, 1 - place, axis)

    in_mine, in_theirs = halves(w_in, (rows, 4, 2, -1), 2, core)
    in_got = other_core(in_theirs.reshape(rows, -1))
    in_core = by_place(core, in_mine.reshape(rows, -1), in_got)
    in_mine, in_theirs = halves(in_core, (2 * rows, 2, 2, -1), 2, xi)
    in_got = over_x(in_theirs.reshape(2 * rows, units))
    in_piece = by_place(xi, in_mine.reshape(2 * rows, units), in_got).reshape(4 * rows, units)

    before = [hidden_own]
    for _ in range(halo):
        before.append(lax.ppermute(before[-1], "z", up))
    pair_own = jnp.stack([hidden_own, grad_own])
    pair_x = over_x(pair_own)
    pair_other, pair_x_other = other_core(pair_own), other_core(pair_x)
    lens_other = other_core(doc_lengths)
    near = [pair_own, pair_other, pair_x, pair_x_other]

    for place, move in ((core, other_core), (xi, over_x), (yi, over_y)):
        small = by_place(place, small, move(small)).reshape(-1, small_len)
    for k, pairs in enumerate(z_pairs(nz)):
        small = by_place((zi >> k) & 1, small, lax.ppermute(small, "z", pairs))
        small = small.reshape(-1, small_len)
    small = small.reshape(nz, 8, small_len).transpose(1, 0, 2).reshape(8 * nz, small_len).astype(F32)
    cuts = [sum(sizes[:i]) for i in range(7)]
    gain, bias, qkv_bias, dense_bias, in_bias, out_bias = (
        small[:, cuts[i] : cuts[i + 1]].reshape(-1) for i in range(6)
    )
    qkv_bias = pick(qkv_bias.reshape(3, 4, 2, -1), core, 2).reshape(-1)
    in_bias = pick(pick(in_bias.reshape(2, 2, 2, -1), core, 2), xi, 1).reshape(-1)

    both = 2 * tok
    kv_rows = (halo + 1) * both
    normed_kv, normed_all = layer_norm(
        [(v, 0) for v in near], gain, bias, kv_rows, halo * both, True
    )
    grads_all = jnp.concatenate([v[1] for v in near])

    w_q_f, w_kv_f, w_dense_f = attention_weights(first_whole, come, core, nz, part)
    queries = matmul(normed_all, w_q_f, "nn", bias=qkv_bias[:part], rows=both)
    grad_att = matmul(grads_all, w_dense_f, "nt", rows=both)
    far = []
    for value in before[:0:-1]:
        far += [(value[None], 0), (other_core(value)[None], 0)]
    (normed_kv,) = layer_norm(far, gain, bias, kv_rows, 0, False, into=normed_kv)
    key_values = (mm(normed_kv, w_kv_f) + qkv_bias[part:]).astype(BF)
    second_whole = lax.all_gather(
        held(jnp.concatenate([in_piece, w_out]), first_whole), ("y", "z"), axis=0, tiled=False
    )

    base = (zi - halo) * tok
    positions = (base + jnp.arange((halo + 1) * tok, dtype=jnp.int32)).astype(F32)
    lane = jnp.arange(LANES, dtype=jnp.int32) % HEAD_DIM
    half_rot = ROT_DIM // 2
    frequency = jnp.exp(-math.log(10000.0) * 2.0 * (lane % half_rot).astype(F32) / ROT_DIM)
    angles = positions[:, None] * frequency[None, :]
    cosine, sine = jnp.cos(angles), jnp.sin(angles)
    keep = jnp.where(lane < ROT_DIM, cosine, 1.0)
    sine = jnp.where(lane < ROT_DIM, sine, 0.0)

    def doc_starts(lens):
        ends = prefix_ends(lens)
        own = zi * tok + jnp.arange(tok, dtype=jnp.int32)
        return jnp.max(jnp.where(own[:, None] >= ends[None, :], ends[None, :], 0), axis=1)

    starts = jnp.stack([doc_starts(doc_lengths[0]), doc_starts(lens_other[0])])
    lower = jnp.maximum((starts[:, ::CHUNK] - base) // CHUNK, 0)
    scalars = jnp.concatenate([lower.reshape(-1), base[None]]).astype(jnp.int32)
    attended, dq, dkv = attention(
        queries.reshape(2, tok, part),
        key_values.reshape(halo + 1, 2, tok, 2 * part),
        grad_att.reshape(2, tok, part),
        keep,
        sine,
        starts[:, None, :],
        scalars,
    )
    attended = attended.reshape(both, part)
    dq = dq.reshape(both, part)
    dkv = dkv.reshape(kv_rows, 2 * part)

    def after(*deps):
        return held(jnp.zeros((1, width), F32), *deps)

    dn_kv = nt(dkv, w_kv_f).astype(BF).reshape(halo + 1, 2, tok, width)
    dn_come = other_core(dn_kv[:halo, 1])
    g_att = attention_weight_grads(normed_kv, attended, dq, dkv, grads_all, nz)
    dn_far = summed(dn_kv[:halo, 0], held(dn_come, g_att))
    dn_q = matmul(dq, w_q_f, "nt").reshape(2, tok, width)
    dn_att = summed(dn_q, dn_kv[halo])

    s_att = lax.psum_scatter(
        g_att.reshape(4, nz, 2, rows, 4 * part), ("y", "x"), scatter_dimension=0, tiled=False
    )
    s_att = lax.psum_scatter(s_att, "z", scatter_dimension=0, tiled=False)

    w_in_f, w_out_f = unit_weights(second_whole, nz, rows, out_rows)
    activated, grad_pre, pre_sum = feed_forward(
        normed_all, grads_all, w_in_f, in_bias, w_out_f, deps=(dn_far, dn_att)
    )
    passed = dn_far[0]
    for step in range(1, halo):
        come = held(lax.ppermute(passed, "z", down), pre_sum)
        passed = summed(dn_far[step], come)
    dn_back = lax.ppermute(passed, "z", down)

    def away_tokens(shared, attn):
        return jnp.stack([summed(shared[0, 1], attn[1]), shared[1, 1]])

    g_in = matmul(normed_all, grad_pre, "tn", deps=(passed,)).reshape(2, -1, units)
    in_away = pick(g_in, 1 - yi, 0)
    in_y = over_y(in_away)
    dn_ff = (nt(grad_pre, w_in_f) + after(in_away)).astype(BF).reshape(2, 2, tok, width)
    dn_away = away_tokens(dn_ff, dn_att)
    g_out = matmul(activated, grads_all, "tn", deps=(dn_away,)).reshape(2, -1, width)
    out_away = pick(g_out, 1 - yi, 0)
    out_y = over_y(out_away)
    dn_come = held(other_core(dn_away), g_out)
    dn_send = summed(dn_ff[1, 0], dn_come[1])
    dn_x = over_x(dn_send)
    branch = (mm(activated, w_out_f) + after(out_away, dn_send)).astype(BF)
    branch = branch.reshape(2, 2, tok, width)
    branch_att = matmul(attended, w_dense_f, "nn", deps=(dn_send,)).reshape(2, tok, width)
    br_come = other_core(away_tokens(branch, branch_att))
    br_send = summed(branch[1, 0], br_come[1])
    br_x = over_x(br_send)

    s_in = summed(pick(g_in, yi, 0), held(in_y, br_send)).reshape(4, nz, rows, units)
    dn_x = held(dn_x, s_in)
    s_in_steps = z_scatter(s_in, 1, zi, nz)
    s_in = s_in_steps[-1].reshape(2, 2, rows, units)
    in_x = over_x(pick(s_in, 1 - xi, 0))
    dn_parts = [dn_ff[0, 0], dn_att[0], dn_come[0]]
    br_parts = [branch[0, 0], branch_att[0], br_come[0]]

    x = hidden_own.astype(F32)
    gy = grad_own.astype(F32)
    dn = sum(v.astype(F32) for v in (*dn_parts, dn_x, dn_back))
    xhat, inv_std = normalise(x)
    scaled = dn * gain
    grad_input = gy + inv_std * (
        scaled
        - jnp.mean(scaled, axis=1, keepdims=True)
        - xhat * jnp.mean(scaled * xhat, axis=1, keepdims=True)
    )
    out_y, br_x = held(out_y, grad_input), held(br_x, grad_input)
    s_out = summed(pick(g_out, yi, 0), out_y).reshape(nz, out_rows, width)
    grad_w_out = z_scatter(s_out, 0, zi, nz)[-1].astype(F32)
    hidden_out = (
        x + sum(v.astype(F32) for v in (*br_parts, br_x)) + dense_bias + out_bias
    ).astype(BF)

    def spread(vector, shape, mine):
        return jnp.where(mine, vector.reshape(shape), 0.0).reshape(-1)

    two = jnp.arange(2)
    g_qkv_bias = jnp.concatenate([jnp.sum(v.astype(F32), axis=0) for v in (dq, dkv)])
    small_grads = [
        jnp.sum(dn * xhat, axis=0),
        jnp.sum(dn, axis=0),
        spread(g_qkv_bias, (3, 4, 1, -1), (two == core)[None, None, :, None]),
        jnp.sum(gy, axis=0),
        spread(
            jnp.sum(pre_sum, axis=0),
            (2, 1, 1, -1),
            ((two == xi)[:, None] & (two == core)[None, :])[None, :, :, None],
        ),
    ]
    small_sizes = [g.shape[0] for g in small_grads]
    total = held(jnp.concatenate(small_grads), s_in_steps[0])
    total = total + other_core(total)
    total = held(total + over_x(total), s_in)
    total = held(total + over_y(total), in_x)
    for pairs in z_pairs(nz):
        total = total + lax.ppermute(total, "z", pairs)
    device = (chip * 2 + core) * nz + zi
    small_out, at = [], 0
    for size in small_sizes:
        share = size // (8 * nz)
        small_out.append(lax.dynamic_slice_in_dim(total, at + device * share, share, 0))
        at += size
    g_gain, g_bias, g_bqkv, g_bdense, g_bin = small_out

    def home_core(columns):
        axis = columns.ndim - 3
        return by_place(core, pick(columns, core, axis), other_core(pick(columns, 1 - core, axis)))

    grad_w_dense = s_att[:, :, 3 * part :].transpose(1, 0, 2).reshape(rows, width).astype(F32)
    s_qkv = home_core(s_att[:, :, : 3 * part])
    grad_w_qkv = s_qkv.reshape(2, rows, 3, 4, -1).transpose(1, 2, 3, 0, 4).reshape(rows, -1)
    s_in = home_core(by_place(xi, pick(s_in, xi, 0), in_x))
    grad_w_in = s_in.reshape(2, 2, rows, 2, -1).transpose(2, 3, 1, 0, 4).reshape(rows, -1)
    return (
        hidden_out[None],
        grad_input[None],
        g_gain,
        g_bias,
        grad_w_qkv.astype(F32),
        g_bqkv,
        grad_w_dense,
        g_bdense,
        grad_w_in.astype(F32),
        g_bin,
        grad_w_out,
        g_bdense,
    )


def solution(mesh):
    n_seq, n_group = mesh.devices.shape
    if n_seq == 8 and n_group == 4:
        mesh = Mesh(mesh.devices.reshape(2, 2, 2, n_group), ("y", "x", "c", "z"))
        seq, group = ("y", "x", "c"), "z"
        both = ("y", "x", "c", "z")
        step = functools.partial(local_plane, n_group)
    else:
        seq, group, both = "seq", "group", ("seq", "group")
        step = local_generic
    matrix, vector = P(both, None), P(both)
    tokens = P(seq, group, None)
    weights = (vector, vector) + (matrix, vector) * 4
    return jax.shard_map(
        step,
        mesh=mesh,
        in_specs=(tokens, P(seq, None)) + weights + (tokens,),
        out_specs=(tokens, tokens) + weights,
        check_vma=False,
    )
```

```python
import functools
import math

import jax
import jax.numpy as jnp
from jax import lax
from jax.experimental import pallas as pl
from jax.experimental.pallas import tpu as pltpu
from jax.sharding import Mesh
from jax.sharding import PartitionSpec as P

HEADS = 16
HEAD_DIM = 64
ROT_DIM = 16


def prefix_ends(doc_lens):
    order = jnp.arange(doc_lens.shape[0], dtype=jnp.int32)
    return jnp.sum(jnp.where(order[None, :] <= order[:, None], doc_lens[None, :], 0), axis=1)


def dot_rows(left, right):
    return lax.dot_general(
        left, right, (((0,), (0,)), ((), ())), preferred_element_type=jnp.float32
    )


def dot_last(left, right):
    return lax.dot_general(
        left, right, (((1,), (1,)), ((), ())), preferred_element_type=jnp.float32
    )


def rope_tables(token_positions, rot_dim):
    half_rot = rot_dim // 2
    frequency = jnp.exp(
        -math.log(10000.0) * 2.0 * jnp.arange(half_rot, dtype=jnp.float32) / rot_dim
    )
    angles = token_positions.astype(jnp.float32)[:, None] * frequency[None, :]
    return (jnp.cos(angles)[:, None, :], jnp.sin(angles)[:, None, :])


def rotate(heads, cosine, sine, rot_dim):
    half_rot = rot_dim // 2
    first_half = heads[:, :, :half_rot]
    second_half = heads[:, :, half_rot:rot_dim]
    remainder = heads[:, :, rot_dim:]
    return jnp.concatenate(
        [
            first_half * cosine - second_half * sine,
            second_half * cosine + first_half * sine,
            remainder,
        ],
        axis=2,
    )


def gelu_exact(preact):
    return jax.nn.gelu(preact, approximate=False)


def block_scores(query_block, key_tile_block, seg_query, seg_key, pos_query, pos_key, score_scale):
    scaled = (
        jnp.einsum("qhd,khd->hqk", query_block, key_tile_block, preferred_element_type=jnp.float32)
        * score_scale
    )
    allowed = (seg_query[:, None] == seg_key[None, :]) & (pos_key[None, :] <= pos_query[:, None])
    return jnp.where(allowed[None], scaled, -1e30)


def owning_block(source, block_index, block_of_rows):
    return lax.dynamic_slice_in_dim(source, block_index * block_of_rows, block_of_rows, 0)


def add_block(source, block_index, block_of_rows, addend):
    current = owning_block(source, block_index, block_of_rows)
    return lax.dynamic_update_slice_in_dim(source, current + addend, block_index * block_of_rows, 0)


def attention_forward(
    query_heads,
    key_head_rows,
    value_head_rows,
    document_segment,
    token_positions,
    seg_start,
    block_of_rows,
):
    seq_len, head_count, head_dim = query_heads.shape
    score_scale = 1.0 / math.sqrt(head_dim)

    def query_step(qindex, state_now):
        outputs, log_sums = state_now
        query_block = owning_block(query_heads, qindex, block_of_rows)
        seg_query = owning_block(document_segment, qindex, block_of_rows)
        pos_query = owning_block(token_positions, qindex, block_of_rows)
        key_lower = seg_start[qindex * block_of_rows] // block_of_rows

        def scores_for_block(key_position_index):
            return block_scores(
                query_block,
                owning_block(key_head_rows, key_position_index, block_of_rows),
                seg_query,
                owning_block(document_segment, key_position_index, block_of_rows),
                pos_query,
                owning_block(token_positions, key_position_index, block_of_rows),
                score_scale,
            )

        def statistics_step(key_position_index, row_statistics):
            run_max, run_sum = row_statistics
            logit_scores = scores_for_block(key_position_index)
            new_max = jnp.maximum(run_max, jnp.max(logit_scores, axis=2))
            run_sum = run_sum * jnp.exp(run_max - new_max) + jnp.sum(
                jnp.exp(logit_scores - new_max[:, :, None]), axis=2
            )
            return (new_max, run_sum)

        start_stats = (
            jnp.full((head_count, block_of_rows), -1e30, jnp.float32),
            jnp.zeros((head_count, block_of_rows), jnp.float32),
        )
        run_max, run_sum = lax.fori_loop(key_lower, qindex + 1, statistics_step, start_stats)
        log_exp_total = run_max + jnp.log(run_sum)

        def value_loop_step(key_position_index, partial_output):
            attention_weights = jnp.exp(
                scores_for_block(key_position_index) - log_exp_total[:, :, None]
            ).astype(jnp.bfloat16)
            return partial_output + jnp.einsum(
                "hqk,khd->qhd",
                attention_weights,
                owning_block(value_head_rows, key_position_index, block_of_rows),
                preferred_element_type=jnp.float32,
            )

        block_out = lax.fori_loop(
            key_lower,
            qindex + 1,
            value_loop_step,
            jnp.zeros((block_of_rows, head_count, head_dim), jnp.float32),
        )
        outputs = lax.dynamic_update_slice_in_dim(outputs, block_out, qindex * block_of_rows, 0)
        log_sums = lax.dynamic_update_slice_in_dim(
            log_sums, log_exp_total, qindex * block_of_rows, 1
        )
        return (outputs, log_sums)

    start_state = (
        jnp.zeros((seq_len, head_count, head_dim), jnp.float32),
        jnp.zeros((head_count, seq_len), jnp.float32),
    )
    return lax.fori_loop(0, seq_len // block_of_rows, query_step, start_state)


def attention_backward(
    query_heads,
    key_head_rows,
    value_head_rows,
    grad_heads,
    outputs,
    log_sums,
    document_segment,
    token_positions,
    seg_start,
    block_of_rows,
):
    seq_len, head_count, head_dim = query_heads.shape
    score_scale = 1.0 / math.sqrt(head_dim)
    delta_all = jnp.sum(grad_heads.astype(jnp.float32) * outputs, axis=2).T

    def query_step(qindex, state_now):
        grad_query_all, grad_key_all, grad_value_all = state_now
        query_block = owning_block(query_heads, qindex, block_of_rows)
        grad_block = owning_block(grad_heads, qindex, block_of_rows)
        seg_query = owning_block(document_segment, qindex, block_of_rows)
        pos_query = owning_block(token_positions, qindex, block_of_rows)
        log_exp_total = lax.dynamic_slice_in_dim(log_sums, qindex * block_of_rows, block_of_rows, 1)
        delta_block = lax.dynamic_slice_in_dim(delta_all, qindex * block_of_rows, block_of_rows, 1)
        key_lower = seg_start[qindex * block_of_rows] // block_of_rows

        def key_loop_step(key_position_index, loop_state_inner):
            grad_query, grad_keys, grad_values = loop_state_inner
            key_tile_block = owning_block(key_head_rows, key_position_index, block_of_rows)
            value_tile_block = owning_block(value_head_rows, key_position_index, block_of_rows)
            logit_scores = block_scores(
                query_block,
                key_tile_block,
                seg_query,
                owning_block(document_segment, key_position_index, block_of_rows),
                pos_query,
                owning_block(token_positions, key_position_index, block_of_rows),
                score_scale,
            )
            probability = jnp.exp(logit_scores - log_exp_total[:, :, None])
            grad_values = add_block(
                grad_values,
                key_position_index,
                block_of_rows,
                jnp.einsum(
                    "hqk,qhd->khd",
                    probability.astype(jnp.bfloat16),
                    grad_block,
                    preferred_element_type=jnp.float32,
                ),
            )
            grad_probs = jnp.einsum(
                "qhd,khd->hqk", grad_block, value_tile_block, preferred_element_type=jnp.float32
            )
            grad_scores = (probability * (grad_probs - delta_block[:, :, None])).astype(
                jnp.bfloat16
            )
            grad_query = (
                grad_query
                + jnp.einsum(
                    "hqk,khd->qhd", grad_scores, key_tile_block, preferred_element_type=jnp.float32
                )
                * score_scale
            )
            grad_keys = add_block(
                grad_keys,
                key_position_index,
                block_of_rows,
                jnp.einsum(
                    "hqk,qhd->khd", grad_scores, query_block, preferred_element_type=jnp.float32
                )
                * score_scale,
            )
            return (grad_query, grad_keys, grad_values)

        start_inner = (
            jnp.zeros((block_of_rows, head_count, head_dim), jnp.float32),
            grad_key_all,
            grad_value_all,
        )
        grad_query, grad_key_all, grad_value_all = lax.fori_loop(
            key_lower, qindex + 1, key_loop_step, start_inner
        )
        grad_query_all = lax.dynamic_update_slice_in_dim(
            grad_query_all, grad_query, qindex * block_of_rows, 0
        )
        return (grad_query_all, grad_key_all, grad_value_all)

    zero_heads = jnp.zeros((seq_len, head_count, head_dim), jnp.float32)
    return lax.fori_loop(
        0, seq_len // block_of_rows, query_step, (zero_heads, zero_heads, zero_heads)
    )


def local_generic(
    hidden_in,
    doc_lengths,
    ln_gain,
    ln_bias,
    w_qkv,
    b_qkv,
    w_dense,
    b_dense,
    w_in,
    b_in,
    w_out,
    b_out,
    out_grad,
):
    (
        full_gain,
        full_bias,
        full_qkv,
        full_qkv_bias,
        full_dense,
        full_dense_bias,
        full_in,
        full_in_bias,
        full_out,
        full_out_bias,
    ) = (
        lax.all_gather(ln_gain, ("seq", "group"), axis=0, tiled=True),
        lax.all_gather(ln_bias, ("seq", "group"), axis=0, tiled=True),
        lax.all_gather(w_qkv, ("seq", "group"), axis=0, tiled=True),
        lax.all_gather(b_qkv, ("seq", "group"), axis=0, tiled=True),
        lax.all_gather(w_dense, ("seq", "group"), axis=0, tiled=True),
        lax.all_gather(b_dense, ("seq", "group"), axis=0, tiled=True),
        lax.all_gather(w_in, ("seq", "group"), axis=0, tiled=True),
        lax.all_gather(b_in, ("seq", "group"), axis=0, tiled=True),
        lax.all_gather(w_out, ("seq", "group"), axis=0, tiled=True),
        lax.all_gather(b_out, ("seq", "group"), axis=0, tiled=True),
    )
    tokens = hidden_in[0].astype(jnp.float32)
    tok_count = tokens.shape[0]
    width = tokens.shape[1]
    row_mean = jnp.mean(tokens, axis=1, keepdims=True)
    centered = tokens - row_mean
    variance = jnp.mean(centered * centered, axis=1, keepdims=True)
    inv_std = lax.rsqrt(variance + 1e-05)
    normal_rows = centered * inv_std
    normed = (normal_rows * full_gain.astype(jnp.float32) + full_bias.astype(jnp.float32)).astype(
        jnp.bfloat16
    )
    mixed = jnp.dot(normed, full_qkv, preferred_element_type=jnp.float32) + full_qkv_bias.astype(
        jnp.float32
    )
    token_positions = lax.axis_index("group") * tok_count + jnp.arange(tok_count, dtype=jnp.int32)
    cosine, sine = rope_tables(token_positions, ROT_DIM)
    head_shape = (tok_count, HEADS, HEAD_DIM)
    queries = (
        rotate(mixed[:, :width].reshape(head_shape), cosine, sine, ROT_DIM)
        .reshape(tok_count, width)
        .astype(jnp.bfloat16)
    )
    key_rows = (
        rotate(mixed[:, width : 2 * width].reshape(head_shape), cosine, sine, ROT_DIM)
        .reshape(tok_count, width)
        .astype(jnp.bfloat16)
    )
    value_rows = mixed[:, 2 * width :].astype(jnp.bfloat16)
    query_cols, key_cols, value_cols = (
        lax.all_to_all(queries, "group", split_axis=1, concat_axis=0, tiled=True),
        lax.all_to_all(key_rows, "group", split_axis=1, concat_axis=0, tiled=True),
        lax.all_to_all(value_rows, "group", split_axis=1, concat_axis=0, tiled=True),
    )
    seq_len = query_cols.shape[0]
    head_count = query_cols.shape[1] // HEAD_DIM
    heads_shape = (seq_len, head_count, HEAD_DIM)
    query_heads = query_cols.reshape(heads_shape)
    key_head_rows = key_cols.reshape(heads_shape)
    value_head_rows = value_cols.reshape(heads_shape)
    all_pos = jnp.arange(seq_len, dtype=jnp.int32)
    doc_lens = doc_lengths[0]
    doc_ends = prefix_ends(doc_lens)
    document_segment = jnp.sum((all_pos[:, None] >= doc_ends[None, :]).astype(jnp.int32), axis=1)
    doc_starts = doc_ends - doc_lens
    doc_index = jnp.arange(doc_ends.shape[0], dtype=jnp.int32)
    seg_start = jnp.sum(
        jnp.where(document_segment[:, None] == doc_index[None, :], doc_starts[None, :], 0), axis=1
    )
    block_of_rows = min(512, seq_len)
    outputs, log_sums = attention_forward(
        query_heads,
        key_head_rows,
        value_head_rows,
        document_segment,
        all_pos,
        seg_start,
        block_of_rows,
    )
    attended = lax.all_to_all(
        outputs.reshape(seq_len, head_count * HEAD_DIM).astype(jnp.bfloat16),
        "group",
        split_axis=0,
        concat_axis=1,
        tiled=True,
    )
    branch_attn = jnp.dot(
        attended, full_dense, preferred_element_type=jnp.float32
    ) + full_dense_bias.astype(jnp.float32)
    pre_act = jnp.dot(normed, full_in, preferred_element_type=jnp.float32) + full_in_bias.astype(
        jnp.float32
    )
    activated = gelu_exact(pre_act).astype(jnp.bfloat16)
    branch_mlp = jnp.dot(
        activated, full_out, preferred_element_type=jnp.float32
    ) + full_out_bias.astype(jnp.float32)
    hidden_out = (tokens + branch_attn + branch_mlp).astype(jnp.bfloat16)
    grad_rows = out_grad[0]
    grad_float = grad_rows.astype(jnp.float32)
    bias_grad = jnp.sum(grad_float, axis=0)
    grad_dense = dot_rows(attended, grad_rows)
    grad_out_w = dot_rows(activated, grad_rows)
    grad_act = dot_last(grad_rows, full_out)
    grad_pre = jax.vjp(gelu_exact, pre_act)[1](grad_act)[0].astype(jnp.bfloat16)
    grad_in_w = dot_rows(normed, grad_pre)
    grad_in_bias = jnp.sum(grad_pre.astype(jnp.float32), axis=0)
    grad_normed = dot_last(grad_pre, full_in)
    grad_attended = dot_last(grad_rows, full_dense).astype(jnp.bfloat16)
    grad_cols = lax.all_to_all(grad_attended, "group", split_axis=1, concat_axis=0, tiled=True)
    grad_query_all, grad_key_all, grad_value_all = attention_backward(
        query_heads,
        key_head_rows,
        value_head_rows,
        grad_cols.reshape(heads_shape),
        outputs,
        log_sums,
        document_segment,
        all_pos,
        seg_start,
        block_of_rows,
    )
    flat_shape = (seq_len, head_count * HEAD_DIM)
    grad_query_tok, grad_key_tok, grad_value_tok = (
        lax.all_to_all(
            grad_query_all.reshape(flat_shape).astype(jnp.bfloat16),
            "group",
            split_axis=0,
            concat_axis=1,
            tiled=True,
        ),
        lax.all_to_all(
            grad_key_all.reshape(flat_shape).astype(jnp.bfloat16),
            "group",
            split_axis=0,
            concat_axis=1,
            tiled=True,
        ),
        lax.all_to_all(
            grad_value_all.reshape(flat_shape).astype(jnp.bfloat16),
            "group",
            split_axis=0,
            concat_axis=1,
            tiled=True,
        ),
    )
    unrot_query = (
        rotate(grad_query_tok.astype(jnp.float32).reshape(head_shape), cosine, -sine, ROT_DIM)
        .reshape(tok_count, width)
        .astype(jnp.bfloat16)
    )
    unrot_key = (
        rotate(grad_key_tok.astype(jnp.float32).reshape(head_shape), cosine, -sine, ROT_DIM)
        .reshape(tok_count, width)
        .astype(jnp.bfloat16)
    )
    grad_mixed = jnp.concatenate([unrot_query, unrot_key, grad_value_tok], axis=1)
    grad_qkv_w = dot_rows(normed, grad_mixed)
    grad_qkv_bias = jnp.sum(grad_mixed.astype(jnp.float32), axis=0)
    grad_normed = grad_normed + dot_last(grad_mixed, full_qkv)
    scaled_grad = grad_normed * full_gain.astype(jnp.float32)
    grad_gain = jnp.sum(grad_normed * normal_rows, axis=0)
    grad_bias = jnp.sum(grad_normed, axis=0)
    grad_input = grad_float + inv_std * (
        scaled_grad
        - jnp.mean(scaled_grad, axis=1, keepdims=True)
        - normal_rows * jnp.mean(scaled_grad * normal_rows, axis=1, keepdims=True)
    )
    sharded = tuple(
        (
            lax.psum_scatter(grad_gain, ("seq", "group"), scatter_dimension=0, tiled=True),
            lax.psum_scatter(grad_bias, ("seq", "group"), scatter_dimension=0, tiled=True),
            lax.psum_scatter(grad_qkv_w, ("seq", "group"), scatter_dimension=0, tiled=True),
            lax.psum_scatter(grad_qkv_bias, ("seq", "group"), scatter_dimension=0, tiled=True),
            lax.psum_scatter(grad_dense, ("seq", "group"), scatter_dimension=0, tiled=True),
            lax.psum_scatter(bias_grad, ("seq", "group"), scatter_dimension=0, tiled=True),
            lax.psum_scatter(grad_in_w, ("seq", "group"), scatter_dimension=0, tiled=True),
            lax.psum_scatter(grad_in_bias, ("seq", "group"), scatter_dimension=0, tiled=True),
            lax.psum_scatter(grad_out_w, ("seq", "group"), scatter_dimension=0, tiled=True),
            lax.psum_scatter(bias_grad, ("seq", "group"), scatter_dimension=0, tiled=True),
        )
    )
    return (hidden_out[None], grad_input[None]) + sharded


SWAP = [(0, 1), (1, 0)]
CHUNK = 256
LANES = 128
BF = jnp.bfloat16
F32 = jnp.float32
ANY = pl.BlockSpec(memory_space=pl.ANY)
SMALL = pl.CostEstimate(flops=0, bytes_accessed=1 << 20, transcendentals=0)


def mm(left, right):
    return jnp.dot(left, right, preferred_element_type=F32)


def other_core(value):
    return lax.ppermute(value, "c", SWAP)


def over_x(value):
    return lax.ppermute(value, "x", SWAP)


def over_y(value):
    return lax.ppermute(value, "y", SWAP)


def nt(left, right):
    return lax.dot_general(left, right, (((1,), (1,)), ((), ())), preferred_element_type=F32)


def tn(left, right):
    return lax.dot_general(left, right, (((0,), (0,)), ((), ())), preferred_element_type=F32)


def matmul(left, right, form, deps=(), bias=None, block=512, dtype=BF, rows=None):
    rows = rows or (left.shape[1] if form == "tn" else left.shape[0])
    depth = left.shape[0] if form == "tn" else left.shape[1]
    columns = right.shape[0] if form == "nt" else right.shape[1]
    block = min(block, rows)
    dot = {"nn": mm, "nt": nt, "tn": tn}[form]

    def body(left_ref, right_ref, *rest):
        value = dot(left_ref[...], right_ref[...])
        if bias is not None:
            value = value + rest[0][...]
        rest[-1][...] = value.astype(dtype)

    if form == "tn":
        left_spec = pl.BlockSpec((depth, block), lambda i: (0, i))
    else:
        left_spec = pl.BlockSpec((block, depth), lambda i: (i, 0))
    whole = pl.BlockSpec(right.shape, lambda i: (0, 0))
    row = [] if bias is None else [pl.BlockSpec((1, columns), lambda i: (0, 0))]
    given = [] if bias is None else [bias.reshape(1, columns)]
    return pl.pallas_call(
        body,
        grid=(rows // block,),
        in_specs=[left_spec, whole] + row + [ANY] * len(deps),
        out_specs=pl.BlockSpec((block, columns), lambda i: (i, 0)),
        out_shape=jax.ShapeDtypeStruct((rows, columns), dtype),
        compiler_params=pltpu.CompilerParams(vmem_limit_bytes=48 << 20),
        cost_estimate=SMALL,
        name="matmul_" + form,
    )(left, right, *given, *deps)


def held(value, *deps):
    def body(*refs):
        pass

    return pl.pallas_call(
        body,
        in_specs=[ANY] * (1 + len(deps)),
        out_specs=ANY,
        out_shape=jax.ShapeDtypeStruct(value.shape, value.dtype),
        input_output_aliases={0: 0},
        compiler_params=pltpu.CompilerParams(vmem_limit_bytes=1 << 20),
        name="held",
    )(value, *deps)


def gelu_parts(value):
    size = jnp.abs(value)
    t = 1.0 / (1.0 + (0.3275911 / math.sqrt(2.0)) * size)
    poly = t * (
        0.254829592
        + t * (-0.284496736 + t * (1.421413741 + t * (-1.453152027 + t * 1.061405429)))
    )
    density = jnp.exp(-0.5 * value * value)
    tail = 0.5 * poly * density
    below = jnp.where(value < 0, tail, 1.0 - tail)
    return value * below, below + value * density * (1.0 / math.sqrt(2.0 * math.pi))


def feed_forward(normed, grads, w_in, bias, w_out, deps=(), block=512):
    tokens, width = normed.shape
    units = w_in.shape[1]

    def body(n_ref, g_ref, wi_ref, b_ref, wo_ref, *rest):
        act_ref, pre_ref, sum_ref = rest[-3:]
        value, slope = gelu_parts(mm(n_ref[...], wi_ref[...]) + b_ref[...])
        act_ref[...] = value.astype(BF)
        grad_pre = (slope * nt(g_ref[...], wo_ref[...])).astype(BF)
        pre_ref[...] = grad_pre
        total = jnp.sum(grad_pre.astype(F32).reshape(block // 8, 8, units), axis=0)

        @pl.when(pl.program_id(0) == 0)
        def _():
            sum_ref[...] = total

        @pl.when(pl.program_id(0) != 0)
        def _():
            sum_ref[...] += total

    rows = lambda n: pl.BlockSpec((block, n), lambda i: (i, 0))
    whole = lambda a: pl.BlockSpec(a.shape, lambda i: (0, 0))
    bias = bias.reshape(1, units)
    return pl.pallas_call(
        body,
        grid=(tokens // block,),
        in_specs=[rows(width), rows(width), whole(w_in), whole(bias), whole(w_out)]
        + [ANY] * len(deps),
        out_specs=[rows(units), rows(units), pl.BlockSpec((8, units), lambda i: (0, 0))],
        out_shape=[
            jax.ShapeDtypeStruct((tokens, units), BF),
            jax.ShapeDtypeStruct((tokens, units), BF),
            jax.ShapeDtypeStruct((8, units), F32),
        ],
        compiler_params=pltpu.CompilerParams(vmem_limit_bytes=48 << 20),
        cost_estimate=SMALL,
        name="feed_forward",
    )(normed, grads, w_in, bias, w_out, *deps)


def attention_kernel(halo, tok, heads, scalar_ref, q_ref, k_ref, v_ref, do_ref, keep_ref, sine_ref, start_ref, *rest):
    att_ref, dq_ref, dkv_ref = rest[-13:-10]
    s_scr, p_scr, k_scr, v_scr, kt_scr, vt_scr, dk_scr, dv_scr, ot_scr, dqt_scr = rest[-10:]
    s, p = pl.program_id(0), pl.program_id(1)
    groups = pl.num_programs(1)
    lanes = heads * HEAD_DIM
    blocks = tok // CHUNK
    chunks = (halo + 1) * blocks
    base = scalar_ref[2 * blocks]
    scale = 1.0 / math.sqrt(HEAD_DIM)
    row = lax.broadcasted_iota(jnp.int32, (CHUNK, CHUNK), 0)
    column = lax.broadcasted_iota(jnp.int32, (CHUNK, CHUNK), 1)
    unit = (row == column).astype(F32).astype(BF)
    from_lane = lax.broadcasted_iota(jnp.int32, (lanes, lanes), 0)
    to_lane = lax.broadcasted_iota(jnp.int32, (lanes, lanes), 1)
    half_rot = ROT_DIM // 2
    place = to_lane % HEAD_DIM
    turn = jnp.where((place < half_rot) & (from_lane == to_lane + half_rot), -1.0, 0.0)
    turn = jnp.where(
        (place >= half_rot) & (place < ROT_DIM) & (from_lane == to_lane - half_rot), 1.0, turn
    ).astype(BF)
    head_of = lax.broadcasted_iota(jnp.int32, (CHUNK, lanes), 1) // HEAD_DIM
    zero = jnp.zeros((CHUNK, lanes), BF)
    head_down = lax.broadcasted_iota(jnp.int32, (lanes, CHUNK), 0) // HEAD_DIM
    zero_down = jnp.zeros((lanes, CHUNK), BF)

    def flip(value):
        return nt(unit, value)

    def wide(table_ref, at):
        value = table_ref[at, :]
        return jnp.concatenate([value] * (lanes // LANES), axis=1)

    def chunk_at(j):
        return pl.ds(pl.multiple_of(j * CHUNK, CHUNK), CHUNK)

    def turned(value, at, sign):
        return value.astype(F32) * wide(keep_ref, at) + mm(value, turn) * (sign * wide(sine_ref, at))

    def by_head(value):
        return jnp.concatenate([jnp.where(head_of == h, value, zero) for h in range(heads)])

    def beside(value):
        return jnp.concatenate([jnp.where(head_down == h, value, zero_down) for h in range(heads)], axis=1)

    def part_of(h):
        return pl.ds(h * CHUNK, CHUNK)

    def prepare(b, carry):
        at = pl.ds(pl.multiple_of(b * tok, tok), tok)
        k_rot = turned(k_ref[b, 0], at, 1.0).astype(BF)
        k_scr[at, :] = k_rot
        kt_scr[:, at] = nt_t(k_rot)
        v_scr[at, :] = v_ref[b, 0]
        vt_scr[:, at] = nt_t(v_ref[b, 0])
        return carry

    unit_lanes = (from_lane == to_lane).astype(F32).astype(BF)

    def nt_t(value):
        return nt(unit_lanes, value).astype(BF)

    lowest = scalar_ref[s * blocks]

    lax.fori_loop(lowest // blocks, halo + 1, prepare, 0)

    def clear(j, carry):
        at = chunk_at(j)
        dk_scr[at, :] = jnp.zeros((CHUNK, lanes), F32)
        dv_scr[at, :] = jnp.zeros((CHUNK, lanes), F32)
        return carry

    lax.fori_loop(0, chunks, clear, 0)

    def both(body, start):
        low = [scalar_ref[s * blocks + b] for b in range(blocks)]
        high = [halo * blocks + b + 1 for b in range(blocks)]
        carry = list(start)
        edges = [(low[b], low[b + 1], b + 1) for b in range(blocks - 1)]
        for lower, upper, n in edges + [(low[-1], high[0], blocks)]:

            def step(j, now, n=n):
                return tuple(body(b, j, c) for b, c in enumerate(now[:n])) + now[n:]

            carry = list(lax.fori_loop(lower, upper, step, tuple(carry)))
        for b in range(1, blocks):

            def tail(j, now, b=b):
                return now[:b] + tuple(body(k, j, now[k]) for k in range(b, blocks))

            carry = list(lax.fori_loop(high[b - 1], high[b], tail, tuple(carry)))
        return carry

    q_down, q_beside, starts, inners, owns = [], [], [], [], []
    for b in range(blocks):
        inner = pl.ds(b * CHUNK, CHUNK)
        own = pl.ds((halo * blocks + b) * CHUNK, CHUNK)
        q_rot = turned(q_ref[0, inner, :], own, 1.0).astype(BF)
        q_scaled = (q_rot.astype(F32) * scale).astype(BF)
        q_down.append(by_head(q_scaled))
        q_beside.append(beside(nt_t(q_scaled)))
        starts.append(start_ref[0, :, inner] - base)
        inners.append(inner)
        owns.append(own)

    def scores(b, j, top):
        at = chunk_at(j)
        k_pos = j * CHUNK + row
        q_pos = (halo * blocks + b) * CHUNK + column
        allowed = (k_pos >= starts[b]) & (k_pos <= q_pos)
        value = mm(k_scr[at, :], q_beside[b])
        out = []
        for h in range(heads):
            masked = jnp.where(allowed, value[:, h * CHUNK : (h + 1) * CHUNK], -1e30)
            s_scr[b, at, part_of(h)] = masked
            out.append(jnp.max(masked.reshape(CHUNK // 8, 8, CHUNK), axis=0))
        return jnp.maximum(top, jnp.concatenate(out, axis=1))

    tops = both(scores, [jnp.full((8, heads * CHUNK), -1e30, F32)] * blocks)
    tops = [jnp.max(top, axis=0, keepdims=True) for top in tops]
    ot_scr[...] = jnp.zeros_like(ot_scr)
    dqt_scr[...] = jnp.zeros_like(dqt_scr)

    def weigh(b, j, total):
        at = chunk_at(j)
        value = jnp.exp(s_scr[b, at, :] - tops[b])
        total = total + jnp.sum(value.reshape(CHUNK // 8, 8, heads * CHUNK), axis=0)
        value = value.astype(BF)
        p_scr[b, at, :] = value
        for h in range(heads):
            rows = pl.ds(h * HEAD_DIM, HEAD_DIM)
            ot_scr[b, rows, :] += mm(vt_scr[rows, at], value[:, h * CHUNK : (h + 1) * CHUNK])
        return total

    totals = both(weigh, [jnp.zeros((8, heads * CHUNK), F32)] * blocks)
    do_down, do_beside, deltas = [], [], []
    for b in range(blocks):
        total = 1.0 / jnp.sum(totals[b], axis=0, keepdims=True)
        inverse = [total[:, h * CHUNK : (h + 1) * CHUNK] for h in range(heads)]
        out_t = jnp.concatenate(
            [ot_scr[b, h * HEAD_DIM : (h + 1) * HEAD_DIM, :] * inverse[h] for h in range(heads)]
        )
        att_ref[0, inners[b], :] = flip(out_t.astype(BF)).astype(BF)
        scaled = do_ref[0, inners[b], :].astype(F32)
        spread = jnp.zeros((CHUNK, lanes), F32)
        for h in range(heads):
            down = jnp.transpose(jnp.broadcast_to(inverse[h], (LANES, CHUNK)))
            down = jnp.concatenate([down] * (lanes // LANES), axis=1)
            spread = jnp.where(head_of == h, down, spread)
        scaled = (scaled * spread).astype(BF)
        scaled_t = nt(unit_lanes, scaled)
        prod = out_t * scaled_t
        do_down.append(by_head(scaled))
        do_beside.append(beside(scaled_t.astype(BF)))
        deltas.append(
            jnp.concatenate(
                [
                    jnp.sum(prod[h * HEAD_DIM : (h + 1) * HEAD_DIM], axis=0, keepdims=True)
                    for h in range(heads)
                ],
                axis=1,
            )
        )

    def backward(b, j, carry):
        at = chunk_at(j)
        prob = p_scr[b, at, :]
        ds = (prob.astype(F32) * (mm(v_scr[at, :], do_beside[b]) - deltas[b])).astype(BF)
        dv_scr[at, :] += mm(prob, do_down[b])
        dk_scr[at, :] += mm(ds, q_down[b])
        for h in range(heads):
            rows = pl.ds(h * HEAD_DIM, HEAD_DIM)
            dqt_scr[b, rows, :] += mm(kt_scr[rows, at], ds[:, h * CHUNK : (h + 1) * CHUNK])
        return carry

    both(backward, [0] * blocks)
    for b in range(blocks):
        dq = flip((dqt_scr[b] * scale).astype(BF)).astype(BF)
        dq_ref[0, inners[b], :] = turned(dq, owns[b], -1.0).astype(BF)

    for j in range(chunks):
        at = pl.ds(j * CHUNK, CHUNK)
        inner = pl.ds((j % blocks) * CHUNK, CHUNK)
        dk = turned(dk_scr[at, :].astype(BF), at, -1.0).astype(BF)
        for k, value in enumerate((dk, dv_scr[at, :].astype(BF))):
            columns = pl.ds(pl.multiple_of((k * groups + p) * lanes, LANES), lanes)
            dkv_ref[j // blocks, 0, inner, columns] = value


def attention(queries, key_values, grad_att, keep, sine, starts, scalars, deps=(), heads=4):
    spans, seqs, tok, width = key_values.shape
    halo = spans - 1
    lanes = heads * HEAD_DIM
    groups = width // 2 // lanes
    keys = spans * tok
    row = pl.BlockSpec((1, tok, lanes), lambda s, p, _: (s, 0, p))
    far = lambda off: pl.BlockSpec((spans, 1, tok, lanes), lambda s, p, _: (0, s, 0, off + p))
    table = pl.BlockSpec((keys, LANES), lambda s, p, _: (0, 0))
    flops = seqs * groups * heads * keys * tok * HEAD_DIM * 12 * 3
    return pl.pallas_call(
        functools.partial(attention_kernel, halo, tok, heads),
        grid_spec=pltpu.PrefetchScalarGridSpec(
            num_scalar_prefetch=1,
            grid=(seqs, groups),
            in_specs=[
                row,
                far(0),
                far(groups),
                row,
                table,
                table,
                pl.BlockSpec((1, 1, tok), lambda s, p, _: (s, 0, 0)),
            ]
            + [ANY] * len(deps),
            out_specs=[
                row,
                row,
                pl.BlockSpec((spans, 1, tok, width), lambda s, p, _: (0, s, 0, 0)),
            ],
            scratch_shapes=[
                pltpu.VMEM((tok // CHUNK, keys, heads * CHUNK), F32),
                pltpu.VMEM((tok // CHUNK, keys, heads * CHUNK), BF),
                pltpu.VMEM((keys, lanes), BF),
                pltpu.VMEM((keys, lanes), BF),
                pltpu.VMEM((lanes, keys), BF),
                pltpu.VMEM((lanes, keys), BF),
                pltpu.VMEM((keys, lanes), F32),
                pltpu.VMEM((keys, lanes), F32),
                pltpu.VMEM((tok // CHUNK, lanes, CHUNK), F32),
                pltpu.VMEM((tok // CHUNK, lanes, CHUNK), F32),
            ],
        ),
        out_shape=[
            jax.ShapeDtypeStruct((seqs, tok, width // 2), BF),
            jax.ShapeDtypeStruct((seqs, tok, width // 2), BF),
            jax.ShapeDtypeStruct((spans, seqs, tok, width), BF),
        ],
        compiler_params=pltpu.CompilerParams(vmem_limit_bytes=48 << 20),
        cost_estimate=SMALL,
        name="attention",
    )(scalars, queries, key_values, key_values, grad_att, keep, sine, starts, *deps)


def away_columns(whole, core, part):
    chips, rows, _ = whole.shape
    strip = part // 4

    def body(core_ref, w_ref, away_ref):
        for b in range(12):
            at = pl.multiple_of((2 * b + 1 - core_ref[0]) * strip, strip)
            away_ref[:, :, b * strip : (b + 1) * strip] = w_ref[:, :, pl.ds(at, strip)]

    return pl.pallas_call(
        body,
        grid=(4,),
        in_specs=[
            pl.BlockSpec(memory_space=pltpu.SMEM),
            pl.BlockSpec((chips // 4, rows, 6 * part), lambda i: (i, 0, 0)),
        ],
        out_specs=pl.BlockSpec((chips // 4, rows, 3 * part), lambda i: (i, 0, 0)),
        out_shape=jax.ShapeDtypeStruct((chips, rows, 3 * part), BF),
        compiler_params=pltpu.CompilerParams(vmem_limit_bytes=16 << 20),
        cost_estimate=SMALL,
        name="away_columns",
    )(core[None], whole)


def attention_weights(whole, come, core, nz, part):
    rows = whole.shape[1]
    depth = 8 * nz * rows
    strip = part // 4

    def body(core_ref, w_ref, c_ref, q_ref, kv_ref, dense_ref):
        mine = core_ref[0]
        for z in range(nz):
            own = pl.ds(pl.multiple_of((mine * nz + z) * rows, rows), rows)
            other = pl.ds(pl.multiple_of(((1 - mine) * nz + z) * rows, rows), rows)
            for b in range(12):
                value = w_ref[z, :, pl.ds(pl.multiple_of((2 * b + mine) * strip, strip), strip)]
                if b < 4:
                    q_ref[own, b * strip : (b + 1) * strip] = value
                else:
                    kv_ref[own, (b - 4) * strip : (b - 3) * strip] = value
            q_ref[other, :] = c_ref[z, :, :part]
            kv_ref[other, :] = c_ref[z, :, part:]
            dense_ref[z * rows : (z + 1) * rows, :] = w_ref[z, :, 6 * part :]

    block = lambda n: pl.BlockSpec((nz, rows, n), lambda i: (i, 0, 0))
    return pl.pallas_call(
        body,
        grid=(4,),
        in_specs=[pl.BlockSpec(memory_space=pltpu.SMEM), block(8 * part), block(3 * part)],
        out_specs=[
            pl.BlockSpec((depth // 4, part), lambda i: (i, 0)),
            pl.BlockSpec((depth // 4, 2 * part), lambda i: (i, 0)),
            pl.BlockSpec((depth // 8, 2 * part), lambda i: (i, 0)),
        ],
        out_shape=[
            jax.ShapeDtypeStruct((depth, part), BF),
            jax.ShapeDtypeStruct((depth, 2 * part), BF),
            jax.ShapeDtypeStruct((depth // 2, 2 * part), BF),
        ],
        compiler_params=pltpu.CompilerParams(vmem_limit_bytes=16 << 20),
        cost_estimate=SMALL,
        name="attention_weights",
    )(core[None], whole, come)


def unit_weights(whole, nz, rows, out_rows):
    columns = whole.shape[2]

    def body(w_ref, in_ref, out_ref):
        for z in range(nz):
            for j in range(4):
                at = (j * nz + z) * rows
                in_ref[at : at + rows, :] = w_ref[z, j * rows : (j + 1) * rows, :]
            out_ref[z * out_rows : (z + 1) * out_rows, :] = w_ref[z, 4 * rows :, :]

    return pl.pallas_call(
        body,
        grid=(2,),
        in_specs=[pl.BlockSpec((nz, 4 * rows + out_rows, columns), lambda i: (i, 0, 0))],
        out_specs=[
            pl.BlockSpec((4 * nz * rows, columns), lambda i: (i, 0)),
            pl.BlockSpec((nz * out_rows, columns), lambda i: (i, 0)),
        ],
        out_shape=[
            jax.ShapeDtypeStruct((8 * nz * rows, columns), BF),
            jax.ShapeDtypeStruct((2 * nz * out_rows, columns), BF),
        ],
        compiler_params=pltpu.CompilerParams(vmem_limit_bytes=16 << 20),
        cost_estimate=SMALL,
        name="unit_weights",
    )(whole)


def layer_norm(pieces, gain, bias, rows, first, extra, into=None, block=256):
    _, tok, width = pieces[0][0].shape
    steps = tok // block
    count = len(pieces)
    kept = 2 if extra else count

    def body(*refs):
        gain_ref, bias_ref = refs[count : count + 2]
        outs = refs[-2:] if extra else refs[-1:]
        i = pl.program_id(0)
        for p in range(count):

            @pl.when(i == p)
            def _():
                x = refs[p][0].astype(F32)
                centered = x - jnp.mean(x, axis=1, keepdims=True)
                variance = jnp.mean(centered * centered, axis=1, keepdims=True)
                value = centered * lax.rsqrt(variance + 1e-05)
                value = value * gain_ref[...] + bias_ref[...]
                if p < kept:
                    outs[0][...] = value.astype(BF)
                if extra:
                    outs[1][...] = value.astype(BF)

    def piece_spec(p):
        return pl.BlockSpec(
            (1, block, width),
            lambda i, b: (pieces[p][1], jnp.where(i == p, b, jnp.where(i < p, 0, steps - 1)), 0),
        )

    def kept_at(i, b):
        return first // block + jnp.where(i < kept, i * steps + b, kept * steps - 1)

    line = pl.BlockSpec((1, width), lambda i, b: (0, 0))
    out_specs = [pl.BlockSpec((block, width), lambda i, b: (kept_at(i, b), 0))]
    out_shape = [jax.ShapeDtypeStruct((rows, width), BF)]
    if extra:
        out_specs += [pl.BlockSpec((block, width), lambda i, b: (i * steps + b, 0))]
        out_shape += [jax.ShapeDtypeStruct((count * tok, width), BF)]
    given = [] if into is None else [into]
    return pl.pallas_call(
        body,
        grid=(count, steps),
        in_specs=[piece_spec(p) for p in range(count)] + [line, line] + [ANY] * len(given),
        out_specs=out_specs,
        out_shape=out_shape,
        input_output_aliases={} if into is None else {count + 2: 0},
        compiler_params=pltpu.CompilerParams(vmem_limit_bytes=32 << 20),
        cost_estimate=SMALL,
        name="layer_norm",
    )(*(p[0] for p in pieces), gain.reshape(1, width), bias.reshape(1, width), *given)


def attention_weight_grads(normed, attended, dq, dkv, grads, nz):
    tokens, part = dq.shape
    all_tokens, width = normed.shape
    near = all_tokens - tokens
    block, strip = width // 4, part // 4

    rows = strip // nz

    def body(n_ref, a_ref, d_ref, dkv_ref, g_ref, o_ref):
        def put(value, at):
            for h in range(2):
                for z in range(nz):
                    low = (h * nz + z) * rows
                    o_ref[0, z, h, :, at] = value[low : low + rows]

        put(tn(n_ref[near:, :], d_ref[...]).astype(BF), slice(0, part))
        put(tn(n_ref[...], dkv_ref[...]).astype(BF), slice(part, 3 * part))
        dense = tn(a_ref[...], g_ref[...]).astype(BF)
        put(jnp.concatenate([dense[:, :part], dense[:, part:]]), slice(3 * part, 4 * part))

    whole = lambda a: pl.BlockSpec(a.shape, lambda i: (0, 0))
    return pl.pallas_call(
        body,
        grid=(4,),
        in_specs=[
            pl.BlockSpec((all_tokens, block), lambda i: (0, i)),
            pl.BlockSpec((tokens, strip), lambda i: (0, i)),
            whole(dq),
            whole(dkv),
            pl.BlockSpec((tokens, width), lambda i: (0, 0)),
        ],
        out_specs=pl.BlockSpec((1, nz, 2, rows, 4 * part), lambda i: (i, 0, 0, 0, 0)),
        out_shape=jax.ShapeDtypeStruct((4, nz, 2, rows, 4 * part), BF),
        compiler_params=pltpu.CompilerParams(vmem_limit_bytes=48 << 20),
        cost_estimate=SMALL,
        name="attention_weight_grads",
    )(normed, attended, dq, dkv, grads)


def summed(*values):
    return sum(v.astype(F32) for v in values).astype(BF)


def z_scatter(parts, axis, zi, nz):
    steps = []
    for k, pairs in enumerate(z_pairs(nz)):
        shape = parts.shape
        blocks = parts.reshape(shape[:axis] + (shape[axis] // 2, 2) + shape[axis + 1 :])
        bit = (zi >> k) & 1
        come = lax.ppermute(pick(blocks, 1 - bit, axis + 1), "z", pairs)
        parts = summed(pick(blocks, bit, axis + 1), come)
        steps.append(parts)
    return steps[:-1] + [lax.squeeze(parts, (axis,))]


def normalise(tokens):
    row_mean = jnp.mean(tokens, axis=-1, keepdims=True)
    centered = tokens - row_mean
    variance = jnp.mean(centered * centered, axis=-1, keepdims=True)
    inv_std = lax.rsqrt(variance + 1e-05)
    return centered * inv_std, inv_std


def pick(blocks, index, axis):
    return lax.dynamic_index_in_dim(blocks, index, axis, keepdims=False)


def by_place(place, mine, theirs):
    low = jnp.where(place == 0, mine, theirs)
    high = jnp.where(place == 0, theirs, mine)
    return jnp.stack([low, high])


def z_pairs(nz):
    return [[(i, i ^ (1 << k)) for i in range(nz)] for k in range(nz.bit_length() - 1)]


def local_plane(
    nz,
    hidden_in,
    doc_lengths,
    ln_gain,
    ln_bias,
    w_qkv,
    b_qkv,
    w_dense,
    b_dense,
    w_in,
    b_in,
    w_out,
    b_out,
    out_grad,
):
    core, xi, yi, zi = (lax.axis_index(a) for a in "cxyz")
    chip = yi * 2 + xi
    halo = nz // 2
    _, tok, width = hidden_in.shape
    rows, ff = w_in.shape
    out_rows = w_out.shape[0]
    part = width // 2
    units = ff // 4
    up = [(i, i + 1) for i in range(nz - 1)]
    down = [(i + 1, i) for i in range(nz - 1)]
    hidden_own, grad_own = hidden_in[0], out_grad[0]

    small = jnp.concatenate([ln_gain, ln_bias, b_qkv, b_dense, b_in, b_out])[None]
    sizes = [v.shape[0] for v in (ln_gain, ln_bias, b_qkv, b_dense, b_in, b_out)]
    small_len = small.shape[1]
    first_whole = lax.all_gather(
        jnp.concatenate([w_qkv, w_dense], axis=1), ("y", "x", "z"), axis=0, tiled=False
    )
    come = other_core(away_columns(first_whole, core, part))

    def halves(weight, shape, axis, place):
        blocks = weight.reshape(shape)
        return pick(blocks, place, axis), pick(blocks, 1 - place, axis)

    in_mine, in_theirs = halves(w_in, (rows, 4, 2, -1), 2, core)
    in_got = other_core(in_theirs.reshape(rows, -1))
    in_core = by_place(core, in_mine.reshape(rows, -1), in_got)
    in_mine, in_theirs = halves(in_core, (2 * rows, 2, 2, -1), 2, xi)
    in_got = over_x(in_theirs.reshape(2 * rows, units))
    in_piece = by_place(xi, in_mine.reshape(2 * rows, units), in_got).reshape(4 * rows, units)

    before = [hidden_own]
    for _ in range(halo):
        before.append(lax.ppermute(before[-1], "z", up))
    pair_own = jnp.stack([hidden_own, grad_own])
    pair_x = over_x(pair_own)
    pair_other, pair_x_other = other_core(pair_own), other_core(pair_x)
    lens_other = other_core(doc_lengths)
    near = [pair_own, pair_other, pair_x, pair_x_other]

    for place, move in ((core, other_core), (xi, over_x), (yi, over_y)):
        small = by_place(place, small, move(small)).reshape(-1, small_len)
    for k, pairs in enumerate(z_pairs(nz)):
        small = by_place((zi >> k) & 1, small, lax.ppermute(small, "z", pairs))
        small = small.reshape(-1, small_len)
    small = small.reshape(nz, 8, small_len).transpose(1, 0, 2).reshape(8 * nz, small_len).astype(F32)
    cuts = [sum(sizes[:i]) for i in range(7)]
    gain, bias, qkv_bias, dense_bias, in_bias, out_bias = (
        small[:, cuts[i] : cuts[i + 1]].reshape(-1) for i in range(6)
    )
    qkv_bias = pick(qkv_bias.reshape(3, 4, 2, -1), core, 2).reshape(-1)
    in_bias = pick(pick(in_bias.reshape(2, 2, 2, -1), core, 2), xi, 1).reshape(-1)

    both = 2 * tok
    kv_rows = (halo + 1) * both
    normed_kv, normed_all = layer_norm(
        [(v, 0) for v in near], gain, bias, kv_rows, halo * both, True
    )
    grads_all = jnp.concatenate([v[1] for v in near])

    w_q_f, w_kv_f, w_dense_f = attention_weights(first_whole, come, core, nz, part)
    queries = matmul(normed_all, w_q_f, "nn", bias=qkv_bias[:part], rows=both)
    grad_att = matmul(grads_all, w_dense_f, "nt", rows=both)
    far = []
    for value in before[:0:-1]:
        far += [(value[None], 0), (other_core(value)[None], 0)]
    (normed_kv,) = layer_norm(far, gain, bias, kv_rows, 0, False, into=normed_kv)
    key_values = (mm(normed_kv, w_kv_f) + qkv_bias[part:]).astype(BF)
    second_whole = lax.all_gather(
        held(jnp.concatenate([in_piece, w_out]), first_whole), ("y", "z"), axis=0, tiled=False
    )

    base = (zi - halo) * tok
    positions = (base + jnp.arange((halo + 1) * tok, dtype=jnp.int32)).astype(F32)
    lane = jnp.arange(LANES, dtype=jnp.int32) % HEAD_DIM
    half_rot = ROT_DIM // 2
    frequency = jnp.exp(-math.log(10000.0) * 2.0 * (lane % half_rot).astype(F32) / ROT_DIM)
    angles = positions[:, None] * frequency[None, :]
    cosine, sine = jnp.cos(angles), jnp.sin(angles)
    keep = jnp.where(lane < ROT_DIM, cosine, 1.0)
    sine = jnp.where(lane < ROT_DIM, sine, 0.0)

    def doc_starts(lens):
        ends = prefix_ends(lens)
        own = zi * tok + jnp.arange(tok, dtype=jnp.int32)
        return jnp.max(jnp.where(own[:, None] >= ends[None, :], ends[None, :], 0), axis=1)

    starts = jnp.stack([doc_starts(doc_lengths[0]), doc_starts(lens_other[0])])
    lower = jnp.maximum((starts[:, ::CHUNK] - base) // CHUNK, 0)
    scalars = jnp.concatenate([lower.reshape(-1), base[None]]).astype(jnp.int32)
    attended, dq, dkv = attention(
        queries.reshape(2, tok, part),
        key_values.reshape(halo + 1, 2, tok, 2 * part),
        grad_att.reshape(2, tok, part),
        keep,
        sine,
        starts[:, None, :],
        scalars,
    )
    attended = attended.reshape(both, part)
    dq = dq.reshape(both, part)
    dkv = dkv.reshape(kv_rows, 2 * part)

    dn_kv = nt(dkv, w_kv_f).astype(BF).reshape(halo + 1, 2, tok, width)
    dn_come = other_core(dn_kv[:halo, 1])
    g_att = attention_weight_grads(normed_kv, attended, dq, dkv, grads_all, nz)
    dn_far = summed(dn_kv[:halo, 0], held(dn_come, g_att))
    dn_q = matmul(dq, w_q_f, "nt").reshape(2, tok, width)
    dn_att = summed(dn_q, dn_kv[halo])

    s_att = lax.psum_scatter(
        g_att.reshape(4, nz, 2, rows, 4 * part), ("y", "x"), scatter_dimension=0, tiled=False
    )
    s_att = lax.psum_scatter(s_att, "z", scatter_dimension=0, tiled=False)

    w_in_f, w_out_f = unit_weights(second_whole, nz, rows, out_rows)
    activated, grad_pre, pre_sum = feed_forward(
        normed_all, grads_all, w_in_f, in_bias, w_out_f, deps=(dn_far, dn_att)
    )
    passed = dn_far[0]
    for step in range(1, halo):
        come = held(lax.ppermute(passed, "z", down), pre_sum)
        passed = summed(dn_far[step], come)
    dn_back = lax.ppermute(passed, "z", down)

    def away_tokens(shared, attn):
        return jnp.stack([summed(shared[0, 1], attn[1]), shared[1, 1]])

    g_in = matmul(normed_all, grad_pre, "tn", deps=(passed,)).reshape(2, -1, units)
    in_away = pick(g_in, 1 - yi, 0)
    in_y = over_y(in_away)
    dn_ff = matmul(grad_pre, w_in_f, "nt", deps=(in_away,)).reshape(2, 2, tok, width)
    dn_away = away_tokens(dn_ff, dn_att)
    g_out = matmul(activated, grads_all, "tn", deps=(dn_away,)).reshape(2, -1, width)
    out_away = pick(g_out, 1 - yi, 0)
    out_y = over_y(out_away)
    dn_come = held(other_core(dn_away), g_out)
    dn_send = summed(dn_ff[1, 0], dn_come[1])
    dn_x = over_x(dn_send)
    branch = matmul(activated, w_out_f, "nn", deps=(out_away, dn_send))
    branch = branch.reshape(2, 2, tok, width)
    branch_att = matmul(attended, w_dense_f, "nn", deps=(dn_send,)).reshape(2, tok, width)
    br_come = other_core(away_tokens(branch, branch_att))
    br_send = summed(branch[1, 0], br_come[1])
    br_x = over_x(br_send)

    s_in = summed(pick(g_in, yi, 0), held(in_y, br_send)).reshape(4, nz, rows, units)
    dn_x = held(dn_x, s_in)
    s_in_steps = z_scatter(s_in, 1, zi, nz)
    s_in = s_in_steps[-1].reshape(2, 2, rows, units)
    in_x = over_x(pick(s_in, 1 - xi, 0))
    dn_parts = [dn_ff[0, 0], dn_att[0], dn_come[0]]
    br_parts = [branch[0, 0], branch_att[0], br_come[0]]

    x = hidden_own.astype(F32)
    gy = grad_own.astype(F32)
    dn = sum(v.astype(F32) for v in (*dn_parts, dn_x, dn_back))
    xhat, inv_std = normalise(x)
    scaled = dn * gain
    grad_input = gy + inv_std * (
        scaled
        - jnp.mean(scaled, axis=1, keepdims=True)
        - xhat * jnp.mean(scaled * xhat, axis=1, keepdims=True)
    )
    out_y, br_x = held(out_y, grad_input), held(br_x, grad_input)
    s_out = summed(pick(g_out, yi, 0), out_y).reshape(nz, out_rows, width)
    grad_w_out = z_scatter(s_out, 0, zi, nz)[-1].astype(F32)
    hidden_out = (
        x + sum(v.astype(F32) for v in (*br_parts, br_x)) + dense_bias + out_bias
    ).astype(BF)

    def spread(vector, shape, mine):
        return jnp.where(mine, vector.reshape(shape), 0.0).reshape(-1)

    two = jnp.arange(2)
    g_qkv_bias = jnp.concatenate([jnp.sum(v.astype(F32), axis=0) for v in (dq, dkv)])
    small_grads = [
        jnp.sum(dn * xhat, axis=0),
        jnp.sum(dn, axis=0),
        spread(g_qkv_bias, (3, 4, 1, -1), (two == core)[None, None, :, None]),
        jnp.sum(gy, axis=0),
        spread(
            jnp.sum(pre_sum, axis=0),
            (2, 1, 1, -1),
            ((two == xi)[:, None] & (two == core)[None, :])[None, :, :, None],
        ),
    ]
    small_sizes = [g.shape[0] for g in small_grads]
    total = held(jnp.concatenate(small_grads), s_in_steps[0])
    total = total + other_core(total)
    total = held(total + over_x(total), s_in)
    total = held(total + over_y(total), in_x)
    for pairs in z_pairs(nz):
        total = total + lax.ppermute(total, "z", pairs)
    device = (chip * 2 + core) * nz + zi
    small_out, at = [], 0
    for size in small_sizes:
        share = size // (8 * nz)
        small_out.append(lax.dynamic_slice_in_dim(total, at + device * share, share, 0))
        at += size
    g_gain, g_bias, g_bqkv, g_bdense, g_bin = small_out

    def home_core(columns):
        axis = columns.ndim - 3
        return by_place(core, pick(columns, core, axis), other_core(pick(columns, 1 - core, axis)))

    grad_w_dense = s_att[:, :, 3 * part :].transpose(1, 0, 2).reshape(rows, width).astype(F32)
    s_qkv = home_core(s_att[:, :, : 3 * part])
    grad_w_qkv = s_qkv.reshape(2, rows, 3, 4, -1).transpose(1, 2, 3, 0, 4).reshape(rows, -1)
    s_in = home_core(by_place(xi, pick(s_in, xi, 0), in_x))
    grad_w_in = s_in.reshape(2, 2, rows, 2, -1).transpose(2, 3, 1, 0, 4).reshape(rows, -1)
    return (
        hidden_out[None],
        grad_input[None],
        g_gain,
        g_bias,
        grad_w_qkv.astype(F32),
        g_bqkv,
        grad_w_dense,
        g_bdense,
        grad_w_in.astype(F32),
        g_bin,
        grad_w_out,
        g_bdense,
    )


def solution(mesh):
    n_seq, n_group = mesh.devices.shape
    if n_seq == 8 and n_group == 4:
        mesh = Mesh(mesh.devices.reshape(2, 2, 2, n_group), ("y", "x", "c", "z"))
        seq, group = ("y", "x", "c"), "z"
        both = ("y", "x", "c", "z")
        step = functools.partial(local_plane, n_group)
    else:
        seq, group, both = "seq", "group", ("seq", "group")
        step = local_generic
    matrix, vector = P(both, None), P(both)
    tokens = P(seq, group, None)
    weights = (vector, vector) + (matrix, vector) * 4
    return jax.shard_map(
        step,
        mesh=mesh,
        in_specs=(tokens, P(seq, None)) + weights + (tokens,),
        out_specs=(tokens, tokens) + weights,
        check_vma=False,
    )
```
